32 devices in a mesh: seq: 16 (over z, y, x), head: 2 (over core).
Axes of the slice: x: 2, y: 2, z: 4, core: 2. Of those that a mesh axis runs over, the one named last changes fastest.
Arguments:
- tokens: bfloat16 [2, 4096, 512], P(None, 'seq'), may hold values from -8 to 8
- counts: int32 [2], replicated, may hold values from 512 to 4096, as said below
- ln_gain: float32 [512], replicated, may hold values from 0.5 to 1.5
- ln_bias: float32 [512], replicated, may hold values from -1.5 to 1.5
- w_qkv: bfloat16 [3, 512, 512], P(None, 'seq', 'head'), may hold values from -0.25 to 0.25
- conv_taps: float32 [8, 33], P('head'), may hold values from -1 to 1
- w_out: bfloat16 [512, 512], P('head', 'seq'), may hold values from -0.25 to 0.25
- out_bias: float32 [512], replicated, may hold values from -1.5 to 1.5
- kernel7: float32 [7, 7, 512], replicated, may hold values from -0.875 to 0.875
- kernel5: float32 [5, 5, 512], replicated, may hold values from -1.25 to 1.25
- kernel3: float32 [3, 3, 512], replicated, may hold values from -2 to 2
- ppeg_bias: float32 [512], replicated, may hold values from -1.5 to 1.5
- cotangent: bfloat16 [2, 4096, 512], P(None, 'seq'), may hold values from -6 to 6
Outputs:
- output: bfloat16 [2, 4096, 512], P(None, 'seq')
- grad_tokens: float32 [2, 4096, 512], P(None, 'seq')
- grad_ln_gain: float32 [512], replicated
- grad_ln_bias: float32 [512], replicated
- grad_w_qkv: float32 [3, 512, 512], P(None, 'seq', 'head')
- grad_conv_taps: float32 [8, 33], P('head')
- grad_w_out: float32 [512, 512], P('head', 'seq')
- grad_out_bias: float32 [512], replicated
- grad_kernel7: float32 [7, 7, 512], replicated
- grad_kernel5: float32 [5, 5, 512], replicated
- grad_kernel3: float32 [3, 3, 512], replicated
- grad_ppeg_bias: float32 [512], replicated
The draws below stay inside these ranges and needn't reach their ends.
Inputs may be any that keep to these rules, and one draw needn't show every extreme that they name: `counts`: one slide of every draw, which one drawn from the seed, fills all 4096 slots.
All inputs are finite; a program needn't handle non-finite values.
Results may differ from the reference program's by a relative error of at most 0.009.
Values may be sent and summed in bfloat16 or wider, within the bound.
A program may use at most 128 MiB of HBM per device.

```python
import math
import jax
import jax.numpy as jnp
from jax import lax

DIM = 512
HEADS = 8
LANDMARKS = 256
PINV_ITERS = 6
TAPS = 33
GRID_W = 64
SLIDES = 2
SEQ_LEN = 4096


def draw_tokens(key, part):
    key = jax.random.fold_in(key, 11)
    rough_key, cycle_key, phase_key = jax.random.split(key, 3)
    positions = jnp.arange(SEQ_LEN, dtype=jnp.int32)
    cycles = jax.random.randint(cycle_key, (DIM,), 1, LANDMARKS // 4 + 1)
    turns = positions[:, None] * cycles[None, :] % SEQ_LEN
    phases = jax.random.uniform(phase_key, (DIM,), jnp.float32, -math.pi, math.pi)
    angles = 2.0 * math.pi / SEQ_LEN * turns.astype(jnp.float32) + phases[None, :]
    smooth_part = 1.5 * jnp.cos(angles)
    rough_part = jnp.clip(jax.random.normal(rough_key, (SLIDES, SEQ_LEN, DIM), jnp.float32), -6.0, 6.0)
    return (rough_part + smooth_part[None]).astype(jnp.bfloat16)


def draw_counts(key, part):
    key = jax.random.fold_in(key, 5)
    pick_key, length_key = jax.random.split(key)
    chosen = jax.random.randint(pick_key, (), 0, SLIDES)
    drawn = jax.random.randint(length_key, (SLIDES,), SEQ_LEN // 8, SEQ_LEN + 1)
    return jnp.where(jnp.arange(SLIDES) == chosen, SEQ_LEN, drawn).astype(jnp.int32)


def shard_levels(own_key, dims, cuts, smallest, high):
    factor_of, own = 1.0, jax.random.fold_in(own_key, 6)
    for axis_at, blocks in cuts:
        steps = jnp.exp(jax.random.uniform(jax.random.fold_in(own, axis_at), (blocks,), jnp.float32, smallest / len(cuts), high / len(cuts)))
        factor_of = factor_of * jnp.repeat(steps, dims[axis_at] // blocks).reshape([-1 if axis == axis_at else 1 for axis in range(len(dims))])
    return factor_of


def noise(rng, extent, width, most, shards=(), kind=jnp.bfloat16):
    level = shard_levels(rng, extent, shards, -0.22, 0.18) if shards else 1.0
    values = jax.random.normal(rng, extent, jnp.float32) * width * level
    return jnp.minimum(jnp.maximum(values, -most), most).astype(kind)


def setup_inputs(seed: int = 0) -> dict:
    arg_keys = jax.random.split(jax.random.key(seed), 14)
    return {
        "tokens": draw_tokens(jax.random.fold_in(arg_keys[13], 71), 0),
        "counts": draw_counts(jax.random.fold_in(arg_keys[13], 71), 0),
        "ln_gain": jnp.clip(1.0 + 0.1 * jax.random.normal(arg_keys[2], (DIM,), jnp.float32), 0.5, 1.5),
        "ln_bias": noise(arg_keys[3], (DIM,), 0.3, 1.5, (), jnp.float32),
        "w_qkv": noise(arg_keys[4], (3, DIM, DIM), DIM ** -0.5, 0.25, ((1, 16), (2, 2))),
        "conv_taps": noise(arg_keys[5], (HEADS, TAPS), TAPS ** -0.5, 1.0, ((0, 2),), jnp.float32),
        "w_out": noise(arg_keys[6], (DIM, DIM), DIM ** -0.5, 0.25, ((0, 2), (1, 16))),
        "out_bias": noise(arg_keys[7], (DIM,), 0.3, 1.5, (), jnp.float32),
        "kernel7": noise(arg_keys[8], (7, 7, DIM), 49 ** -0.5, 0.875, (), jnp.float32),
        "kernel5": noise(arg_keys[9], (5, 5, DIM), 25 ** -0.5, 1.25, (), jnp.float32),
        "kernel3": noise(arg_keys[10], (3, 3, DIM), 9 ** -0.5, 2.0, (), jnp.float32),
        "ppeg_bias": noise(arg_keys[11], (DIM,), 0.3, 1.5, (), jnp.float32),
        "cotangent": noise(arg_keys[12], (SLIDES, SEQ_LEN, DIM), 1.0, 6.0, ((1, 16),)),
    }


EPSILON = 1e-05
FULL_PRECISION = lax.Precision.HIGHEST

@jax.custom_vjp
def landmark_inverse(v):
    return lax.optimization_barrier(v.astype(jnp.bfloat16)).astype(jnp.float32)

@jax.custom_vjp
def landmark_inverse_gradient(v):
    return v

def low_keep(v):
    return (landmark_inverse(v), None)

def low_pass(kept, grad):
    return (grad,)

def back_keep(v):
    return (v, None)

def back_low(kept, grad):
    return (landmark_inverse(grad),)
landmark_inverse.defvjp(low_keep, low_pass)
landmark_inverse_gradient.defvjp(back_keep, back_low)

def batched_product(left_matrix, right_matrix):
    return jnp.einsum('hij,hjk->hik', left_matrix, right_matrix, precision=FULL_PRECISION)

def pseudo_inverse(matrix):
    column_sums = lax.optimization_barrier(jnp.sum(matrix, axis=1))
    row_sums = lax.optimization_barrier(jnp.sum(matrix, axis=2))
    scaling = lax.optimization_barrier(jnp.max(column_sums, axis=-1)) * lax.optimization_barrier(jnp.max(row_sums, axis=-1))
    iterate = jnp.swapaxes(matrix, 1, 2) / scaling[:, None, None]
    identity = jnp.eye(matrix.shape[-1], dtype=matrix.dtype)
    for sweep in range(PINV_ITERS):
        product = batched_product(matrix, iterate)
        inner_term = 7.0 * identity - product
        inner_term = 15.0 * identity - batched_product(product, inner_term)
        inner_term = 13.0 * identity - batched_product(product, inner_term)
        iterate = 0.25 * batched_product(iterate, inner_term)
    return iterate

def landmark_chain(query_landmarks, key_landmarks, value_landmarks):
    scores_scale_factor = query_landmarks.shape[-1] ** (-0.5)
    scores = scores_scale_factor * jnp.einsum('ihd,jhd->hij', query_landmarks, key_landmarks, precision=FULL_PRECISION)
    inverse = pseudo_inverse(jax.nn.softmax(scores, axis=-1))
    return jnp.einsum('hij,jhd->ihd', inverse, value_landmarks, precision=FULL_PRECISION)

def segment_sizes(count):
    slot_ids = jnp.arange(LANDMARKS, dtype=jnp.int32)
    seg_upper = ((slot_ids + 1) * count + LANDMARKS - 1) // LANDMARKS
    seg_lower = (slot_ids * count + LANDMARKS - 1) // LANDMARKS
    return (seg_upper - seg_lower).astype(jnp.float32)

def value_conv(value_rows_masked, conv_taps):
    margin = conv_taps.shape[1] // 2
    length = value_rows_masked.shape[0]
    padded = jnp.pad(value_rows_masked, ((margin, margin), (0, 0), (0, 0)))
    running = jnp.zeros_like(value_rows_masked)
    for shift in range(conv_taps.shape[1]):
        running = running + conv_taps[:, shift][None, :, None] * padded[shift:shift + length]
    return running

def depthwise(grid_cells, kernel_taps):
    radius = kernel_taps.shape[0] // 2
    height, across = (grid_cells.shape[0], grid_cells.shape[1])
    padded = jnp.pad(grid_cells, ((radius, radius), (radius, radius), (0, 0)))
    running = jnp.zeros_like(grid_cells)
    for row_shift in range(2 * radius + 1):
        for col_shift in range(2 * radius + 1):
            running = running + kernel_taps[row_shift, col_shift] * padded[row_shift:row_shift + height, col_shift:col_shift + across]
    return running

def slide_forward(inputs, count, params):
    gain, shift_bias, w_qkv, conv_taps, w_out, out_bias, kernel7, kernel5, kernel3, ppeg_bias = params
    length, model_width = inputs.shape
    head_width = model_width // HEADS
    scores_scale_factor = head_width ** (-0.5)
    positions = jnp.arange(length, dtype=jnp.int32)
    is_valid = positions < count
    mask_float = is_valid.astype(inputs.dtype)
    centred = inputs - lax.optimization_barrier(jnp.mean(inputs, axis=-1, keepdims=True))
    variance = lax.optimization_barrier(jnp.mean(centred * centred, axis=-1, keepdims=True))
    normed = landmark_inverse(centred * lax.rsqrt(variance + EPSILON) * gain + shift_bias)
    projected = landmark_inverse(landmark_inverse_gradient(jnp.einsum('ld,kdc->klc', normed, w_qkv, precision=FULL_PRECISION)))
    query_row_block = projected[0].reshape(length, HEADS, head_width)
    key_row_block = projected[1].reshape(length, HEADS, head_width)
    value_rows = projected[2].reshape(length, HEADS, head_width)
    segment = jnp.where(is_valid, positions * LANDMARKS // count, LANDMARKS).astype(jnp.int32)
    sizes = segment_sizes(count)
    query_landmarks = landmark_inverse(jax.ops.segment_sum(query_row_block, segment, num_segments=LANDMARKS + 1)[:LANDMARKS] / sizes[:, None, None])
    key_landmarks = landmark_inverse(jax.ops.segment_sum(key_row_block, segment, num_segments=LANDMARKS + 1)[:LANDMARKS] / sizes[:, None, None])
    query_landmark_scores = landmark_inverse_gradient(scores_scale_factor * jnp.einsum('wox,vox->owv', query_row_block, key_landmarks, precision=FULL_PRECISION))
    attention_query_side = landmark_inverse(jax.nn.softmax(query_landmark_scores, axis=-1))
    landmark_key_scores = landmark_inverse_gradient(scores_scale_factor * jnp.einsum('oue,fue->uof', query_landmarks, key_row_block, precision=FULL_PRECISION))
    landmark_key_scores = jnp.where(is_valid[None, None, :], landmark_key_scores, -1e+30)
    attention_key_side = jax.nn.softmax(landmark_key_scores, axis=-1)
    value_rows_masked = value_rows * mask_float[:, None, None]
    value_landmarks = landmark_inverse_gradient(jnp.einsum('uqy,yut->qut', landmark_inverse(attention_key_side), value_rows_masked, precision=FULL_PRECISION))
    mixed_landmarks = landmark_inverse(landmark_chain(query_landmarks, key_landmarks, value_landmarks))
    attention_matrix = jnp.einsum('kjo,okx->jkx', attention_query_side, mixed_landmarks, precision=FULL_PRECISION)
    attention_matrix = attention_matrix + value_conv(value_rows_masked, conv_taps)
    attention_matrix = landmark_inverse(landmark_inverse_gradient(attention_matrix.reshape(length, model_width)))
    hidden = inputs + landmark_inverse_gradient(jnp.dot(attention_matrix, w_out, precision=FULL_PRECISION)) + out_bias
    grid_cells = (hidden * mask_float[:, None]).reshape(length // GRID_W, GRID_W, model_width)
    mixed_grid = depthwise(grid_cells, kernel7) + depthwise(grid_cells, kernel5) + depthwise(grid_cells, kernel3)
    return hidden + mixed_grid.reshape(length, model_width) + ppeg_bias

def reference(tokens, counts, ln_gain, ln_bias, w_qkv, conv_taps, w_out, out_bias, kernel7, kernel5, kernel3, ppeg_bias, cotangent):
    params = tuple((entry.astype(jnp.float32) for entry in (ln_gain, ln_bias, w_qkv, conv_taps, w_out, out_bias, kernel7, kernel5, kernel3, ppeg_bias)))
    inputs = tokens.astype(jnp.float32)

    def whole_layer(inputs, params):

        def slide_step(running, slide_item):
            return (running, jax.checkpoint(slide_forward)(slide_item[0], slide_item[1], params))
        unused, outputs = lax.scan(slide_step, (), (inputs, counts))
        return outputs
    outputs, pull_back = jax.vjp(whole_layer, inputs, params)
    grad_inputs, grad_params = pull_back(cotangent.astype(jnp.float32))
    return (outputs.astype(jnp.bfloat16), grad_inputs, grad_params[0], grad_params[1], grad_params[2], grad_params[3], grad_params[4], grad_params[5], grad_params[6], grad_params[7], grad_params[8], grad_params[9])
```

```python
import functools

import jax
import jax.numpy as jnp
from jax import lax
from jax.experimental import pallas as pl
from jax.experimental.pallas import tpu as pltpu
from jax.sharding import PartitionSpec as P

MESH = pl.DeviceIdType.MESH
GRID_W = 64
MARKS = 256
SWEEPS = 6
EPSILON = 1e-05
f32, bf16 = jnp.float32, jnp.bfloat16
VMEM = pl.BlockSpec(memory_space=pltpu.VMEM)
SMEM = pl.BlockSpec(memory_space=pltpu.SMEM)
DMA = pltpu.SemaphoreType.DMA
BLK = 144


def sds(shape, dtype=f32):
    return jax.ShapeDtypeStruct(shape, dtype)


def call(kernel, outs, specs, scratch=(), cid=None, vmem=56):
    extra = {} if cid is None else dict(collective_id=cid, has_side_effects=True)
    return pl.pallas_call(
        kernel,
        out_shape=outs,
        in_specs=specs,
        out_specs=jax.tree.map(lambda _: VMEM, outs),
        scratch_shapes=list(scratch),
        compiler_params=pltpu.CompilerParams(vmem_limit_bytes=vmem * 2**20, **extra),
    )


def mm(left, right, cl=1, cr=0):
    return lax.dot_general(left, right, (((cl,), (cr,)), ((), ())), preferred_element_type=f32)


def split(value):
    high = value.astype(bf16)
    return high, (value - high.astype(f32)).astype(bf16)


def split3(row):
    high = row.astype(bf16).astype(f32)
    rest = row - high
    mid = rest.astype(bf16).astype(f32)
    return [high, mid, rest - mid]


def mm3(left, right, cl=1, cr=0):
    (lh, ll), (rh, rl) = left, right
    return mm(lh, rh, cl, cr) + (mm(lh, rl, cl, cr) + mm(ll, rh, cl, cr))


def iota(shape, dim):
    return lax.broadcasted_iota(jnp.int32, shape, dim)


def edges(count, marks):
    return (marks * count + (MARKS - 1)) >> 8, ((marks + 1) * count + (MARKS - 1)) >> 8


def member(count, start, rows):
    low, high = edges(count, iota((MARKS, rows), 0))
    slot = iota((MARKS, rows), 1) + start
    return jnp.where((slot >= low) & (slot < high), 1.0, 0.0).astype(bf16)


def owner_of(pair):
    return (pair // 2) * 4 + (pair % 2) * 3


def pair_of(me):
    z = lax.rem(me, 16) // 4
    return 2 * z + jnp.where(lax.rem(me, 4) == 3, 1, 0)


def is_owner(me):
    return (me < 16) & ((lax.rem(me, 4) == 0) | (lax.rem(me, 4) == 3))


def norm_kernel(rows, cnt, tok, gain, bias, normed, xpart):
    me, hd = lax.axis_index("seq"), lax.axis_index("head")
    for s in range(2):
        x = tok[s].astype(f32)
        xc = x - jnp.mean(x, axis=-1, keepdims=True)
        inv = lax.rsqrt(jnp.mean(xc * xc, axis=-1, keepdims=True) + EPSILON)
        normed[s] = (xc * inv * gain[...] + bias[...]).astype(bf16)
        mem = member(cnt[s], me * rows, rows)
        xpart[s] = mm(mem, normed[s, :, pl.ds(hd * 256, 256)]).astype(bf16)


def greet(n, pair=True):
    me, hd = lax.axis_index("seq"), lax.axis_index("head")
    sem = pltpu.get_barrier_semaphore()
    for i in range(1, n):
        pl.semaphore_signal(sem, inc=1, device_id={"seq": lax.rem(me + i, n)}, device_id_type=MESH)
    if pair:
        pl.semaphore_signal(sem, inc=1, device_id={"head": 1 - hd}, device_id_type=MESH)
    pl.semaphore_wait(sem, n - 1 + (1 if pair else 0))


def remote(src, dst, send, recv, **where):
    return pltpu.make_async_remote_copy(
        src_ref=src, dst_ref=dst, send_sem=send, recv_sem=recv, device_id=where, device_id_type=MESH
    )


def start_kernel(n, cnt, xpart, wts, cot, xbar, wall, halo, xr, xm, sx, rx, sw, rw, sh, rh, sp, rp, sg, rg):
    me, hd = lax.axis_index("seq"), lax.axis_index("head")
    mb = MARKS // n
    wr = wts.shape[1]
    rows = cot.shape[1]
    mine = pl.ds(pl.multiple_of(hd * 256, 256), 256)
    greet(n)
    peers = [lax.rem(me + i, n) for i in range(n)]
    cx, cw, cg = [], [], []
    for i in range(1, n):
        cx.append(
            remote(xpart.at[:, pl.ds(pl.multiple_of(peers[i] * mb, mb), mb)], xr.at[me], sx.at[i], rx.at[i], seq=peers[i])
        )
        cx[-1].start()
    ch = [
        remote(cot.at[:, pl.ds(rows - 192, 192), mine], halo.at[0], sh.at[0], rh.at[0], seq=peers[1]),
        remote(cot.at[:, pl.ds(0, 192), mine], halo.at[1], sh.at[1], rh.at[1], seq=peers[n - 1]),
    ]
    for c in ch:
        c.start()
    wrow = pl.ds(pl.multiple_of(me * wr, wr), wr)
    for i in range(1, n):
        cw.append(remote(wts, wall.at[:, wrow], sw.at[i], rw.at[i], seq=peers[i]))
        cw[-1].start()
    wall[:, wrow] = wts[...]
    row = pl.ds(pl.multiple_of(me * mb, mb), mb)
    xr[pl.ds(me, 1)] = xpart[:, row][None]
    for c in cx:
        c.wait_recv()
    total = xr[0].astype(f32)
    for d in range(1, n):
        total = total + xr[d].astype(f32)
    for s in range(2):
        low, high = edges(cnt[s], iota((mb, 256), 0) + me * mb)
        xm[s] = (total[s] / (high - low).astype(f32)).astype(bf16)
    xbar[:, row, mine] = xm[...]
    for i in range(1, n):
        cg.append(remote(xm, xbar.at[:, row, mine], sg.at[i], rg.at[i], seq=peers[i]))
        cg[-1].start()
    for c in cg:
        c.wait_recv()
    cp = remote(xbar.at[:, :, mine], xbar.at[:, :, mine], sp, rp, head=1 - hd)
    cp.start()
    for c in ch + cw:
        c.wait_recv()
    cp.wait_recv()
    for c in cx + ch + cw + cg + [cp]:
        c.wait_send()


def fill_kernel(half, full, ss, rs):
    hd = lax.axis_index("head")
    sem = pltpu.get_barrier_semaphore()
    pl.semaphore_signal(sem, inc=1, device_id={"head": 1 - hd}, device_id_type=MESH)
    pl.semaphore_wait(sem, 1)
    mine = pl.ds(pl.multiple_of(hd * 256, 256), 256)
    c = remote(half, full.at[:, :, mine], ss, rs, head=1 - hd)
    c.start()
    full[:, :, mine] = half[...]
    c.wait()


def reduce_kernel(n, blk, hal, recv, hrecv, ss, rs, sh, rh):
    me = lax.axis_index("seq")
    greet(n, False)
    right, left = lax.rem(me + 1, n), lax.rem(me + n - 1, n)
    ch = [
        remote(hal.at[1], hrecv.at[0], sh.at[0], rh.at[0], seq=right),
        remote(hal.at[0], hrecv.at[1], sh.at[1], rh.at[1], seq=left),
    ]
    for p in range(8):
        o = owner_of(p)

        @pl.when(me != o)
        def _():
            remote(blk.at[p], recv.at[me], ss.at[p], rs.at[me], seq=o).start()

        @pl.when(me == o)
        def _():
            recv[pl.ds(me, 1)] = blk[pl.ds(p, 1)]

    for c in ch:
        c.start()
    for c in ch:
        c.wait()
    for p in range(8):
        o = owner_of(p)

        @pl.when(me != o)
        def _():
            remote(blk.at[p], recv.at[me], ss.at[p], rs.at[me], seq=o).wait_send()

        @pl.when(me == o)
        def _():
            for d in range(n):
                if d != o:
                    remote(blk.at[p], recv.at[d], ss.at[p], rs.at[d], seq=o).wait_recv()


def spread_kernel(n, res, out, ss, rs):
    me = lax.axis_index("seq")
    greet(n, False)
    for p in range(8):
        o = owner_of(p)

        @pl.when(me == o)
        def _():
            for i in range(1, n):
                remote(res, out.at[p], ss.at[i], rs.at[p], seq=lax.rem(me + i, n)).start()
            out[p] = res[...]

    for p in range(8):
        o = owner_of(p)

        @pl.when(me != o)
        def _():
            remote(res, out.at[p], ss.at[0], rs.at[p], seq=o).wait_recv()

        @pl.when(me == o)
        def _():
            for i in range(1, n):
                remote(res, out.at[p], ss.at[i], rs.at[p], seq=lax.rem(me + i, n)).wait_send()


def late_kernel(n, cnt, tok, obias, po, ep, dn, wpart, hid, dnr, eall, gw, zhalo,
                por, er, es, erv, em, wrv, zs, *sems):
    (sp, rp, se, re, sa, ra, sw, rw, sz, rz, sf, rf) = sems
    me, hd = lax.axis_index("seq"), lax.axis_index("head")
    mb = MARKS // n
    wr = wpart.shape[1] // n
    rows = tok.shape[1]
    mine = pl.ds(pl.multiple_of(hd * 256, 256), 256)
    other = pl.ds(pl.multiple_of((1 - hd) * 256, 256), 256)
    peers = [lax.rem(me + i, n) for i in range(n)]
    greet(n)
    cp = [
        remote(ep.at[:, :, other], er, sp.at[0], rp.at[0], head=1 - hd),
        remote(po.at[:, :, other], por, sp.at[1], rp.at[1], head=1 - hd),
        remote(dn, dnr, sp.at[2], rp.at[2], head=1 - hd),
    ]
    for c in cp:
        c.start()
    cp[0].wait_recv()
    es[...] = (ep[:, :, mine].astype(f32) + er[...].astype(f32)).astype(bf16)
    row = pl.ds(pl.multiple_of(me * mb, mb), mb)
    ce, ca, cw = [], [], []
    for i in range(1, n):
        ce.append(remote(es.at[:, pl.ds(pl.multiple_of(peers[i] * mb, mb), mb)], erv.at[me], se.at[i], re.at[i], seq=peers[i]))
        ce[-1].start()
    cp[1].wait_recv()
    for s in range(2):
        h = tok[s, :, mine].astype(f32) + (po[s, :, mine].astype(f32) + por[s].astype(f32)) + obias[:, mine]
        hid[s] = h
        slot = iota((rows, 256), 0) + me * rows
        zs[s] = jnp.where(slot < cnt[s], h, 0.0).astype(bf16)
    cz = [
        remote(zs.at[:, pl.ds(rows - 192, 192)], zhalo.at[0], sz.at[0], rz.at[0], seq=peers[1]),
        remote(zs.at[:, pl.ds(0, 192)], zhalo.at[1], sz.at[1], rz.at[1], seq=peers[n - 1]),
    ]
    for c in cz:
        c.start()
    for i in range(1, n):
        cw.append(remote(wpart.at[:, pl.ds(pl.multiple_of(peers[i] * wr, wr), wr)], wrv.at[me], sw.at[i], rw.at[i], seq=peers[i]))
        cw[-1].start()
    erv[pl.ds(me, 1)] = es[:, row][None]
    wrv[pl.ds(me, 1)] = wpart[:, pl.ds(pl.multiple_of(me * wr, wr), wr)][None]
    for c in ce:
        c.wait_recv()
    total = erv[0].astype(f32)
    for d in range(1, n):
        total = total + erv[d].astype(f32)
    em[...] = total.astype(bf16)
    eall[:, row, mine] = em[...]
    for i in range(1, n):
        ca.append(remote(em, eall.at[:, row, mine], sa.at[i], ra.at[i], seq=peers[i]))
        ca[-1].start()
    for c in ca:
        c.wait_recv()
    cf = remote(eall.at[:, :, mine], eall.at[:, :, mine], sf, rf, head=1 - hd)
    cf.start()
    for c in cw:
        c.wait_recv()
    total = wrv[0].astype(f32)
    for d in range(1, n):
        total = total + wrv[d].astype(f32)
    gw[...] = total
    cf.wait_recv()
    cp[2].wait_recv()
    for c in cz:
        c.wait_recv()
    for c in cp + ce + ca + cw + cz + [cf]:
        c.wait_send()


def last_kernel(n, outh, gk, small, out, gkall, ssum, gkr, gkm, smr, *sems):
    (so, ro, sk, rk, sa, ra, sp, rp, ss, rs) = sems
    me, hd = lax.axis_index("seq"), lax.axis_index("head")
    mine = pl.ds(pl.multiple_of(hd * 256, 256), 256)
    peers = [lax.rem(me + i, n) for i in range(n)]
    greet(n)
    co = remote(outh, out.at[:, :, mine], so, ro, head=1 - hd)
    co.start()
    cs = []
    for i in range(1, n):
        cs.append(remote(small, smr.at[me], ss.at[i], rs.at[i], seq=peers[i]))
        cs[-1].start()
    nb = gk.shape[0] // 8

    def to(b):
        return remote(gk.at[pl.ds(8 * b, 8)], gkr.at[me], sk.at[b], rk.at[me], seq=b)

    def back(b, i):
        return remote(gkm, gkall.at[pl.ds(8 * b, 8), mine], sa.at[i], ra.at[b], seq=peers[i])

    for b in range(nb):

        @pl.when(me != b)
        def _():
            to(b).start()

    out[:, :, mine] = outh[...]
    smr[pl.ds(me, 1)] = small[...][None]
    for b in range(nb):

        @pl.when(me == b)
        def _():
            gkr[pl.ds(me, 1)] = gk[pl.ds(8 * b, 8)][None]
            for d in range(n):
                if d != b:
                    remote(gk.at[pl.ds(8 * b, 8)], gkr.at[d], sk.at[b], rk.at[d], seq=b).wait_recv()
            total = gkr[0]
            for d in range(1, n):
                total = total + gkr[d]
            gkm[...] = total
            gkall[pl.ds(8 * b, 8), mine] = total
            for i in range(1, n):
                back(b, i).start()

    for c in cs:
        c.wait_recv()
    total = smr[0]
    for d in range(1, n):
        total = total + smr[d]
    ssum[...] = total
    for b in range(nb):

        @pl.when(me != b)
        def _():
            back(b, 0).wait_recv()
            to(b).wait_send()

        @pl.when(me == b)
        def _():
            for i in range(1, n):
                back(b, i).wait_send()

    cg = remote(gkall.at[:, mine], gkall.at[:, mine], sp, rp, head=1 - hd)
    cg.start()
    cg.wait()
    co.wait()
    for c in cs:
        c.wait_send()


def load_grid(zs, pad, body, top, bottom):
    grid = body.shape[0] // GRID_W
    pad[...] = jnp.zeros_like(pad)
    pad[0:3, 8:8 + GRID_W] = top.reshape(3, GRID_W, 256)
    pad[3:3 + grid, 8:8 + GRID_W] = body.reshape(grid, GRID_W, 256)
    pad[3 + grid:6 + grid, 8:8 + GRID_W] = bottom.reshape(3, GRID_W, 256)
    for b in range(7):
        zs[b] = pad[:, 5 + b:5 + b + GRID_W, :]


def conv_row(zs, taps, i, flip):
    acc = jnp.zeros((GRID_W, 256), f32)
    for a in range(7):
        for b in range(7):
            t = 48 - (a * 7 + b) if flip else a * 7 + b
            acc = acc + taps[t:t + 1, :] * zs[b, i + a]
    return acc


def ends(me, n, top, bottom):
    top = jnp.where(me > 0, top.astype(f32), 0.0)
    bottom = jnp.where(me < n - 1, bottom.astype(f32), 0.0)
    return top, bottom


def back_conv_kernel(n, cnt, cot, halo, taps, dh, zs, pad):
    me, hd = lax.axis_index("seq"), lax.axis_index("head")
    rows = cot.shape[1]
    mine = pl.ds(pl.multiple_of(hd * 256, 256), 256)
    for s in range(2):
        top, bottom = ends(me, n, halo[0, s], halo[1, s])
        load_grid(zs, pad, cot[s, :, mine].astype(f32), top, bottom)

        @pl.loop(0, rows // GRID_W)
        def _(i):
            acc = conv_row(zs, taps, i, True)
            here = pl.ds(pl.multiple_of(i * GRID_W, GRID_W), GRID_W)
            slot = iota((GRID_W, 256), 0) + (me * rows + i * GRID_W)
            dh[s, here] = cot[s, here, mine].astype(f32) + jnp.where(slot < cnt[s], acc, 0.0)


def scores_kernel(cnt, normed, xbar, wall, dh, qt, kt, vt, qlt, klt, dot, wback, a1, e3, blk, hal):
    me = lax.axis_index("seq")
    rows = normed.shape[1]
    scale = 64 ** -0.5
    wback[...] = wall[3].astype(f32).T.astype(bf16)
    for s in range(2):
        nr = normed[s]
        qt[s] = mm(wall[0], nr, 0, 1).astype(bf16)
        kt[s] = mm(wall[1], nr, 0, 1).astype(bf16)
        slots = iota((256, rows), 1) + me * rows
        vt[s] = jnp.where(slots < cnt[s], mm(wall[2], nr, 0, 1), 0.0).astype(bf16)
        qlt[s] = mm(wall[0], xbar[s], 0, 1).astype(bf16)
        klt[s] = mm(wall[1], xbar[s], 0, 1).astype(bf16)
        dhr = dh[s].astype(bf16)
        dot[s] = mm(wback[...], dhr, 1, 1).astype(bf16)
        for side, first in ((0, 0), (1, rows - 16)):
            slot = iota((16, 256), 0) + (me * rows + first)
            v = mm(normed[s, first:first + 16], wall[2])
            hal[side, s, 0] = jnp.where(slot < cnt[s], v, 0.0).astype(bf16)
            hal[side, s, 1] = mm(dhr[first:first + 16], wback[...], 1, 1).astype(bf16)

    @pl.loop(0, 8)
    def _(p):
        s, h = p // 4, lax.rem(p, 4)
        here = pl.ds(pl.multiple_of(h * 64, 64), 64)
        count = cnt[s]
        s1 = mm(klt[s, here] * scale, qt[s, here], 0, 0)
        e1 = jnp.exp(s1 - jnp.max(s1, axis=0, keepdims=True))
        a = (e1 / jnp.sum(e1, axis=0, keepdims=True)).astype(bf16)
        a1[p] = a
        blk[p, 64:128] = mm(dot[s, here], a, 1, 1).astype(bf16)
        s3 = mm(kt[s, here] * scale, qlt[s, here], 0, 0)
        ok = iota((rows, MARKS), 0) + me * rows < count
        s3 = jnp.where(ok, s3, -1e30)
        top = jnp.max(s3, axis=0, keepdims=True)
        e = jnp.where(ok, jnp.exp(s3 - top), 0.0)
        total = jnp.sum(e, axis=0, keepdims=True)
        er = e.astype(bf16)
        e3[p] = er
        blk[p, 0:64] = mm(vt[s, here], er).astype(bf16)
        stat = jnp.concatenate(split3(top) + split3(total) + [jnp.zeros((10, MARKS), f32)], axis=0)
        blk[p, 128:144] = stat.astype(bf16)


def three(stat, first):
    return (stat[first:first + 1] + stat[first + 1:first + 2]) + stat[first + 2:first + 3]


def chain_kernel(recv, qlt, klt, res, dqz, ps, ts, xs):
    me = lax.axis_index("seq")
    pair = pair_of(me)
    s, h = pair // 4, lax.rem(pair, 4)
    here = pl.ds(pl.multiple_of(h * 64, 64), 64)
    scale = 64 ** -0.5
    parts = recv.shape[0]
    dqz[...] = jnp.zeros_like(dqz)

    @pl.when(is_owner(me))
    def _():
        tops = [three(recv[d, 128:144].astype(f32), 0) for d in range(parts)]
        top = functools.reduce(jnp.maximum, tops)
        total, value, dct = 0.0, 0.0, 0.0
        for d in range(parts):
            w = jnp.exp(tops[d] - top)
            total = total + three(recv[d, 128:144].astype(f32), 3) * w
            value = value + recv[d, 0:64].astype(f32) * w
            dct = dct + recv[d, 64:128].astype(f32)
        value = value / total
        ql, kl = qlt[s, here], klt[s, here]
        s2 = mm(ql * scale, kl, 0, 0)
        e2 = jnp.exp(s2 - jnp.max(s2, axis=1, keepdims=True))
        a = e2 / jnp.sum(e2, axis=1, keepdims=True)
        asp = split(a)
        cs, rs = jnp.sum(a, axis=0, keepdims=True), jnp.sum(a, axis=1, keepdims=True)
        cm, rm = jnp.max(cs, axis=1, keepdims=True), jnp.max(rs, axis=0, keepdims=True)
        inv = 1.0 / (cm * rm)
        p = mm3(asp, asp, 1, 1) * inv
        x = value
        for k in range(SWEEPS):
            psp = split(p)
            t = mm3(psp, psp)
            tsp = split(t)
            ps[k, 0], ps[k, 1] = psp
            ts[k, 0], ts[k, 1] = tsp
            xs[k] = x
            if k < SWEEPS - 1:
                p = 0.25 * (13.0 * p - 15.0 * t + mm3(tsp, split(7.0 * p - t)))
            xt = mm3(split(x), tsp)
            x = 0.25 * (13.0 * x + 7.0 * xt - mm3(split(15.0 * x + xt), psp))
        ct = mm3(split(x), asp) * inv
        res[0:64] = ct.astype(bf16)
        dcs = split(dct)
        y = mm3(dcs, asp, 1, 1) * inv
        da = mm3(split(x), dcs, 0, 0) * inv
        ds = -jnp.sum(jnp.sum(dct * ct, axis=0, keepdims=True), axis=1, keepdims=True) * inv * (cm * rm) * inv
        e = None
        for k in range(SWEEPS - 1, -1, -1):
            psp = (ps[k, 0], ps[k, 1])
            tsp = (ts[k, 0], ts[k, 1])
            outer = mm3(split(y), split(xs[k]), 0, 0) * 0.125
            d = outer + outer.T
            pd = mm3(psp, split(d))
            if e is None:
                v = 7.0 * pd
                w = -d
                new = -15.0 * d + mm3(split(-pd), psp)
                half = mm3(tsp, split(w))
            else:
                eq = 0.25 * e
                pe = mm3(psp, split(eq))
                v = 7.0 * pd - 15.0 * pe
                new = 13.0 * eq - 15.0 * d + mm3(split(7.0 * pe - pd), psp)
                half = mm3(tsp, split(7.0 * eq - d - (pe + pe.T)))
            half = half + v
            e = new + (half + half.T)
            yt = mm3(split(y), tsp)
            y = 0.25 * (13.0 * y + 7.0 * yt - mm3(split(15.0 * y + yt), psp))
        dbr = y.astype(bf16)
        res[64:128] = dbr
        rt = jnp.sum(dbr.astype(f32) * value, axis=0, keepdims=True)
        stat = jnp.concatenate(split3(top) + split3(total) + split3(rt) + [jnp.zeros((7, MARKS), f32)], axis=0)
        res[128:144] = stat.astype(bf16)
        da = da + mm3(split(e), asp) * (2.0 * inv)
        p0 = ps[0, 0].astype(f32) + ps[0, 1].astype(f32)
        ds = ds - jnp.sum(jnp.sum(e * p0, axis=0, keepdims=True), axis=1, keepdims=True) * inv
        eqc, eqr = jnp.where(cs == cm, 1.0, 0.0), jnp.where(rs == rm, 1.0, 0.0)
        da = da + (ds * rm) * (eqc / jnp.sum(eqc, axis=1, keepdims=True))
        da = da + (ds * cm) * (eqr / jnp.sum(eqr, axis=0, keepdims=True))
        dsc = a * (da - jnp.sum(a * da, axis=1, keepdims=True)) * scale
        dh, dl = split(dsc)
        dqz[0] = mm(kl, dh, 1, 1) + mm(kl, dl, 1, 1)
        dqz[1] = mm(ql, dh) + mm(ql, dl)


def band(base, shift, rows):
    wide = jnp.broadcast_to(base, (rows, 256))
    return pltpu.roll(wide, shift, 1, stride=1, stride_axis=0)


def diagonals(g, shift):
    return jnp.sum(pltpu.roll(g, shift, 1, stride=1, stride_axis=0), axis=0, keepdims=True)


def grads_kernel(n, cnt, normed, xbar, wall, wback, dh, qt, kt, vt, qlt, klt, dot, a1, e3, blk, res, hrecv, base, dqz,
                 po, dn, ep, wpart, gtaps, att, dp, dlm, gsum, tm, th, ht, vr):
    me = lax.axis_index("seq")
    rows = normed.shape[1]
    scale = 64 ** -0.5
    pi, pj = iota((rows, rows), 0), iota((rows, rows), 1)
    inside = (pi - pj <= 16) & (pj - pi <= 16)
    hi, hj = iota((32, rows), 0), iota((32, rows), 1)
    far = jnp.where(hi < 16, hi - hj, hj - hi - (rows - 32)) >= 0
    for f in range(2):
        for h in range(4):
            line = base[4 * f + h:4 * f + h + 1, :]
            full = jnp.where(inside, band(line, 0, rows), 0.0)
            tm[f, h, 0], tm[f, h, 1] = split(full)
            both = jnp.concatenate([band(line, 240, 16), band(line, 0, 16)], axis=0)
            th[f, h, 0], th[f, h, 1] = split(jnp.where(far, both, 0.0))
    gsum[...] = jnp.zeros_like(gsum)
    mirror = jnp.where(pi + pj == rows - 1, 1.0, 0.0).astype(bf16)
    si, sj = iota((32, 32), 0), iota((32, 32), 1)
    mirror32 = jnp.where(si + sj == jnp.where(si < 16, 15, 47), 1.0, 0.0).astype(bf16)
    for s in range(2):
        for k in range(2):
            top, bottom = ends(me, n, hrecv[0, s, k], hrecv[1, s, k])
            ht[k, s] = jnp.concatenate([top, bottom], axis=0).T.astype(bf16)
        vr[s] = mm(vt[s], mirror).astype(bf16)
        ht[2, s] = mm(ht[0, s], mirror32).astype(bf16)
    mine = pair_of(me)
    use = jnp.where(is_owner(me), 1.0, 0.0)

    @pl.loop(0, 8)
    def _(p):
        s, h = p // 4, lax.rem(p, 4)
        here = pl.ds(pl.multiple_of(h * 64, 64), 64)
        ct, dbt = res[p, 0:64], res[p, 64:128]
        stat = res[p, 128:144].astype(f32)
        own = three(blk[p, 128:144].astype(f32), 0)
        factor = jnp.exp(own - three(stat, 0)) / three(stat, 3)
        rt = three(stat, 6)
        do, v, vh, doh = dot[s, here], vt[s, here], ht[0, s, here], ht[1, s, here]
        conv = mm(v, tm[0, h, 0]) + mm(v, tm[0, h, 1]) + mm(vh, th[0, h, 0]) + mm(vh, th[0, h, 1])
        dconv = mm(do, tm[1, h, 0]) + mm(do, tm[1, h, 1]) + mm(doh, th[1, h, 0]) + mm(doh, th[1, h, 1])
        gsum[h, 0:rows] = gsum[h, 0:rows] + mm(vr[s, here], do, 0, 0)
        gsum[h, rows:rows + 32] = gsum[h, rows:rows + 32] + mm(ht[2, s, here], do, 0, 0)
        a = a1[p]
        af = a.astype(f32)
        att[s, here] = (mm(ct, a) + conv).astype(bf16)
        da = mm(ct, do, 0, 0)
        d1 = (af * (da - jnp.sum(af * da, axis=0, keepdims=True))).astype(bf16)
        dp[0, s, here] = mm(klt[s, here] * scale, d1).astype(bf16)
        own_chain = jnp.where(p == mine, use, 0.0)
        dlm[1, s, here] = (mm(qt[s, here] * scale, d1, 1, 1) + own_chain * dqz[1]).astype(bf16)
        a3 = e3[p].astype(f32) * factor
        d3 = (a3 * (mm(v, dbt, 0, 0) - rt)).astype(bf16)
        dlm[0, s, here] = (mm(kt[s, here] * scale, d3) + own_chain * dqz[0]).astype(bf16)
        dp[1, s, here] = mm(qlt[s, here] * scale, d3, 1, 1).astype(bf16)
        dv = mm(dbt, a3.astype(bf16), 1, 1) + dconv
        slot = iota((64, rows), 1) + me * rows
        dp[2, s, here] = jnp.where(slot < cnt[s], dv, 0.0).astype(bf16)

    near = (pi + pj >= rows - 17) & (pi + pj <= rows + 15)
    beyond = jnp.where(hi < 16, 15 - hi - hj, hi + hj - (rows + 15)) >= 0
    for h in range(4):
        g = jnp.where(near, gsum[h, 0:rows], 0.0)
        gh = jnp.where(beyond, gsum[h, rows:rows + 32], 0.0)
        gtaps[h:h + 1, :] = diagonals(g, 1) + diagonals(gh[0:16], 1) + diagonals(gh[16:32], 241)
    gtaps[4:8, :] = jnp.zeros((4, 256), f32)
    for j in range(3):
        g = mm(dp[j, 0], normed[0]) + mm(dp[j, 1], normed[1])
        if j < 2:
            g = g + (mm(dlm[j, 0], xbar[0]) + mm(dlm[j, 1], xbar[1]))
        wpart[j] = g.T.astype(bf16)
    g = mm(att[0], dh[0].astype(bf16)) + mm(att[1], dh[1].astype(bf16))
    wpart[3] = g.T.astype(bf16)
    for s in range(2):
        po[s] = mm(att[s], wback[...], 0, 0).astype(bf16)
        d = mm(wall[0], dp[0, s]) + mm(wall[1], dp[1, s]) + mm(wall[2], dp[2, s])
        dn[s] = d.T.astype(bf16)
        e = mm(wall[0], dlm[0, s]) + mm(wall[1], dlm[1, s])
        ep[s] = e.T.astype(bf16)


def final_kernel(n, cnt, hid, zhalo, cot, taps, pbias, tok, dh, dn, dnr, eall, gain, gtaps, outh, gx, gk, small, zs, pad, gacc):
    me, hd = lax.axis_index("seq"), lax.axis_index("head")
    rows = tok.shape[1]
    mine = pl.ds(pl.multiple_of(hd * 256, 256), 256)
    gacc[...] = jnp.zeros_like(gacc)
    small[...] = jnp.zeros_like(small)
    small[4:8, 0:256] = gtaps[0:4, :]
    for s in range(2):
        count = cnt[s]
        slot = iota((rows, 256), 0) + me * rows
        top, bottom = ends(me, n, zhalo[0, s], zhalo[1, s])
        load_grid(zs, pad, jnp.where(slot < count, hid[s], 0.0), top, bottom)

        @pl.loop(0, rows // GRID_W)
        def _(i):
            here = pl.ds(pl.multiple_of(i * GRID_W, GRID_W), GRID_W)
            acc = conv_row(zs, taps, i, False)
            outh[s, here] = (hid[s, here] + acc + pbias[:, mine]).astype(bf16)
            g = cot[s, here, mine].astype(f32)
            for a in range(7):
                for b in range(7):
                    t = a * 7 + b
                    part = (g * zs[b, i + a]).reshape(GRID_W // 8, 8, 256)
                    gacc[t] = gacc[t] + jnp.sum(part, axis=0)

        low, high = edges(count, iota((MARKS, 512), 0))
        e = (eall[s].astype(f32) / (high - low).astype(f32)).astype(bf16)
        mem = member(count, me * rows, rows)
        total = (dn[s].astype(f32) + dnr[s].astype(f32)) + mm(mem, e, 0, 0)
        x = tok[s].astype(f32)
        xc = x - jnp.mean(x, axis=-1, keepdims=True)
        inv = lax.rsqrt(jnp.mean(xc * xc, axis=-1, keepdims=True) + EPSILON)
        xh = xc * inv
        dg = total * gain[...]
        m1 = jnp.mean(dg, axis=-1, keepdims=True)
        m2 = jnp.mean(dg * xh, axis=-1, keepdims=True)
        gx[s] = dh[s] + (dg - m1 - xh * m2) * inv
        small[0:1] = small[0:1] + jnp.sum(total * xh, axis=0, keepdims=True)
        small[1:2] = small[1:2] + jnp.sum(total, axis=0, keepdims=True)
        small[2:3] = small[2:3] + jnp.sum(dh[s], axis=0, keepdims=True)
        small[3:4] = small[3:4] + jnp.sum(cot[s].astype(f32), axis=0, keepdims=True)
    for t in range(49):
        gk[t:t + 1] = jnp.sum(gacc[t], axis=0, keepdims=True)
    gk[49:56] = jnp.zeros((7, 256), f32)


def ring(rows_up, rows_down):
    count = lax.axis_size("seq")
    up = lax.ppermute(rows_up, "seq", [(i, (i + 1) % count) for i in range(count)])
    down = lax.ppermute(rows_down, "seq", [((i + 1) % count, i) for i in range(count)])
    return jnp.stack([up, down])


def half_of(full, axis):
    return lax.dynamic_slice_in_dim(full, lax.axis_index("head") * 256, 256, axis)


def start_plain(counts, xpart, wts, cot):
    low, high = edges(counts[:, None], jnp.arange(MARKS, dtype=jnp.int32)[None])
    xs = lax.psum(xpart.astype(f32), "seq") / (high - low).astype(f32)[..., None]
    xbar = lax.all_gather(xs.astype(bf16), "head", axis=2, tiled=True)
    wall = lax.all_gather(wts, "seq", axis=1, tiled=True)
    mine = half_of(cot, 2)
    return xbar, wall, ring(mine[:, -192:], mine[:, :192])


def reduce_plain(blk, hal):
    hrecv = ring(hal[1], hal[0])
    stat = blk[:, 128:].astype(f32)
    top, total = three_rows(stat, 0), three_rows(stat, 3)
    best = lax.pmax(top, "seq")
    w = jnp.exp(top - best)
    total, value, dct = lax.psum(
        (total * w, blk[:, 0:64].astype(f32) * w, blk[:, 64:128].astype(f32)), "seq"
    )
    rows = [jnp.concatenate([r[p] for p in range(8)], 0) for r in split3(best) + split3(total)]
    stat = jnp.stack(rows + [jnp.zeros_like(rows[0])] * 10, axis=1)
    whole = jnp.concatenate([value, dct, stat], axis=1).astype(bf16)
    return lax.dynamic_slice_in_dim(whole, pair_of(lax.axis_index("seq")), 1, 0), hrecv


def three_rows(stat, first):
    return (stat[:, first:first + 1] + stat[:, first + 1:first + 2]) + stat[:, first + 2:first + 3]


def spread_plain(res):
    me = lax.axis_index("seq")
    held = jnp.where((jnp.arange(8) == pair_of(me)) & is_owner(me), 1, 0)[:, None, None] == 1
    return lax.psum(jnp.where(held, res[None].astype(f32), 0.0), "seq").astype(bf16)


def late_plain(counts, tok, obias, po, ep, dn, wpart):
    rows = tok.shape[1]
    both = lax.psum(po.astype(f32), "head")
    hid = half_of(tok.astype(f32) + both + obias, 2)
    slots = lax.axis_index("seq") * rows + jnp.arange(rows)
    z = jnp.where((slots[None] < counts[:, None])[..., None], hid, 0.0).astype(bf16)
    zhalo = ring(z[:, -192:], z[:, :192])
    dnr = lax.ppermute(dn, "head", [(0, 1), (1, 0)])
    eall = lax.psum(ep.astype(f32), ("seq", "head")).astype(bf16)
    gw = lax.psum_scatter(wpart.astype(f32), "seq", scatter_dimension=1, tiled=True)
    return hid, dnr, eall, gw, zhalo


def last_plain(outh, gk, small):
    out = lax.all_gather(outh, "head", axis=2, tiled=True)
    gkall = lax.all_gather(lax.psum(gk, "seq"), "head", axis=1, tiled=True)
    return out, gkall, lax.psum(small, "seq")


def shards(n, tokens, counts, ln_gain, ln_bias, w_qkv, conv_taps, w_out, out_bias, kernel7, kernel5, kernel3, ppeg_bias, cotangent):
    rows = tokens.shape[1]
    direct = n == 16
    grid = rows // GRID_W
    mb, wr = MARKS // n, w_qkv.shape[1]
    gain, bias, obias, pbias = (v[None, :] for v in (ln_gain, ln_bias, out_bias, ppeg_bias))
    taps = kernel7 + jnp.pad(kernel5, ((1, 1), (1, 1), (0, 0))) + jnp.pad(kernel3, ((2, 2), (2, 2), (0, 0)))
    taps = half_of(taps.reshape(49, -1), 1)
    lines = jnp.concatenate([conv_taps, conv_taps[:, ::-1]], axis=0)
    base = jnp.concatenate([lines[:, 16::-1], jnp.zeros((8, 223), f32), lines[:, :16:-1]], axis=1)
    wts = jnp.concatenate([w_qkv, w_out.T[None]], axis=0)
    me_arg = counts

    normed, xpart = call(
        functools.partial(norm_kernel, rows),
        [sds((2, rows, 512), bf16), sds((2, MARKS, 256), bf16)],
        [SMEM, VMEM, VMEM, VMEM],
    )(me_arg, tokens, gain, bias)

    if direct:
        xbar, wall, halo = call(
            functools.partial(start_kernel, n),
            [sds((2, MARKS, 512), bf16), sds((4, 512, 256), bf16), sds((2, 2, 192, 256), bf16)],
            [SMEM, VMEM, VMEM, VMEM],
            [pltpu.VMEM((n, 2, mb, 256), bf16), pltpu.VMEM((2, mb, 256), bf16)]
            + [DMA((n,)), DMA((n,)), DMA((n,)), DMA((n,)), DMA((2,)), DMA((2,)), DMA, DMA, DMA((n,)), DMA((n,))],
            cid=0,
        )(counts, xpart, wts, cotangent)
    else:
        xbar, wall, halo = start_plain(counts, xpart, wts, cotangent)

    conv_scratch = [pltpu.VMEM((7, grid + 6, GRID_W, 256), f32), pltpu.VMEM((grid + 6, GRID_W + 16, 256), f32)]
    dhh = call(
        functools.partial(back_conv_kernel, n), sds((2, rows, 256)), [SMEM, VMEM, VMEM, VMEM], conv_scratch
    )(counts, cotangent, halo, taps)
    if direct:
        dh = call(fill_kernel, sds((2, rows, 512)), [VMEM], [DMA, DMA], cid=1)(dhh)
    else:
        dh = lax.all_gather(dhh, "head", axis=2, tiled=True)

    t2 = sds((2, 256, rows), bf16)
    m2 = sds((2, 256, MARKS), bf16)
    qt, kt, vt, qlt, klt, dot, wback, a1, e3, blk, hal = call(
        scores_kernel,
        [t2, t2, t2, m2, m2, t2, sds((256, 512), bf16), sds((8, MARKS, rows), bf16), sds((8, rows, MARKS), bf16),
         sds((8, BLK, MARKS), bf16), sds((2, 2, 2, 16, 256), bf16)],
        [SMEM, VMEM, VMEM, VMEM, VMEM],
    )(counts, normed, xbar, wall, dh)

    if direct:
        recv, hrecv = call(
            functools.partial(reduce_kernel, n),
            [sds((n, BLK, MARKS), bf16), sds(hal.shape, bf16)],
            [VMEM, VMEM],
            [DMA((8,)), DMA((n,)), DMA((2,)), DMA((2,))],
            cid=2,
        )(blk, hal)
    else:
        recv, hrecv = reduce_plain(blk, hal)

    square = pltpu.VMEM((SWEEPS, 2, 256, 256), bf16)
    res, dqz = call(
        chain_kernel,
        [sds((BLK, MARKS), bf16), sds((2, 64, MARKS))],
        [VMEM, VMEM, VMEM],
        [square, square, pltpu.VMEM((SWEEPS, 64, 256), f32)],
    )(recv, qlt, klt)

    if direct:
        res = call(
            functools.partial(spread_kernel, n), sds((8, BLK, MARKS), bf16), [VMEM], [DMA((n,)), DMA((8,))], cid=3
        )(res)
    else:
        res = spread_plain(res)

    po, dn, ep, wpart, gtaps = call(
        functools.partial(grads_kernel, n),
        [sds((2, rows, 512), bf16), sds((2, rows, 512), bf16), sds((2, MARKS, 512), bf16), sds((4, 512, 256), bf16),
         sds((8, 256))],
        [SMEM] + [VMEM] * 18,
        [pltpu.VMEM((2, 256, rows), bf16), pltpu.VMEM((3, 2, 256, rows), bf16), pltpu.VMEM((2, 2, 256, MARKS), bf16),
         pltpu.VMEM((4, rows + 32, rows), f32), pltpu.VMEM((2, 4, 2, rows, rows), bf16), pltpu.VMEM((2, 4, 2, 32, rows), bf16),
         pltpu.VMEM((3, 2, 256, 32), bf16), pltpu.VMEM((2, 256, rows), bf16)],
    )(counts, normed, xbar, wall, wback, dh, qt, kt, vt, qlt, klt, dot, a1, e3, blk, res, hrecv, base, dqz)

    if direct:
        hid, dnr, eall, gw, zhalo = call(
            functools.partial(late_kernel, n),
            [sds((2, rows, 256)), sds((2, rows, 512), bf16), sds((2, MARKS, 512), bf16), sds((4, wr, 256)),
             sds((2, 2, 192, 256), bf16)],
            [SMEM] + [VMEM] * 6,
            [pltpu.VMEM((2, rows, 256), bf16), pltpu.VMEM((2, MARKS, 256), bf16), pltpu.VMEM((2, MARKS, 256), bf16),
             pltpu.VMEM((n, 2, mb, 256), bf16), pltpu.VMEM((2, mb, 256), bf16), pltpu.VMEM((n, 4, wr, 256), bf16),
             pltpu.VMEM((2, rows, 256), bf16)]
            + [DMA((3,)), DMA((3,))] + [DMA((n,))] * 6 + [DMA((2,)), DMA((2,)), DMA, DMA],
            cid=4,
        )(counts, tokens, obias, po, ep, dn, wpart)
    else:
        hid, dnr, eall, gw, zhalo = late_plain(counts, tokens, obias, po, ep, dn, wpart)

    outh, gx, gk, small = call(
        functools.partial(final_kernel, n),
        [sds((2, rows, 256), bf16), sds((2, rows, 512)), sds((56, 256)), sds((8, 512))],
        [SMEM] + [VMEM] * 12,
        conv_scratch + [pltpu.VMEM((49, 8, 256), f32)],
    )(counts, hid, zhalo, cotangent, taps, pbias, tokens, dh, dn, dnr, eall, gain, gtaps)

    if direct:
        out, gk, small = call(
            functools.partial(last_kernel, n),
            [sds((2, rows, 512), bf16), sds((56, 512)), sds((8, 512))],
            [VMEM] * 3,
            [pltpu.VMEM((n, 8, 256), f32), pltpu.VMEM((8, 256), f32), pltpu.VMEM((n, 8, 512), f32),
             DMA, DMA, DMA((7,)), DMA((n,)), DMA((n,)), DMA((7,)), DMA, DMA, DMA((n,)), DMA((n,))],
            cid=5,
        )(outh, gk, small)
    else:
        out, gk, small = last_plain(outh, gk, small)

    gk = gk[:49].reshape(7, 7, 512)
    gtaps = jnp.concatenate([small[4:8, 16::-1][:, :17], small[4:8, 255:239:-1]], axis=1)
    return (
        out, gx, small[0], small[1], gw[0:3], gtaps, gw[3].T, small[2], gk, gk[1:6, 1:6], gk[2:5, 2:5], small[3],
    )


def solution(mesh):
    rows, cols = P(None, "seq", None), P(None, "seq", "head")
    return jax.shard_map(
        functools.partial(shards, mesh.shape["seq"]),
        mesh=mesh,
        in_specs=(rows, P(), P(), P(), cols, P("head", None), P("head", "seq"), P(), P(), P(), P(), P(), rows),
        out_specs=(rows, rows, P(), P(), cols, P("head", None), P("head", "seq"), P(), P(), P(), P(), P()),
        check_vma=False,
    )
```

```python
import functools

import jax
import jax.numpy as jnp
from jax import lax
from jax.experimental import pallas as pl
from jax.experimental.pallas import tpu as pltpu
from jax.sharding import PartitionSpec as P

MESH = pl.DeviceIdType.MESH
GRID_W = 64
MARKS = 256
SWEEPS = 6
EPSILON = 1e-05
f32, bf16 = jnp.float32, jnp.bfloat16
VMEM = pl.BlockSpec(memory_space=pltpu.VMEM)
SMEM = pl.BlockSpec(memory_space=pltpu.SMEM)
DMA = pltpu.SemaphoreType.DMA
BLK = 144


def sds(shape, dtype=f32):
    return jax.ShapeDtypeStruct(shape, dtype)


def call(kernel, outs, specs, scratch=(), cid=None, vmem=56):
    extra = {} if cid is None else dict(collective_id=cid, has_side_effects=True)
    return pl.pallas_call(
        kernel,
        out_shape=outs,
        in_specs=specs,
        out_specs=jax.tree.map(lambda _: VMEM, outs),
        scratch_shapes=list(scratch),
        compiler_params=pltpu.CompilerParams(vmem_limit_bytes=vmem * 2**20, **extra),
    )


def mm(left, right, cl=1, cr=0):
    return lax.dot_general(left, right, (((cl,), (cr,)), ((), ())), preferred_element_type=f32)


def split(value):
    high = value.astype(bf16)
    return high, (value - high.astype(f32)).astype(bf16)


def split3(row):
    high = row.astype(bf16).astype(f32)
    rest = row - high
    mid = rest.astype(bf16).astype(f32)
    return [high, mid, rest - mid]


def mm3(left, right, cl=1, cr=0):
    (lh, ll), (rh, rl) = left, right
    return mm(lh, rh, cl, cr) + (mm(lh, rl, cl, cr) + mm(ll, rh, cl, cr))


def iota(shape, dim):
    return lax.broadcasted_iota(jnp.int32, shape, dim)


def edges(count, marks):
    return (marks * count + (MARKS - 1)) >> 8, ((marks + 1) * count + (MARKS - 1)) >> 8


def member(count, start, rows):
    low, high = edges(count, iota((MARKS, rows), 0))
    slot = iota((MARKS, rows), 1) + start
    return jnp.where((slot >= low) & (slot < high), 1.0, 0.0).astype(bf16)

OWNERS = (0, 3, 5, 6)


def place(n):
    me = lax.axis_index("seq")
    return me // (n // 2), lax.rem(me, n // 2), lax.rem(me + n // 2, n)


def head_of(g):
    return jnp.where(g == 0, 0, jnp.where(g == 3, 1, jnp.where(g == 5, 2, 3)))


def is_owner(g):
    return (g == 0) | (g == 3) | (g == 5) | (g == 6)


def my_half():
    return pl.ds(pl.multiple_of(lax.axis_index("head") * 256, 256), 256)


def block_start(n, g, b, rows):
    return (g + b * (n // 2)) * rows


def places(n, g, rows, shape, dim):
    at = iota(shape, dim)
    return at + g * rows + jnp.where(at >= rows, (n // 2 - 1) * rows, 0)


def norm_rows(x, gain, bias):
    x = x.astype(f32)
    xc = x - jnp.mean(x, axis=-1, keepdims=True)
    inv = lax.rsqrt(jnp.mean(xc * xc, axis=-1, keepdims=True) + EPSILON)
    return (xc * inv * gain + bias).astype(bf16)


def segment_sums(n, g, count, normed):
    rows = normed.shape[1]
    mine = my_half()
    return sum(mm(member(count, block_start(n, g, b, rows), rows), normed[b, :, mine]) for b in range(2))


def join_taps(kc, k7, k5, k3):
    mine = my_half()
    kc[...] = jnp.zeros_like(kc)
    for a in range(7):
        kc[a, 0:7] = k7[a, :, mine]
    for a in range(5):
        kc[a + 1, 1:6] = kc[a + 1, 1:6] + k5[a, :, mine]
    for a in range(3):
        kc[a + 2, 2:5] = kc[a + 2, 2:5] + k3[a, :, mine]


def load_grid(zs, pad, body, top, bottom):
    grid = body.shape[0] // GRID_W
    pad[...] = jnp.zeros_like(pad)
    pad[0:3, 8:8 + GRID_W] = top.reshape(3, GRID_W, 256)
    pad[3:3 + grid, 8:8 + GRID_W] = body.reshape(grid, GRID_W, 256)
    pad[3 + grid:6 + grid, 8:8 + GRID_W] = bottom.reshape(3, GRID_W, 256)
    for b in range(7):
        zs[b] = pad[:, 5 + b:5 + b + GRID_W, :]


def conv_row(zs, kc, i, flip):
    acc = jnp.zeros((GRID_W, 256), f32)
    for a in range(7):
        for b in range(7):
            ka, kb = (6 - a, 6 - b) if flip else (a, b)
            acc = acc + kc[ka, kb:kb + 1, :] * zs[b, i + a]
    return acc


def ends(n, top, bottom):
    me = lax.axis_index("seq")
    return jnp.where(me > 0, top.astype(f32), 0.0), jnp.where(me < n - 1, bottom.astype(f32), 0.0)


def back_conv(n, count, s, cot, halo, kc, dh, zs, pad):
    me = lax.axis_index("seq")
    rows = cot.shape[1]
    mine = my_half()
    top, bottom = ends(n, halo[0, s], halo[1, s])
    load_grid(zs, pad, cot[s, :, mine].astype(f32), top, bottom)

    @pl.loop(0, rows // GRID_W)
    def _(i):
        acc = conv_row(zs, kc, i, True)
        here = pl.ds(pl.multiple_of(i * GRID_W, GRID_W), GRID_W)
        slot = iota((GRID_W, 256), 0) + (me * rows + i * GRID_W)
        dh[s, here] = cot[s, here, mine].astype(f32) + jnp.where(slot < count, acc, 0.0)


def hidden_rows(count, s, tok, obias, part, hid):
    rows = tok.shape[1]
    mine = my_half()
    hid[s] = tok[s, :, mine].astype(f32) + part.astype(f32) + obias[:, mine]
    slot = iota((rows, 256), 0) + lax.axis_index("seq") * rows
    return jnp.where(slot < count, hid[s], 0.0)


def grid_forward(n, count, s, hid, halo, cot, kc, pbias, outh, zs, pad, gacc):
    rows = hid.shape[1]
    mine = my_half()
    slot = iota((rows, 256), 0) + lax.axis_index("seq") * rows
    top, bottom = ends(n, halo[0, s], halo[1, s])
    load_grid(zs, pad, jnp.where(slot < count, hid[s], 0.0), top, bottom)

    @pl.loop(0, rows // GRID_W)
    def _(i):
        here = pl.ds(pl.multiple_of(i * GRID_W, GRID_W), GRID_W)
        acc = conv_row(zs, kc, i, False)
        outh[s, here] = (hid[s, here] + acc + pbias[:, mine]).astype(bf16)
        g = cot[s, here, mine].astype(f32)
        for a in range(7):
            for b in range(7):
                part = (g * zs[b, i + a]).reshape(GRID_W // 8, 8, 256)
                gacc[a * 7 + b] = gacc[a * 7 + b] + jnp.sum(part, axis=0)


def grid_sums(gacc, dh, cot, gtaps, gk):
    mine = my_half()
    for t in range(49):
        gk[t:t + 1] = jnp.sum(gacc[t], axis=0, keepdims=True)
    gk[49:50] = jnp.sum(dh[0], axis=0, keepdims=True) + jnp.sum(dh[1], axis=0, keepdims=True)
    g = cot[0, :, mine].astype(f32) + cot[1, :, mine].astype(f32)
    gk[50:51] = jnp.sum(g, axis=0, keepdims=True)
    gk[51:55] = gtaps[0:4]
    gk[55:56] = jnp.zeros((1, 256), f32)


def norm_back(n, g, count, b, x, dn, dnr, eall, gain, small):
    rows = x.shape[1]
    low, high = edges(count, iota((MARKS, 512), 0))
    e = (eall[...].astype(f32) / (high - low).astype(f32)).astype(bf16)
    mem = member(count, block_start(n, g, b, rows), rows)
    total = (dn[b].astype(f32) + dnr[b].astype(f32)) + mm(mem, e, 0, 0)
    x = x[b].astype(f32)
    xc = x - jnp.mean(x, axis=-1, keepdims=True)
    inv = lax.rsqrt(jnp.mean(xc * xc, axis=-1, keepdims=True) + EPSILON)
    xh = xc * inv
    dg = total * gain[...]
    m1 = jnp.mean(dg, axis=-1, keepdims=True)
    m2 = jnp.mean(dg * xh, axis=-1, keepdims=True)
    small[0:1] = small[0:1] + jnp.sum(total * xh, axis=0, keepdims=True)
    small[1:2] = small[1:2] + jnp.sum(total, axis=0, keepdims=True)
    return (dg - m1 - xh * m2) * inv


def spill_kernels(gkall, k7o, k5o, k3o):
    for a in range(7):
        k7o[a] = gkall[7 * a:7 * a + 7]
    for a in range(5):
        k5o[a] = gkall[7 * a + 8:7 * a + 13]
    for a in range(3):
        k3o[a] = gkall[7 * a + 16:7 * a + 19]


def greet(peers, pair=True):
    sem = pltpu.get_barrier_semaphore()
    for peer in peers:
        pl.semaphore_signal(sem, inc=1, device_id={"seq": peer}, device_id_type=MESH)
    if pair:
        hd = lax.axis_index("head")
        pl.semaphore_signal(sem, inc=1, device_id={"head": 1 - hd}, device_id_type=MESH)
    pl.semaphore_wait(sem, len(peers) + (1 if pair else 0))


def everyone(n):
    me = lax.axis_index("seq")
    return [lax.rem(me + i, n) for i in range(n)]


def cube(n):
    half, g, _ = place(n)
    return [half * (n // 2) + lax.rem(g + i, n // 2) for i in range(n // 2)]


def remote(src, dst, sems, i, **where):
    return pltpu.make_async_remote_copy(
        src_ref=src, dst_ref=dst, send_sem=sems.at[0, i], recv_sem=sems.at[1, i], device_id=where, device_id_type=MESH
    )


def go(copies):
    for c in copies:
        c.start()
    return copies


def got(copies):
    for c in copies:
        c.wait_recv()


def sent(copies):
    for c in copies:
        c.wait_send()


def start_kernel(n, cnt, tok, cot, gain, bias, wqkv, wout, k7, k5, k3,
                 xblk, normed, xbar, wall, dh, dhrb,
                 wts, halo, xp, xr, xm, kc, zs, pad, dhs, s_w, s_t, s_h, s_v, s_x, s_g, s_p, s_d):
    half, g, partner = place(n)
    me = lax.axis_index("seq")
    other = 1 - half
    size = n // 2
    rows = tok.shape[1]
    mb, wr = MARKS // size, wts.shape[1]
    hd = lax.axis_index("head")
    mine = my_half()
    count = cnt[half]
    near, far = cube(n), everyone(n)
    wts[0:3] = wqkv[...]
    wts[3] = wout[...].astype(f32).T.astype(bf16)

    def wrow(device):
        return pl.ds(pl.multiple_of(device * wr, wr), wr)

    greet(far[1:])
    c_w = go([remote(wts, wall.at[:, wrow(me)], s_w, 0, seq=partner)])
    c_t = go([remote(tok.at[other, :, mine], xblk.at[half, :, mine], s_t, 0, seq=partner)])
    c_h = go([
        remote(cot.at[:, pl.ds(rows - 192, 192), mine], halo.at[0], s_h, 0, seq=far[1]),
        remote(cot.at[:, pl.ds(0, 192), mine], halo.at[1], s_h, 1, seq=far[n - 1]),
    ])
    wall[:, wrow(me)] = wts[...]
    xblk[half] = tok[half]
    normed[half] = norm_rows(tok[half], gain[...], bias[...])
    join_taps(kc, k7, k5, k3)
    got(c_w)
    c_v = []
    for i in range(1, size):
        c_v += go([remote(wts, wall.at[:, wrow(me)], s_v, 2 * i, seq=near[i])])
        c_v += go([remote(wall.at[:, wrow(partner)], wall.at[:, wrow(partner)], s_v, 2 * i + 1, seq=near[i])])
    got(c_t)
    c_p = go([remote(xblk.at[other, :, mine], xblk.at[other, :, mine], s_p, 0, head=1 - hd)])
    got(c_p)
    normed[other] = norm_rows(xblk[other], gain[...], bias[...])
    xp[...] = segment_sums(n, g, count, normed).astype(bf16)
    c_x = []
    for i in range(1, size):
        at = pl.ds(pl.multiple_of(lax.rem(g + i, size) * mb, mb), mb)
        c_x += go([remote(xp.at[at], xr.at[g], s_x, i, seq=near[i])])
    row = pl.ds(pl.multiple_of(g * mb, mb), mb)
    xr[pl.ds(g, 1)] = xp[row][None]
    got(c_h)
    back_conv(n, cnt[other], other, cot, halo, kc, dh, zs, pad)
    dhs[...] = dh[other].astype(bf16)
    c_d = go([remote(dhs, dhrb.at[half, :, mine], s_d, 0, seq=partner)])
    got(c_x)
    total = xr[0].astype(f32)
    for d in range(1, size):
        total = total + xr[d].astype(f32)
    low, high = edges(count, iota((mb, 256), 0) + g * mb)
    xm[...] = (total / (high - low).astype(f32)).astype(bf16)
    xbar[row, mine] = xm[...]
    c_g = go([remote(xm, xbar.at[row, mine], s_g, i, seq=near[i]) for i in range(1, size)])
    back_conv(n, cnt[half], half, cot, halo, kc, dh, zs, pad)
    dhrb[half, :, mine] = dh[half].astype(bf16)
    got(c_g)
    c_p += go([remote(xbar.at[:, mine], xbar.at[:, mine], s_p, 1, head=1 - hd)])
    got(c_d)
    c_p += go([remote(dhrb.at[:, :, mine], dhrb.at[:, :, mine], s_p, 2, head=1 - hd)])
    got(c_v)
    got(c_p[1:])
    sent(c_w + c_t + c_h + c_v + c_x + c_d + c_g + c_p)


def reduce_kernel(n, blk, hal, recv, hrecv, s_b, s_h):
    half, g, _ = place(n)
    size = n // 2
    near = cube(n)
    greet(near[1:], False)

    def to(h, d):
        return pltpu.make_async_remote_copy(
            src_ref=blk.at[h], dst_ref=recv.at[d], send_sem=s_b.at[0, h], recv_sem=s_b.at[1, d],
            device_id={"seq": half * size + OWNERS[h]}, device_id_type=MESH,
        )

    for h, o in enumerate(OWNERS):

        @pl.when(g != o)
        def _():
            to(h, g).start()

        @pl.when(g == o)
        def _():
            recv[pl.ds(g, 1)] = blk[h:h + 1]

    c_h = go([
        remote(hal.at[1], hrecv.at[0], s_h, 0, seq=near[1]),
        remote(hal.at[0], hrecv.at[1], s_h, 1, seq=near[size - 1]),
    ])
    for c in c_h:
        c.wait()
    for h, o in enumerate(OWNERS):

        @pl.when(g != o)
        def _():
            to(h, g).wait_send()

        @pl.when(g == o)
        def _():
            for d in range(size):
                if d != o:
                    to(h, d).wait_recv()


def spread_kernel(n, res, out, s_r):
    half, g, _ = place(n)
    size = n // 2
    near = cube(n)
    greet(near[1:], False)

    def to(h, i):
        return pltpu.make_async_remote_copy(
            src_ref=res, dst_ref=out.at[h], send_sem=s_r.at[0, i], recv_sem=s_r.at[1, h],
            device_id={"seq": near[i]}, device_id_type=MESH,
        )

    for h, o in enumerate(OWNERS):

        @pl.when(g == o)
        def _():
            for i in range(1, size):
                to(h, i).start()
            out[h] = res[...]

    for h, o in enumerate(OWNERS):

        @pl.when(g != o)
        def _():
            to(h, 1).wait_recv()

        @pl.when(g == o)
        def _():
            for i in range(1, size):
                to(h, i).wait_send()


def late_kernel(n, cnt, tok, cot, xblk, dh, po, ep, dn, wpart, gtaps, gain, obias, pbias, k7, k5, k3,
                out, gx, gwqkv, gwout, sums, gkall, k7o, k5o, k3o,
                er, es, erv, em, eall, por, ps, psr, dnr, dhr, hid, z, halo, lnb, lnr, lns, wrv, wsum, wone,
                kc, zs, pad, gacc, outh, gk, gkr, gkm, small, smr, smx,
                s_a, s_e, s_g, s_o, s_z, s_l, s_w, s_v, s_k, s_b, s_s):
    half, g, partner = place(n)
    me = lax.axis_index("seq")
    other = 1 - half
    size = n // 2
    rows = tok.shape[1]
    mb, wr = MARKS // size, wone.shape[1]
    hd = lax.axis_index("head")
    mine = my_half()
    theirs = pl.ds(pl.multiple_of((1 - hd) * 256, 256), 256)
    count = cnt[half]
    near, far = cube(n), everyone(n)
    greet(far[1:])
    c_a = go([
        remote(ep.at[:, theirs], er, s_a, 0, head=1 - hd),
        remote(po.at[:, :, theirs], por, s_a, 1, head=1 - hd),
        remote(dn, dnr, s_a, 2, head=1 - hd),
        remote(dh, dhr, s_a, 3, head=1 - hd),
    ])
    got(c_a[0:1])
    es[...] = (ep[:, mine].astype(f32) + er[...].astype(f32)).astype(bf16)
    c_e = []
    for i in range(1, size):
        at = pl.ds(pl.multiple_of(lax.rem(g + i, size) * mb, mb), mb)
        c_e += go([remote(es.at[at], erv.at[g], s_e, i, seq=near[i])])
    row = pl.ds(pl.multiple_of(g * mb, mb), mb)
    erv[pl.ds(g, 1)] = es[row][None]
    got(c_a[1:2])
    ps[...] = (po[:, :, mine].astype(f32) + por[...].astype(f32)).astype(bf16)
    c_o = go([remote(ps.at[other], psr, s_o, 0, seq=partner)])
    join_taps(kc, k7, k5, k3)
    small[...] = jnp.zeros_like(small)
    gacc[...] = jnp.zeros_like(gacc)
    got(c_e)
    total = erv[0].astype(f32)
    for d in range(1, size):
        total = total + erv[d].astype(f32)
    em[...] = total.astype(bf16)
    eall[row, mine] = em[...]
    c_g = go([remote(em, eall.at[row, mine], s_g, i, seq=near[i]) for i in range(1, size)])

    def wrow(device):
        return pl.ds(pl.multiple_of(device * wr, wr), wr)

    c_w = []
    for i in range(1, size):
        for k, device in enumerate((near[i], lax.rem(near[i] + size, n))):
            c_w += go([remote(wpart.at[:, wrow(device)], wrv.at[g, k], s_w, 2 * i + k, seq=near[i])])
    wrv[pl.ds(g, 1), 0] = wpart[:, wrow(me)][None]
    wrv[pl.ds(g, 1), 1] = wpart[:, wrow(partner)][None]
    z[half] = hidden_rows(count, half, tok, obias, ps[half], hid).astype(bf16)
    got(c_o)
    z[other] = hidden_rows(cnt[other], other, tok, obias, psr[...], hid).astype(bf16)
    c_z = go([
        remote(z.at[:, pl.ds(rows - 192, 192)], halo.at[0], s_z, 0, seq=far[1]),
        remote(z.at[:, pl.ds(0, 192)], halo.at[1], s_z, 1, seq=far[n - 1]),
    ])
    got(c_g)
    c_a += go([remote(eall.at[:, mine], eall.at[:, mine], s_a, 4, head=1 - hd)])
    got(c_a[2:5])
    lnb[...] = norm_back(n, g, count, other, xblk, dn, dnr, eall, gain, small)
    lns[...] = lnb[:, mine].astype(bf16)
    c_l = go([remote(lns, lnr.at[:, mine], s_l, 0, seq=partner)])
    lnb[...] = norm_back(n, g, count, half, xblk, dn, dnr, eall, gain, small)
    gx[half, :, mine] = dh[half] + lnb[:, mine]
    gx[half, :, theirs] = dhr[half] + lnb[:, theirs]
    for a in range(2):
        for b in range(4):
            smx[4 * a + b:4 * a + b + 1] = small[a:a + 1, 128 * b:128 * b + 128]
    c_s = go([remote(smx, smr.at[me], s_s, i, seq=far[i]) for i in range(1, n)])
    smr[pl.ds(me, 1)] = smx[...][None]
    got(c_l)
    c_l += go([remote(lnr.at[:, mine], lnr.at[:, mine], s_l, 1, head=1 - hd)])
    got(c_z)
    for s in range(2):
        grid_forward(n, cnt[s], s, hid, halo, cot, kc, pbias, outh, zs, pad, gacc)
    c_l += go([remote(outh, out.at[:, :, mine], s_l, 2, head=1 - hd)])
    out[:, :, mine] = outh[...]
    grid_sums(gacc, dh, cot, gtaps, gk)
    blocks = gk.shape[0] // 8

    def to(b, d):
        return pltpu.make_async_remote_copy(
            src_ref=gk.at[pl.ds(8 * b, 8)], dst_ref=gkr.at[d], send_sem=s_k.at[0, b], recv_sem=s_k.at[1, d],
            device_id={"seq": b}, device_id_type=MESH,
        )

    def back(b, i):
        return pltpu.make_async_remote_copy(
            src_ref=gkm, dst_ref=gkall.at[pl.ds(8 * b, 8), mine], send_sem=s_b.at[0, i], recv_sem=s_b.at[1, b],
            device_id={"seq": far[i]}, device_id_type=MESH,
        )

    for b in range(blocks):

        @pl.when(me != b)
        def _():
            to(b, me).start()

    got(c_w)
    for k in (1, 0):
        total = wrv[0, k].astype(f32)
        for d in range(1, size):
            total = total + wrv[d, k].astype(f32)
        if k == 1:
            wsum[...] = total.astype(bf16)
            c_v = go([remote(wsum, wone, s_v, 0, seq=partner)])
    for b in range(blocks):

        @pl.when(me == b)
        def _():
            gkr[pl.ds(me, 1)] = gk[pl.ds(8 * b, 8)][None]
            for d in range(n):
                if d != b:
                    to(b, d).wait_recv()
            gsum = gkr[0]
            for d in range(1, n):
                gsum = gsum + gkr[d]
            gkm[...] = gsum
            gkall[pl.ds(8 * b, 8), mine] = gsum
            for i in range(1, n):
                back(b, i).start()

    got(c_l[1:2])
    gx[other, :, mine] = dh[other] + lnr[:, mine].astype(f32)
    gx[other, :, theirs] = dhr[other] + lnr[:, theirs].astype(f32)
    got(c_s)
    acc = smr[0]
    for d in range(1, n):
        acc = acc + smr[d]
    sums[...] = acc
    got(c_v)
    total = total + wone[...].astype(f32)
    gwqkv[...] = total[0:3]
    gwout[...] = total[3].T
    for b in range(blocks):

        @pl.when(me != b)
        def _():
            back(b, 0).wait_recv()
            to(b, me).wait_send()

        @pl.when(me == b)
        def _():
            for i in range(1, n):
                back(b, i).wait_send()

    c_k = go([remote(gkall.at[:, mine], gkall.at[:, mine], s_l, 3, head=1 - hd)])
    got(c_k)
    spill_kernels(gkall, k7o, k5o, k3o)
    got(c_l[2:])
    sent(c_a + c_e + c_o + c_g + c_w + c_z + c_l + c_s + c_v + c_k)


def scores_kernel(n, cnt, normed, xbar, wall, dhrb, qt, kt, vt, qlt, klt, dot, wback, a1, e3, blk, hal):
    half, g, _ = place(n)
    rows = normed.shape[1]
    wide = 2 * rows
    count = cnt[half]
    scale = 64 ** -0.5
    wback[...] = wall[3].astype(f32).T.astype(bf16)
    nr = normed[...].reshape(wide, 512)
    dhr = dhrb[...].reshape(wide, 512)
    qt[...] = mm(wall[0], nr, 0, 1).astype(bf16)
    kt[...] = mm(wall[1], nr, 0, 1).astype(bf16)
    slots = places(n, g, rows, (256, wide), 1)
    vt[...] = jnp.where(slots < count, mm(wall[2], nr, 0, 1), 0.0).astype(bf16)
    qlt[...] = mm(wall[0], xbar[...], 0, 1).astype(bf16)
    klt[...] = mm(wall[1], xbar[...], 0, 1).astype(bf16)
    dot[...] = mm(wback[...], dhr, 1, 1).astype(bf16)
    for b in range(2):
        for side, first in ((0, 0), (1, rows - 16)):
            slot = iota((16, 256), 0) + (block_start(n, g, b, rows) + first)
            v = mm(normed[b, first:first + 16], wall[2])
            hal[side, b, 0] = jnp.where(slot < count, v, 0.0).astype(bf16)
            hal[side, b, 1] = mm(dhrb[b, first:first + 16], wback[...], 1, 1).astype(bf16)
    ok = places(n, g, rows, (wide, MARKS), 0) < count

    @pl.loop(0, 4)
    def _(h):
        here = pl.ds(pl.multiple_of(h * 64, 64), 64)
        s1 = mm(klt[here] * scale, qt[here], 0, 0)
        e1 = jnp.exp(s1 - jnp.max(s1, axis=0, keepdims=True))
        a = (e1 / jnp.sum(e1, axis=0, keepdims=True)).astype(bf16)
        a1[h] = a
        blk[h, 64:128] = mm(dot[here], a, 1, 1).astype(bf16)
        s3 = jnp.where(ok, mm(kt[here] * scale, qlt[here], 0, 0), -1e30)
        top = jnp.max(s3, axis=0, keepdims=True)
        e = jnp.where(ok, jnp.exp(s3 - top), 0.0)
        total = jnp.sum(e, axis=0, keepdims=True)
        er = e.astype(bf16)
        e3[h] = er
        blk[h, 0:64] = mm(vt[here], er).astype(bf16)
        stat = jnp.concatenate(split3(top) + split3(total) + [jnp.zeros((10, MARKS), f32)], axis=0)
        blk[h, 128:144] = stat.astype(bf16)


def three(stat, first):
    return (stat[first:first + 1] + stat[first + 1:first + 2]) + stat[first + 2:first + 3]


def chain_kernel(n, recv, qlt, klt, res, dqz, ps, ts, xs):
    _, g, _ = place(n)
    h = head_of(g)
    here = pl.ds(pl.multiple_of(h * 64, 64), 64)
    scale = 64 ** -0.5
    parts = recv.shape[0]
    dqz[...] = jnp.zeros_like(dqz)

    @pl.when(is_owner(g))
    def _():
        tops = [three(recv[d, 128:144].astype(f32), 0) for d in range(parts)]
        top = functools.reduce(jnp.maximum, tops)
        total, value, dct = 0.0, 0.0, 0.0
        for d in range(parts):
            w = jnp.exp(tops[d] - top)
            total = total + three(recv[d, 128:144].astype(f32), 3) * w
            value = value + recv[d, 0:64].astype(f32) * w
            dct = dct + recv[d, 64:128].astype(f32)
        value = value / total
        ql, kl = qlt[here], klt[here]
        s2 = mm(ql * scale, kl, 0, 0)
        e2 = jnp.exp(s2 - jnp.max(s2, axis=1, keepdims=True))
        a = e2 / jnp.sum(e2, axis=1, keepdims=True)
        asp = split(a)
        cs, rs = jnp.sum(a, axis=0, keepdims=True), jnp.sum(a, axis=1, keepdims=True)
        cm, rm = jnp.max(cs, axis=1, keepdims=True), jnp.max(rs, axis=0, keepdims=True)
        inv = 1.0 / (cm * rm)
        p = mm3(asp, asp, 1, 1) * inv
        x = value
        for k in range(SWEEPS):
            psp = split(p)
            t = mm3(psp, psp)
            tsp = split(t)
            ps[k, 0], ps[k, 1] = psp
            ts[k, 0], ts[k, 1] = tsp
            xs[k] = x
            if k < SWEEPS - 1:
                p = 0.25 * (13.0 * p - 15.0 * t + mm3(tsp, split(7.0 * p - t)))
            xt = mm3(split(x), tsp)
            x = 0.25 * (13.0 * x + 7.0 * xt - mm3(split(15.0 * x + xt), psp))
        ct = mm3(split(x), asp) * inv
        res[0:64] = ct.astype(bf16)
        dcs = split(dct)
        y = mm3(dcs, asp, 1, 1) * inv
        da = mm3(split(x), dcs, 0, 0) * inv
        ds = -jnp.sum(jnp.sum(dct * ct, axis=0, keepdims=True), axis=1, keepdims=True) * inv * (cm * rm) * inv
        e = None
        for k in range(SWEEPS - 1, -1, -1):
            psp = (ps[k, 0], ps[k, 1])
            tsp = (ts[k, 0], ts[k, 1])
            outer = mm3(split(y), split(xs[k]), 0, 0) * 0.125
            d = outer + outer.T
            pd = mm3(psp, split(d))
            if e is None:
                v = 7.0 * pd
                w = -d
                new = -15.0 * d + mm3(split(-pd), psp)
                half = mm3(tsp, split(w))
            else:
                eq = 0.25 * e
                pe = mm3(psp, split(eq))
                v = 7.0 * pd - 15.0 * pe
                new = 13.0 * eq - 15.0 * d + mm3(split(7.0 * pe - pd), psp)
                half = mm3(tsp, split(7.0 * eq - d - (pe + pe.T)))
            half = half + v
            e = new + (half + half.T)
            yt = mm3(split(y), tsp)
            y = 0.25 * (13.0 * y + 7.0 * yt - mm3(split(15.0 * y + yt), psp))
        dbr = y.astype(bf16)
        res[64:128] = dbr
        rt = jnp.sum(dbr.astype(f32) * value, axis=0, keepdims=True)
        stat = jnp.concatenate(split3(top) + split3(total) + split3(rt) + [jnp.zeros((7, MARKS), f32)], axis=0)
        res[128:144] = stat.astype(bf16)
        da = da + mm3(split(e), asp) * (2.0 * inv)
        p0 = ps[0, 0].astype(f32) + ps[0, 1].astype(f32)
        ds = ds - jnp.sum(jnp.sum(e * p0, axis=0, keepdims=True), axis=1, keepdims=True) * inv
        eqc, eqr = jnp.where(cs == cm, 1.0, 0.0), jnp.where(rs == rm, 1.0, 0.0)
        da = da + (ds * rm) * (eqc / jnp.sum(eqc, axis=1, keepdims=True))
        da = da + (ds * cm) * (eqr / jnp.sum(eqr, axis=0, keepdims=True))
        dsc = a * (da - jnp.sum(a * da, axis=1, keepdims=True)) * scale
        dh, dl = split(dsc)
        dqz[0] = mm(kl, dh, 1, 1) + mm(kl, dl, 1, 1)
        dqz[1] = mm(ql, dh) + mm(ql, dl)


def band(base, shift, rows):
    wide = jnp.broadcast_to(base, (rows, 256))
    return pltpu.roll(wide, shift, 1, stride=1, stride_axis=0)


def diagonals(g, shift):
    return jnp.sum(pltpu.roll(g, shift, 1, stride=1, stride_axis=0), axis=0, keepdims=True)


def ring_ends(n, g, b, hrecv, k):
    top = jnp.where(g > 0, hrecv[0, b, k].astype(f32), hrecv[0, 0, k].astype(f32) if b else 0.0)
    bottom = jnp.where(g < n // 2 - 1, hrecv[1, b, k].astype(f32), 0.0 if b else hrecv[1, 1, k].astype(f32))
    return top, bottom


def grads_kernel(n, cnt, normed, xbar, wall, wback, dhrb, qt, kt, vt, qlt, klt, dot, a1, e3, blk, res, hrecv, taps, dqz,
                 po, dn, ep, wpart, gtaps, att, dp, dlm, gsum, tm, th, ht, vr):
    half, g, _ = place(n)
    rows = normed.shape[1]
    wide = 2 * rows
    count = cnt[half]
    scale = 64 ** -0.5
    pi, pj = iota((rows, rows), 0), iota((rows, rows), 1)
    inside = (pi - pj <= 16) & (pj - pi <= 16)
    hi, hj = iota((32, rows), 0), iota((32, rows), 1)
    far = jnp.where(hi < 16, hi - hj, hj - hi - (rows - 32)) >= 0
    ti, tl = iota((33, 256), 0), iota((33, 256), 1)
    spots = [jnp.where(((ti + tl if f == 0 else tl - ti + 32) & 255) == 16, 1.0, 0.0).astype(bf16) for f in range(2)]
    pieces = [piece.astype(bf16) for piece in split3(taps[...])]
    for f in range(2):
        lines = mm(pieces[0], spots[f]) + mm(pieces[1], spots[f]) + mm(pieces[2], spots[f])
        for h in range(4):
            line = lines[h:h + 1, :]
            full = jnp.where(inside, band(line, 0, rows), 0.0)
            tm[f, h, 0], tm[f, h, 1] = split(full)
            both = jnp.concatenate([band(line, 240, 16), band(line, 0, 16)], axis=0)
            th[f, h, 0], th[f, h, 1] = split(jnp.where(far, both, 0.0))
    gsum[...] = jnp.zeros_like(gsum)
    mirror = jnp.where(pi + pj == rows - 1, 1.0, 0.0).astype(bf16)
    si, sj = iota((32, 32), 0), iota((32, 32), 1)
    mirror32 = jnp.where(si + sj == jnp.where(si < 16, 15, 47), 1.0, 0.0).astype(bf16)
    for b in range(2):
        for k in range(2):
            top, bottom = ring_ends(n, g, b, hrecv, k)
            ht[k, b] = jnp.concatenate([top, bottom], axis=0).T.astype(bf16)
        vr[b] = mm(vt[:, b * rows:(b + 1) * rows], mirror).astype(bf16)
        ht[2, b] = mm(ht[0, b], mirror32).astype(bf16)
    mine = head_of(g)
    use = jnp.where(is_owner(g), 1.0, 0.0)
    slots = places(n, g, rows, (64, wide), 1)

    @pl.loop(0, 4)
    def _(h):
        here = pl.ds(pl.multiple_of(h * 64, 64), 64)
        ct, dbt = res[h, 0:64], res[h, 64:128]
        stat = res[h, 128:144].astype(f32)
        own = three(blk[h, 128:144].astype(f32), 0)
        factor = jnp.exp(own - three(stat, 0)) / three(stat, 3)
        rt = three(stat, 6)
        do, v = dot[here], vt[here]
        conv, dconv = [], []
        for b in range(2):
            part = slice(b * rows, (b + 1) * rows)
            vb, db, vh, dh = v[:, part], do[:, part], ht[0, b, here], ht[1, b, here]
            conv.append(mm(vb, tm[0, h, 0]) + mm(vb, tm[0, h, 1]) + mm(vh, th[0, h, 0]) + mm(vh, th[0, h, 1]))
            dconv.append(mm(db, tm[1, h, 0]) + mm(db, tm[1, h, 1]) + mm(dh, th[1, h, 0]) + mm(dh, th[1, h, 1]))
            gsum[h, 0:rows] = gsum[h, 0:rows] + mm(vr[b, here], db, 0, 0)
            gsum[h, rows:rows + 32] = gsum[h, rows:rows + 32] + mm(ht[2, b, here], db, 0, 0)
        a = a1[h]
        af = a.astype(f32)
        att[here] = (mm(ct, a) + jnp.concatenate(conv, axis=1)).astype(bf16)
        da = mm(ct, do, 0, 0)
        d1 = (af * (da - jnp.sum(af * da, axis=0, keepdims=True))).astype(bf16)
        dp[0, here] = mm(klt[here] * scale, d1).astype(bf16)
        own_chain = jnp.where(h == mine, use, 0.0)
        dlm[1, here] = (mm(qt[here] * scale, d1, 1, 1) + own_chain * dqz[1]).astype(bf16)
        a3 = e3[h].astype(f32) * factor
        d3 = (a3 * (mm(v, dbt, 0, 0) - rt)).astype(bf16)
        dlm[0, here] = (mm(kt[here] * scale, d3) + own_chain * dqz[0]).astype(bf16)
        dp[1, here] = mm(qlt[here] * scale, d3, 1, 1).astype(bf16)
        dv = mm(dbt, a3.astype(bf16), 1, 1) + jnp.concatenate(dconv, axis=1)
        dp[2, here] = jnp.where(slots < count, dv, 0.0).astype(bf16)

    ep[...] = (mm(wall[0], dlm[0]) + mm(wall[1], dlm[1])).T.astype(bf16)
    po[...] = mm(att[...], wback[...], 0, 0).astype(bf16).reshape(2, rows, 512)
    d = mm(wall[0], dp[0]) + mm(wall[1], dp[1]) + mm(wall[2], dp[2])
    dn[...] = d.T.astype(bf16).reshape(2, rows, 512)
    nr = normed[...].reshape(wide, 512)
    for j in range(3):
        grad = mm(dp[j], nr)
        if j < 2:
            grad = grad + mm(dlm[j], xbar[...])
        wpart[j] = grad.T.astype(bf16)
    wpart[3] = mm(att[...], dhrb[...].reshape(wide, 512)).T.astype(bf16)
    near = (pi + pj >= rows - 17) & (pi + pj <= rows + 15)
    beyond = jnp.where(hi < 16, 15 - hi - hj, hi + hj - (rows + 15)) >= 0
    for h in range(4):
        s = jnp.where(near, gsum[h, 0:rows], 0.0)
        sh = jnp.where(beyond, gsum[h, rows:rows + 32], 0.0)
        gtaps[h:h + 1, :] = diagonals(s, 1) + diagonals(sh[0:16], 1) + diagonals(sh[16:32], 241)
    gtaps[4:8, :] = jnp.zeros((4, 256), f32)


def ring(rows_up, rows_down):
    count = lax.axis_size("seq")
    up = lax.ppermute(rows_up, "seq", [(i, (i + 1) % count) for i in range(count)])
    down = lax.ppermute(rows_down, "seq", [((i + 1) % count, i) for i in range(count)])
    return jnp.stack([up, down])


def half_of(full, axis):
    return lax.dynamic_slice_in_dim(full, lax.axis_index("head") * 256, 256, axis)


def swap(n, blocks):
    half, _, _ = place(n)
    theirs = lax.ppermute(jnp.where(half == 0, blocks[1], blocks[0]), "seq", [(i, (i + n // 2) % n) for i in range(n)])
    own = jnp.where(half == 0, blocks[0], blocks[1])
    return jnp.where(half == 0, jnp.stack([own, theirs]), jnp.stack([theirs, own]))


def half_sum(n, value):
    half, _, _ = place(n)
    pair = lax.psum(jnp.stack([jnp.where(half == s, value, 0.0) for s in range(2)]), "seq")
    return jnp.where(half == 0, pair[0], pair[1])


def half_max(n, value):
    half, _, _ = place(n)
    pair = lax.pmax(jnp.stack([jnp.where(half == s, value, -jnp.inf) for s in range(2)]), "seq")
    return jnp.where(half == 0, pair[0], pair[1])


def norm_kernel(n, cnt, xblk, gain, bias, normed, xp):
    half, g, _ = place(n)
    for b in range(2):
        normed[b] = norm_rows(xblk[b], gain[...], bias[...])
    xp[...] = segment_sums(n, g, cnt[half], normed)


def back_conv_kernel(n, cnt, cot, halo, k7, k5, k3, dh, kc, zs, pad):
    join_taps(kc, k7, k5, k3)
    for s in range(2):
        back_conv(n, cnt[s], s, cot, halo, kc, dh, zs, pad)


def start_plain(n, counts, tok, cot, gain, bias, wqkv, wout, k7, k5, k3, scratch):
    half, _, _ = place(n)
    rows = tok.shape[1]
    count = counts[half]
    xblk = swap(n, tok)
    normed, xp = call(
        functools.partial(norm_kernel, n), [sds((2, rows, 512), bf16), sds((MARKS, 256))], [SMEM] + [VMEM] * 3
    )(counts, xblk, gain, bias)
    low, high = edges(count, jnp.arange(MARKS, dtype=jnp.int32))
    xbar = (half_sum(n, xp) / (high - low).astype(f32)[:, None]).astype(bf16)
    xbar = lax.all_gather(xbar, "head", axis=1, tiled=True)
    wts = jnp.concatenate([wqkv, wout.T[None]], axis=0)
    wall = lax.all_gather(wts, "seq", axis=1, tiled=True)
    mine = half_of(cot, 2)
    dh = call(functools.partial(back_conv_kernel, n), sds((2, rows, 256)), [SMEM] + [VMEM] * 5, scratch)(
        counts, cot, ring(mine[:, -192:], mine[:, :192]), k7, k5, k3
    )
    dhrb = swap(n, lax.all_gather(dh.astype(bf16), "head", axis=2, tiled=True))
    return xblk, normed, xbar, wall, dh, dhrb


def half_ring(n, hal):
    size = n // 2
    up = [(i, i // size * size + (i + 1) % size) for i in range(n)]
    return jnp.stack([lax.ppermute(hal[1], "seq", up), lax.ppermute(hal[0], "seq", [(j, i) for i, j in up])])


def three_rows(stat, first):
    return (stat[:, first:first + 1] + stat[:, first + 1:first + 2]) + stat[:, first + 2:first + 3]


def reduce_plain(n, blk, hal):
    _, g, _ = place(n)
    stat = blk[:, 128:].astype(f32)
    top, total = three_rows(stat, 0), three_rows(stat, 3)
    best = half_max(n, top)
    w = jnp.exp(top - best)
    total = half_sum(n, total * w)
    value = half_sum(n, blk[:, 0:64].astype(f32) * w)
    dct = half_sum(n, blk[:, 64:128].astype(f32))
    stat = jnp.concatenate(split3(best) + split3(total) + [jnp.zeros((4, 10, MARKS), f32)], axis=1)
    whole = jnp.concatenate([value, dct, stat], axis=1).astype(bf16)
    return lax.dynamic_slice_in_dim(whole, head_of(g), 1, 0), half_ring(n, hal)


def spread_plain(n, res):
    _, g, _ = place(n)
    held = ((jnp.arange(4) == head_of(g)) & is_owner(g))[:, None, None]
    return half_sum(n, jnp.where(held, res[None].astype(f32), 0.0)).astype(bf16)


def hidden_kernel(cnt, tok, obias, part, hid, z):
    for s in range(2):
        z[s] = hidden_rows(cnt[s], s, tok, obias, part[s], hid).astype(bf16)


def final_kernel(n, cnt, hid, halo, cot, k7, k5, k3, pbias, xblk, dn, dnr, eall, gain, dh, gtaps,
                 outh, lnb, gk, small, kc, zs, pad, gacc):
    half, g, _ = place(n)
    join_taps(kc, k7, k5, k3)
    gacc[...] = jnp.zeros_like(gacc)
    small[...] = jnp.zeros_like(small)
    for s in range(2):
        grid_forward(n, cnt[s], s, hid, halo, cot, kc, pbias, outh, zs, pad, gacc)
    grid_sums(gacc, dh, cot, gtaps, gk)
    for b in range(2):
        lnb[b] = norm_back(n, g, cnt[half], b, xblk, dn, dnr, eall, gain, small)


def late_plain(n, counts, tok, cot, xblk, dh, po, ep, dn, wpart, gtaps, gain, obias, pbias, k7, k5, k3, scratch):
    rows = tok.shape[1]
    part = half_of(swap(n, lax.psum(po.astype(f32), "head").astype(bf16)), 2)
    hid, z = call(hidden_kernel, [sds((2, rows, 256)), sds((2, rows, 256), bf16)], [SMEM] + [VMEM] * 3)(
        counts, tok, obias, part
    )
    dnr = lax.ppermute(dn, "head", [(0, 1), (1, 0)])
    eall = half_sum(n, lax.psum(ep.astype(f32), "head")).astype(bf16)
    outh, lnb, gk, small = call(
        functools.partial(final_kernel, n),
        [sds((2, rows, 256), bf16), sds((2, rows, 512)), sds((56, 256)), sds((8, 512))],
        [SMEM] + [VMEM] * 14,
        scratch + [pltpu.VMEM((49, 8, 256), f32)],
    )(counts, hid, ring(z[:, -192:], z[:, :192]), cot, k7, k5, k3, pbias, xblk, dn, dnr, eall, gain, dh, gtaps)
    out = lax.all_gather(outh, "head", axis=2, tiled=True)
    gx = lax.all_gather(dh, "head", axis=2, tiled=True) + swap(n, lnb)
    gw = lax.psum_scatter(wpart.astype(f32), "seq", scatter_dimension=1, tiled=True)
    gk, small = lax.psum((gk, small), "seq")
    gkall = lax.all_gather(gk, "head", axis=1, tiled=True)
    k7o = gkall[:49].reshape(7, 7, 512)
    return out, gx, gw[0:3], gw[3].T, small[0:2].reshape(8, 128), gkall, k7o, k7o[1:6, 1:6], k7o[2:5, 2:5]


def sem(count):
    return DMA((2, count))


def shards(n, tokens, counts, ln_gain, ln_bias, w_qkv, conv_taps, w_out, out_bias, kernel7, kernel5, kernel3, ppeg_bias, cotangent):
    rows = tokens.shape[1]
    direct = n == 16
    size = n // 2
    grid = rows // GRID_W
    wide = 2 * rows
    mb, wr = MARKS // size, w_qkv.shape[1]
    gain, bias, obias, pbias = (v[None, :] for v in (ln_gain, ln_bias, out_bias, ppeg_bias))
    kernels = (kernel7, kernel5, kernel3)
    scratch = [
        pltpu.VMEM((7, 8, 256), f32),
        pltpu.VMEM((7, grid + 6, GRID_W, 256), f32),
        pltpu.VMEM((grid + 6, GRID_W + 16, 256), f32),
    ]
    blocks = sds((2, rows, 512), bf16)

    if direct:
        xblk, normed, xbar, wall, dh, dhrb = call(
            functools.partial(start_kernel, n),
            [blocks, blocks, sds((MARKS, 512), bf16), sds((4, 512, 256), bf16), sds((2, rows, 256)), blocks],
            [SMEM] + [VMEM] * 9,
            [pltpu.VMEM((4, wr, 256), bf16), pltpu.VMEM((2, 2, 192, 256), bf16), pltpu.VMEM((MARKS, 256), bf16),
             pltpu.VMEM((size, mb, 256), bf16), pltpu.VMEM((mb, 256), bf16)] + scratch
            + [pltpu.VMEM((rows, 256), bf16)]
            + [sem(1), sem(1), sem(2), sem(2 * size), sem(size), sem(size), sem(3), sem(1)],
            cid=0,
        )(counts, tokens, cotangent, gain, bias, w_qkv, w_out, *kernels)
    else:
        xblk, normed, xbar, wall, dh, dhrb = start_plain(
            n, counts, tokens, cotangent, gain, bias, w_qkv, w_out, *kernels, scratch
        )

    t2, m2 = sds((256, wide), bf16), sds((256, MARKS), bf16)
    qt, kt, vt, qlt, klt, dot, wback, a1, e3, blk, hal = call(
        functools.partial(scores_kernel, n),
        [t2, t2, t2, m2, m2, t2, sds((256, 512), bf16), sds((4, MARKS, wide), bf16), sds((4, wide, MARKS), bf16),
         sds((4, BLK, MARKS), bf16), sds((2, 2, 2, 16, 256), bf16)],
        [SMEM, VMEM, VMEM, VMEM, VMEM],
    )(counts, normed, xbar, wall, dhrb)

    if direct:
        recv, hrecv = call(
            functools.partial(reduce_kernel, n),
            [sds((size, BLK, MARKS), bf16), sds(hal.shape, bf16)],
            [VMEM, VMEM],
            [sem(size), sem(2)],
            cid=1,
        )(blk, hal)
    else:
        recv, hrecv = reduce_plain(n, blk, hal)

    square = pltpu.VMEM((SWEEPS, 2, 256, 256), bf16)
    res, dqz = call(
        functools.partial(chain_kernel, n),
        [sds((BLK, MARKS), bf16), sds((2, 64, MARKS))],
        [VMEM, VMEM, VMEM],
        [square, square, pltpu.VMEM((SWEEPS, 64, 256), f32)],
    )(recv, qlt, klt)

    if direct:
        res = call(functools.partial(spread_kernel, n), sds((4, BLK, MARKS), bf16), [VMEM], [sem(size)], cid=2)(res)
    else:
        res = spread_plain(n, res)

    po, dn, ep, wpart, gtaps = call(
        functools.partial(grads_kernel, n),
        [blocks, blocks, sds((MARKS, 512), bf16), sds((4, 512, 256), bf16), sds((8, 256))],
        [SMEM] + [VMEM] * 18,
        [pltpu.VMEM((256, wide), bf16), pltpu.VMEM((3, 256, wide), bf16), pltpu.VMEM((2, 256, MARKS), bf16),
         pltpu.VMEM((4, rows + 32, rows), f32), pltpu.VMEM((2, 4, 2, rows, rows), bf16), pltpu.VMEM((2, 4, 2, 32, rows), bf16),
         pltpu.VMEM((3, 2, 256, 32), bf16), pltpu.VMEM((2, 256, rows), bf16)],
    )(counts, normed, xbar, wall, wback, dhrb, qt, kt, vt, qlt, klt, dot, a1, e3, blk, res, hrecv, conv_taps, dqz)

    late = (counts, tokens, cotangent, xblk, dh, po, ep, dn, wpart, gtaps, gain, obias, pbias, *kernels)
    if direct:
        halfb = (2, rows, 256)
        out, gx, gwqkv, gwout, sums, gkall, k7o, k5o, k3o = call(
            functools.partial(late_kernel, n),
            [blocks, sds((2, rows, 512)), sds((3, wr, 256)), sds((256, wr)), sds((8, 128)), sds((56, 512)),
             sds((7, 7, 512)), sds((5, 5, 512)), sds((3, 3, 512))],
            [SMEM] + [VMEM] * 15,
            [pltpu.VMEM((MARKS, 256), bf16), pltpu.VMEM((MARKS, 256), bf16), pltpu.VMEM((size, mb, 256), bf16),
             pltpu.VMEM((mb, 256), bf16), pltpu.VMEM((MARKS, 512), bf16), pltpu.VMEM(halfb, bf16), pltpu.VMEM(halfb, bf16),
             pltpu.VMEM((rows, 256), bf16), pltpu.VMEM((2, rows, 512), bf16), pltpu.VMEM(halfb, f32), pltpu.VMEM(halfb, f32),
             pltpu.VMEM(halfb, bf16), pltpu.VMEM((2, 2, 192, 256), bf16), pltpu.VMEM((rows, 512), f32),
             pltpu.VMEM((rows, 512), bf16), pltpu.VMEM((rows, 256), bf16), pltpu.VMEM((size, 2, 4, wr, 256), bf16),
             pltpu.VMEM((4, wr, 256), bf16), pltpu.VMEM((4, wr, 256), bf16)] + scratch
            + [pltpu.VMEM((49, 8, 256), f32), pltpu.VMEM(halfb, bf16), pltpu.VMEM((56, 256), f32),
               pltpu.VMEM((n, 8, 256), f32), pltpu.VMEM((8, 256), f32), pltpu.VMEM((8, 512), f32),
               pltpu.VMEM((n, 8, 128), f32), pltpu.VMEM((8, 128), f32)]
            + [sem(5), sem(size), sem(size), sem(1), sem(2), sem(4), sem(2 * size), sem(1), sem(n), sem(n), sem(n)],
            cid=3,
        )(*late)
    else:
        out, gx, gwqkv, gwout, sums, gkall, k7o, k5o, k3o = late_plain(n, *late, scratch)

    sums = sums.reshape(2, 512)
    gtaps = half_of(gkall[51:55], 1)
    gtaps = jnp.concatenate([gtaps[:, 16::-1], gtaps[:, 255:239:-1]], axis=1)
    return out, gx, sums[0], sums[1], gwqkv, gtaps, gwout, gkall[49], k7o, k5o, k3o, gkall[50]


def solution(mesh):
    rows, cols = P(None, "seq", None), P(None, "seq", "head")
    return jax.shard_map(
        functools.partial(shards, mesh.shape["seq"]),
        mesh=mesh,
        in_specs=(rows, P(), P(), P(), cols, P("head", None), P("head", "seq"), P(), P(), P(), P(), P(), rows),
        out_specs=(rows, rows, P(), P(), cols, P("head", None), P("head", "seq"), P(), P(), P(), P(), P()),
        check_vma=False,
    )
```

```python
import functools

import jax
import jax.numpy as jnp
from jax import lax
from jax.experimental import pallas as pl
from jax.experimental.pallas import tpu as pltpu
from jax.sharding import PartitionSpec as P

MESH = pl.DeviceIdType.MESH
GRID_W = 64
MARKS = 256
SWEEPS = 6
EPSILON = 1e-05
f32, bf16 = jnp.float32, jnp.bfloat16
VMEM = pl.BlockSpec(memory_space=pltpu.VMEM)
SMEM = pl.BlockSpec(memory_space=pltpu.SMEM)
DMA = pltpu.SemaphoreType.DMA
SCALE = 64 ** -0.5
BLK = 144
PART = 80


def sds(shape, dtype=f32):
    return jax.ShapeDtypeStruct(shape, dtype)


def call(kernel, outs, specs, scratch=(), cid=None, vmem=56):
    extra = {} if cid is None else dict(collective_id=cid, has_side_effects=True)
    return pl.pallas_call(
        kernel,
        out_shape=outs,
        in_specs=specs,
        out_specs=jax.tree.map(lambda _: VMEM, outs),
        scratch_shapes=list(scratch),
        compiler_params=pltpu.CompilerParams(vmem_limit_bytes=vmem * 2**20, **extra),
    )


def mm(left, right, cl=1, cr=0):
    return lax.dot_general(left, right, (((cl,), (cr,)), ((), ())), preferred_element_type=f32)


def split(value):
    high = value.astype(bf16)
    return high, (value - high.astype(f32)).astype(bf16)


def split3(row):
    high = row.astype(bf16).astype(f32)
    rest = row - high
    mid = rest.astype(bf16).astype(f32)
    return [high, mid, rest - mid]


def mm3(left, right, cl=1, cr=0):
    (lh, ll), (rh, rl) = left, right
    return mm(lh, rh, cl, cr) + (mm(lh, rl, cl, cr) + mm(ll, rh, cl, cr))


def iota(shape, dim):
    return lax.broadcasted_iota(jnp.int32, shape, dim)


def edges(count, marks):
    return (marks * count + (MARKS - 1)) >> 8, ((marks + 1) * count + (MARKS - 1)) >> 8


def member(count, start, rows):
    low, high = edges(count, iota((MARKS, rows), 0))
    slot = iota((MARKS, rows), 1) + start
    return jnp.where((slot >= low) & (slot < high), 1.0, 0.0).astype(bf16)

OWNERS = (0, 3, 5, 6)


def place(n):
    me = lax.axis_index("seq")
    return me // (n // 2), lax.rem(me, n // 2), lax.rem(me + n // 2, n)


def head_of(g):
    return jnp.where(g == 0, 0, jnp.where(g == 3, 1, jnp.where(g == 5, 2, 3)))


def is_owner(g):
    return (g == 0) | (g == 3) | (g == 5) | (g == 6)


def my_half():
    return pl.ds(pl.multiple_of(lax.axis_index("head") * 256, 256), 256)


def block_start(n, g, b, rows):
    return (g + b * (n // 2)) * rows


def places(n, g, rows, shape, dim):
    at = iota(shape, dim)
    return at + g * rows + jnp.where(at >= rows, (n // 2 - 1) * rows, 0)


def norm_rows(x, gain, bias):
    x = x.astype(f32)
    xc = x - jnp.mean(x, axis=-1, keepdims=True)
    inv = lax.rsqrt(jnp.mean(xc * xc, axis=-1, keepdims=True) + EPSILON)
    return (xc * inv * gain + bias).astype(bf16)


def segment_sums(n, g, count, normed):
    rows = normed.shape[1]
    mine = my_half()
    return sum(mm(member(count, block_start(n, g, b, rows), rows), normed[b, :, mine]) for b in range(2))


def join_taps(kc, k7, k5, k3):
    mine = my_half()
    kc[...] = jnp.zeros_like(kc)
    for a in range(7):
        kc[a, 0:7] = k7[a, :, mine]
    for a in range(5):
        kc[a + 1, 1:6] = kc[a + 1, 1:6] + k5[a, :, mine]
    for a in range(3):
        kc[a + 2, 2:5] = kc[a + 2, 2:5] + k3[a, :, mine]


def load_grid(zs, pad, body, top, bottom):
    grid = body.shape[0] // GRID_W
    pad[...] = jnp.zeros_like(pad)
    pad[0:3, 8:8 + GRID_W] = top.reshape(3, GRID_W, 256)
    pad[3:3 + grid, 8:8 + GRID_W] = body.reshape(grid, GRID_W, 256)
    pad[3 + grid:6 + grid, 8:8 + GRID_W] = bottom.reshape(3, GRID_W, 256)
    for b in range(7):
        zs[b] = pad[:, 5 + b:5 + b + GRID_W, :]


def conv_row(zs, kc, i, flip):
    acc = jnp.zeros((GRID_W, 256), f32)
    for a in range(7):
        for b in range(7):
            ka, kb = (6 - a, 6 - b) if flip else (a, b)
            acc = acc + kc[ka, kb:kb + 1, :] * zs[b, i + a]
    return acc


def ends(n, top, bottom):
    me = lax.axis_index("seq")
    return jnp.where(me > 0, top.astype(f32), 0.0), jnp.where(me < n - 1, bottom.astype(f32), 0.0)


def back_conv(n, count, s, cot, halo, kc, dh, zs, pad):
    me = lax.axis_index("seq")
    rows = cot.shape[1]
    mine = my_half()
    top, bottom = ends(n, halo[0, s], halo[1, s])
    load_grid(zs, pad, cot[s, :, mine].astype(f32), top, bottom)

    @pl.loop(0, rows // GRID_W)
    def _(i):
        acc = conv_row(zs, kc, i, True)
        here = pl.ds(pl.multiple_of(i * GRID_W, GRID_W), GRID_W)
        slot = iota((GRID_W, 256), 0) + (me * rows + i * GRID_W)
        dh[s, here] = cot[s, here, mine].astype(f32) + jnp.where(slot < count, acc, 0.0)


def hidden_rows(count, s, tok, obias, part, hid):
    rows = tok.shape[1]
    mine = my_half()
    hid[s] = tok[s, :, mine].astype(f32) + part.astype(f32) + obias[:, mine]
    slot = iota((rows, 256), 0) + lax.axis_index("seq") * rows
    return jnp.where(slot < count, hid[s], 0.0)


def grid_forward(n, count, s, hid, halo, cot, kc, pbias, outh, zs, pad, gacc):
    rows = hid.shape[1]
    mine = my_half()
    slot = iota((rows, 256), 0) + lax.axis_index("seq") * rows
    top, bottom = ends(n, halo[0, s], halo[1, s])
    load_grid(zs, pad, jnp.where(slot < count, hid[s], 0.0), top, bottom)

    @pl.loop(0, rows // GRID_W)
    def _(i):
        here = pl.ds(pl.multiple_of(i * GRID_W, GRID_W), GRID_W)
        acc = conv_row(zs, kc, i, False)
        outh[s, here] = (hid[s, here] + acc + pbias[:, mine]).astype(bf16)
        g = cot[s, here, mine].astype(f32)
        for a in range(7):
            for b in range(7):
                part = (g * zs[b, i + a]).reshape(GRID_W // 8, 8, 256)
                gacc[a * 7 + b] = gacc[a * 7 + b] + jnp.sum(part, axis=0)


def grid_sums(gacc, dh, cot, gtaps, gk):
    mine = my_half()
    for t in range(49):
        gk[t:t + 1] = jnp.sum(gacc[t], axis=0, keepdims=True)
    gk[49:50] = jnp.sum(dh[0], axis=0, keepdims=True) + jnp.sum(dh[1], axis=0, keepdims=True)
    g = cot[0, :, mine].astype(f32) + cot[1, :, mine].astype(f32)
    gk[50:51] = jnp.sum(g, axis=0, keepdims=True)
    gk[51:55] = gtaps[0:4]
    gk[55:56] = jnp.zeros((1, 256), f32)


def norm_back(n, g, count, b, x, dn, dnr, eall, gain, small):
    rows = x.shape[1]
    low, high = edges(count, iota((MARKS, 512), 0))
    e = (eall[...].astype(f32) / (high - low).astype(f32)).astype(bf16)
    mem = member(count, block_start(n, g, b, rows), rows)
    total = (dn[b].astype(f32) + dnr[b].astype(f32)) + mm(mem, e, 0, 0)
    x = x[b].astype(f32)
    xc = x - jnp.mean(x, axis=-1, keepdims=True)
    inv = lax.rsqrt(jnp.mean(xc * xc, axis=-1, keepdims=True) + EPSILON)
    xh = xc * inv
    dg = total * gain[...]
    m1 = jnp.mean(dg, axis=-1, keepdims=True)
    m2 = jnp.mean(dg * xh, axis=-1, keepdims=True)
    small[0:1] = small[0:1] + jnp.sum(total * xh, axis=0, keepdims=True)
    small[1:2] = small[1:2] + jnp.sum(total, axis=0, keepdims=True)
    return (dg - m1 - xh * m2) * inv


def spill_kernels(gkall, k7o, k5o, k3o):
    for a in range(7):
        k7o[a] = gkall[7 * a:7 * a + 7]
    for a in range(5):
        k5o[a] = gkall[7 * a + 8:7 * a + 13]
    for a in range(3):
        k3o[a] = gkall[7 * a + 16:7 * a + 19]


def greet(peers, pair=True):
    sem = pltpu.get_barrier_semaphore()
    for peer in peers:
        pl.semaphore_signal(sem, inc=1, device_id={"seq": peer}, device_id_type=MESH)
    if pair:
        hd = lax.axis_index("head")
        pl.semaphore_signal(sem, inc=1, device_id={"head": 1 - hd}, device_id_type=MESH)
    pl.semaphore_wait(sem, len(peers) + (1 if pair else 0))


def everyone(n):
    me = lax.axis_index("seq")
    return [lax.rem(me + i, n) for i in range(n)]


def cube(n):
    half, g, _ = place(n)
    return [half * (n // 2) + lax.rem(g + i, n // 2) for i in range(n // 2)]


def remote(src, dst, sems, i, **where):
    return pltpu.make_async_remote_copy(
        src_ref=src, dst_ref=dst, send_sem=sems.at[0, i], recv_sem=sems.at[1, i], device_id=where, device_id_type=MESH
    )


def go(copies):
    for c in copies:
        c.start()
    return copies


def got(copies):
    for c in copies:
        c.wait_recv()


def sent(copies):
    for c in copies:
        c.wait_send()


def project(n, count, normed, wall, qt, kt, vt):
    _, g, _ = place(n)
    rows = normed.shape[1]
    nr = normed[...].reshape(2 * rows, 512)
    qt[...] = mm(wall[0], nr, 0, 1).astype(bf16)
    kt[...] = mm(wall[1], nr, 0, 1).astype(bf16)
    slots = places(n, g, rows, (256, 2 * rows), 1)
    vt[...] = jnp.where(slots < count, mm(wall[2], nr, 0, 1), 0.0).astype(bf16)


def value_edges(n, count, normed, wall, halv):
    _, g, _ = place(n)
    rows = normed.shape[1]
    for b in range(2):
        for side, first in ((0, 0), (1, rows - 16)):
            slot = iota((16, 256), 0) + (block_start(n, g, b, rows) + first)
            v = mm(normed[b, first:first + 16], wall[2])
            halv[side, b] = jnp.where(slot < count, v, 0.0).astype(bf16)


def landmarks(xbar, wall, qlt, klt):
    qlt[...] = mm(wall[0], xbar[...], 0, 1).astype(bf16)
    klt[...] = mm(wall[1], xbar[...], 0, 1).astype(bf16)


def head_rows(h):
    return pl.ds(pl.multiple_of(h * 64, 64), 64)


def key_scores(n, count, kt, qlt, vt, e3, blkb):
    _, g, _ = place(n)
    wide = kt.shape[1]
    ok = places(n, g, wide // 2, (wide, MARKS), 0) < count

    @pl.loop(0, 4)
    def _(h):
        here = head_rows(h)
        s3 = jnp.where(ok, mm(kt[here] * SCALE, qlt[here], 0, 0), -1e30)
        top = jnp.max(s3, axis=0, keepdims=True)
        e = jnp.where(ok, jnp.exp(s3 - top), 0.0)
        total = jnp.sum(e, axis=0, keepdims=True)
        er = e.astype(bf16)
        e3[h] = er
        blkb[h, 0:64] = mm(vt[here], er).astype(bf16)
        stat = jnp.concatenate(split3(top) + split3(total) + [jnp.zeros((10, MARKS), f32)], axis=0)
        blkb[h, 64:80] = stat.astype(bf16)


def query_scores(qt, klt, a1):
    @pl.loop(0, 4)
    def _(h):
        here = head_rows(h)
        s1 = mm(klt[here] * SCALE, qt[here], 0, 0)
        e1 = jnp.exp(s1 - jnp.max(s1, axis=0, keepdims=True))
        a1[h] = (e1 / jnp.sum(e1, axis=0, keepdims=True)).astype(bf16)


def out_grads(dhrb, wback, dot, hald):
    rows = dhrb.shape[1]
    dot[...] = mm(wback[...], dhrb[...].reshape(2 * rows, 512), 1, 1).astype(bf16)
    for b in range(2):
        for side, first in ((0, 0), (1, rows - 16)):
            hald[side, b] = mm(dhrb[b, first:first + 16], wback[...], 1, 1).astype(bf16)


def partial_dc(dot, a1, blkd):
    @pl.loop(0, 4)
    def _(h):
        blkd[h] = mm(dot[head_rows(h)], a1[h], 1, 1).astype(bf16)


def three(stat, first):
    return (stat[first:first + 1] + stat[first + 1:first + 2]) + stat[first + 2:first + 3]


def chain(ql, kl, recvb, recvd, res, dqz, ps, ts, xs, got_b=None, got_d=None):
    parts = recvb.shape[0]
    s2 = mm(ql * SCALE, kl, 0, 0)
    e2 = jnp.exp(s2 - jnp.max(s2, axis=1, keepdims=True))
    a = e2 / jnp.sum(e2, axis=1, keepdims=True)
    asp = split(a)
    cs, rs = jnp.sum(a, axis=0, keepdims=True), jnp.sum(a, axis=1, keepdims=True)
    cm, rm = jnp.max(cs, axis=1, keepdims=True), jnp.max(rs, axis=0, keepdims=True)
    inv = 1.0 / (cm * rm)
    p = mm3(asp, asp, 1, 1) * inv
    for k in range(SWEEPS):
        psp = split(p)
        t = mm3(psp, psp)
        tsp = split(t)
        ps[k, 0], ps[k, 1] = psp
        ts[k, 0], ts[k, 1] = tsp
        if k < SWEEPS - 1:
            p = 0.25 * (13.0 * p - 15.0 * t + mm3(tsp, split(7.0 * p - t)))
    if got_b:
        got_b()
    tops = [three(recvb[d, 64:80].astype(f32), 0) for d in range(parts)]
    top = functools.reduce(jnp.maximum, tops)
    total, value = 0.0, 0.0
    for d in range(parts):
        w = jnp.exp(tops[d] - top)
        total = total + three(recvb[d, 64:80].astype(f32), 3) * w
        value = value + recvb[d, 0:64].astype(f32) * w
    value = value / total
    x = value
    for k in range(SWEEPS):
        psp, tsp = (ps[k, 0], ps[k, 1]), (ts[k, 0], ts[k, 1])
        xs[k] = x
        xt = mm3(split(x), tsp)
        x = 0.25 * (13.0 * x + 7.0 * xt - mm3(split(15.0 * x + xt), psp))
    ct = mm3(split(x), asp) * inv
    res[0:64] = ct.astype(bf16)
    if got_d:
        got_d()
    dct = recvd[0].astype(f32)
    for d in range(1, parts):
        dct = dct + recvd[d].astype(f32)
    dcs = split(dct)
    y = mm3(dcs, asp, 1, 1) * inv
    da = mm3(split(x), dcs, 0, 0) * inv
    ds = -jnp.sum(jnp.sum(dct * ct, axis=0, keepdims=True), axis=1, keepdims=True) * inv
    e = None
    for k in range(SWEEPS - 1, -1, -1):
        psp, tsp = (ps[k, 0], ps[k, 1]), (ts[k, 0], ts[k, 1])
        outer = mm3(split(y), split(xs[k]), 0, 0) * 0.125
        d = outer + outer.T
        pd = mm3(psp, split(d))
        if e is None:
            new = -15.0 * d + mm3(split(-pd), psp)
            left = 7.0 * pd + mm3(tsp, split(-d))
        else:
            eq = 0.25 * e
            pe = mm3(psp, split(eq))
            new = 13.0 * eq - 15.0 * d + mm3(split(7.0 * pe - pd), psp)
            left = 7.0 * pd - 15.0 * pe + mm3(tsp, split(7.0 * eq - d - (pe + pe.T)))
        e = new + (left + left.T)
        yt = mm3(split(y), tsp)
        y = 0.25 * (13.0 * y + 7.0 * yt - mm3(split(15.0 * y + yt), psp))
    dbr = y.astype(bf16)
    res[64:128] = dbr
    rt = jnp.sum(dbr.astype(f32) * value, axis=0, keepdims=True)
    stat = jnp.concatenate(split3(top) + split3(total) + split3(rt) + [jnp.zeros((7, MARKS), f32)], axis=0)
    res[128:144] = stat.astype(bf16)

    def rest():
        p0 = ps[0, 0].astype(f32) + ps[0, 1].astype(f32)
        grad = da + mm3(split(e), asp) * (2.0 * inv)
        slope = ds - jnp.sum(jnp.sum(e * p0, axis=0, keepdims=True), axis=1, keepdims=True) * inv
        eqc, eqr = jnp.where(cs == cm, 1.0, 0.0), jnp.where(rs == rm, 1.0, 0.0)
        grad = grad + (slope * rm) * (eqc / jnp.sum(eqc, axis=1, keepdims=True))
        grad = grad + (slope * cm) * (eqr / jnp.sum(eqr, axis=0, keepdims=True))
        dsc = a * (grad - jnp.sum(a * grad, axis=1, keepdims=True)) * SCALE
        dh, dl = split(dsc)
        dqz[0] = mm(kl, dh, 1, 1) + mm(kl, dl, 1, 1)
        dqz[1] = mm(ql, dh) + mm(ql, dl)

    return rest


def band(base, shift, rows):
    wide = jnp.broadcast_to(base, (rows, 256))
    return pltpu.roll(wide, shift, 1, stride=1, stride_axis=0)


def diagonals(g, shift):
    return jnp.sum(pltpu.roll(g, shift, 1, stride=1, stride_axis=0), axis=0, keepdims=True)


def ring_ends(n, g, b, recv):
    top = jnp.where(g > 0, recv[0, b].astype(f32), recv[0, 0].astype(f32) if b else 0.0)
    bottom = jnp.where(g < n // 2 - 1, recv[1, b].astype(f32), 0.0 if b else recv[1, 1].astype(f32))
    return jnp.concatenate([top, bottom], axis=0)


def make_bands(taps, rows, tm, th):
    pi, pj = iota((rows, rows), 0), iota((rows, rows), 1)
    inside = (pi - pj <= 16) & (pj - pi <= 16)
    hi, hj = iota((32, rows), 0), iota((32, rows), 1)
    far = jnp.where(hi < 16, hi - hj, hj - hi - (rows - 32)) >= 0
    ti, tl = iota((33, 256), 0), iota((33, 256), 1)
    spots = [jnp.where(((ti + tl if f == 0 else tl - ti + 32) & 255) == 16, 1.0, 0.0).astype(bf16) for f in range(2)]
    pieces = [piece.astype(bf16) for piece in split3(taps[...])]
    for f in range(2):
        lines = mm(pieces[0], spots[f]) + mm(pieces[1], spots[f]) + mm(pieces[2], spots[f])
        for h in range(4):
            line = lines[h:h + 1, :]
            full = jnp.where(inside, band(line, 0, rows), 0.0)
            tm[f, h, 0], tm[f, h, 1] = split(full)
            both = jnp.concatenate([band(line, 240, 16), band(line, 0, 16)], axis=0)
            th[f, h, 0], th[f, h, 1] = split(jnp.where(far, both, 0.0))


def value_conv(n, vt, recvv, tm, th, hv, vr, hvr, conv):
    _, g, _ = place(n)
    rows = vt.shape[1] // 2
    pi, pj = iota((rows, rows), 0), iota((rows, rows), 1)
    mirror = jnp.where(pi + pj == rows - 1, 1.0, 0.0).astype(bf16)
    si, sj = iota((32, 32), 0), iota((32, 32), 1)
    mirror32 = jnp.where(si + sj == jnp.where(si < 16, 15, 47), 1.0, 0.0).astype(bf16)
    for b in range(2):
        part = slice(b * rows, (b + 1) * rows)
        hv[b] = ring_ends(n, g, b, recvv).T.astype(bf16)
        vr[b] = mm(vt[:, part], mirror).astype(bf16)
        hvr[b] = mm(hv[b], mirror32).astype(bf16)

        @pl.loop(0, 4)
        def _(h):
            here = head_rows(h)
            v, vh = vt[here, part], hv[b, here]
            conv[here, part] = mm(v, tm[0, h, 0]) + mm(v, tm[0, h, 1]) + mm(vh, th[0, h, 0]) + mm(vh, th[0, h, 1])


def value_conv_back(n, dot, recvd, tm, th, hd, vr, hvr, dconv, gsum, gtaps):
    _, g, _ = place(n)
    rows = dot.shape[1] // 2
    pi, pj = iota((rows, rows), 0), iota((rows, rows), 1)
    hi, hj = iota((32, rows), 0), iota((32, rows), 1)
    near = (pi + pj >= rows - 17) & (pi + pj <= rows + 15)
    beyond = jnp.where(hi < 16, 15 - hi - hj, hi + hj - (rows + 15)) >= 0
    for b in range(2):
        hd[b] = ring_ends(n, g, b, recvd).T.astype(bf16)

    @pl.loop(0, 4)
    def _(h):
        here = head_rows(h)
        s, sh = 0.0, 0.0
        for b in range(2):
            part = slice(b * rows, (b + 1) * rows)
            d, dh = dot[here, part], hd[b, here]
            dconv[here, part] = mm(d, tm[1, h, 0]) + mm(d, tm[1, h, 1]) + mm(dh, th[1, h, 0]) + mm(dh, th[1, h, 1])
            s = s + mm(vr[b, here], d, 0, 0)
            sh = sh + mm(hvr[b, here], d, 0, 0)
        s, sh = jnp.where(near, s, 0.0), jnp.where(beyond, sh, 0.0)
        gsum[h] = jnp.broadcast_to(diagonals(s, 1) + diagonals(sh[0:16], 1) + diagonals(sh[16:32], 241), (8, 256))

    for h in range(4):
        gtaps[h:h + 1, :] = gsum[h, 0:1]
    gtaps[4:8, :] = jnp.zeros((4, 256), f32)


def attend(res, a1, conv, att):
    @pl.loop(0, 4)
    def _(h):
        here = head_rows(h)
        att[here] = (mm(res[h, 0:64], a1[h]) + conv[here]).astype(bf16)


def score_grads(n, count, qt, kt, vt, qlt, klt, dot, a1, e3, blkb, res, dqz, dconv, dp, dlm):
    _, g, _ = place(n)
    wide = qt.shape[1]
    mine = head_of(g)
    use = jnp.where(is_owner(g), 1.0, 0.0)
    slots = places(n, g, wide // 2, (64, wide), 1)

    @pl.loop(0, 4)
    def _(h):
        here = head_rows(h)
        ct, dbt = res[h, 0:64], res[h, 64:128]
        stat = res[h, 128:144].astype(f32)
        own = three(blkb[h, 64:80].astype(f32), 0)
        factor = jnp.exp(own - three(stat, 0)) / three(stat, 3)
        rt = three(stat, 6)
        do, v = dot[here], vt[here]
        a = a1[h].astype(f32)
        da = mm(ct, do, 0, 0)
        d1 = (a * (da - jnp.sum(a * da, axis=0, keepdims=True))).astype(bf16)
        dp[0, here] = mm(klt[here] * SCALE, d1).astype(bf16)
        own_chain = jnp.where(h == mine, use, 0.0)
        dlm[1, here] = (mm(qt[here] * SCALE, d1, 1, 1) + own_chain * dqz[1]).astype(bf16)
        a3 = e3[h].astype(f32) * factor
        d3 = (a3 * (mm(v, dbt, 0, 0) - rt)).astype(bf16)
        dlm[0, here] = (mm(kt[here] * SCALE, d3) + own_chain * dqz[0]).astype(bf16)
        dp[1, here] = mm(qlt[here] * SCALE, d3, 1, 1).astype(bf16)
        dv = mm(dbt, a3.astype(bf16), 1, 1) + dconv[here]
        dp[2, here] = jnp.where(slots < count, dv, 0.0).astype(bf16)


def mark_rows(wall, dlm, ep):
    ep[...] = (mm(wall[0], dlm[0]) + mm(wall[1], dlm[1])).T.astype(bf16)


def input_rows(wall, dp, dn):
    rows = dn.shape[1]
    d = mm(wall[0], dp[0]) + mm(wall[1], dp[1]) + mm(wall[2], dp[2])
    dn[...] = d.T.astype(bf16).reshape(2, rows, 512)


def output_rows(att, wback, po):
    rows = po.shape[1]
    po[...] = mm(att[...], wback[...], 0, 0).astype(bf16).reshape(2, rows, 512)


def weight_grads(normed, xbar, dhrb, att, dp, dlm, wpart):
    rows = normed.shape[1]
    nr = normed[...].reshape(2 * rows, 512)
    for j in range(3):
        grad = mm(dp[j], nr)
        if j < 2:
            grad = grad + mm(dlm[j], xbar[...])
        wpart[j] = grad.T.astype(bf16)
    wpart[3] = mm(att[...], dhrb[...].reshape(2 * rows, 512)).T.astype(bf16)


class Refs:
    def __init__(self, names, refs):
        self.__dict__.update(zip(names, refs))


INPUTS = ("cnt", "tok", "cot", "gain", "bias", "wqkv", "woutt", "taps", "obias", "pbias", "k7", "k5", "k3")


def layer_results(n, rows, wr):
    return dict(
        outf=((2, rows, 512), bf16), lnf=((2, rows, 512), f32), dhf=((2, rows, 512), f32), gw=((4, wr, 256), f32),
        sums=((8, 128), f32), gkall=((56, 512), f32),
    )


def layer_buffers(n, rows, wr):
    size = n // 2
    mb, wide, grid = MARKS // size, 2 * rows, rows // GRID_W
    half2 = (2, rows, 256)
    return dict(
        wts=((4, wr, 256), bf16), wall=((4, 512, 256), bf16), wback=((256, 512), bf16),
        xblk=((2, rows, 512), bf16), normed=((2, rows, 512), bf16), xbar=((MARKS, 512), bf16),
        xp=((MARKS, 256), bf16), xr=((size, mb, 256), bf16), xm=((mb, 256), bf16),
        halo=((2, 2, 192, 256), bf16), dh=(half2, f32), dhs=((rows, 256), bf16), dhrb=((2, rows, 512), bf16),
        kc=((7, 8, 256), f32), zs=((7, grid + 6, GRID_W, 256), f32), pad=((grid + 6, GRID_W + 16, 256), f32),
        qt=((256, wide), bf16), kt=((256, wide), bf16), vt=((256, wide), bf16), dot=((256, wide), bf16),
        qlt=((256, MARKS), bf16), klt=((256, MARKS), bf16), a1=((4, MARKS, wide), bf16), e3=((4, wide, MARKS), bf16),
        blkb=((4, PART, MARKS), bf16), blkd=((4, 64, MARKS), bf16),
        recvb=((size, PART, MARKS), bf16), recvd=((size, 64, MARKS), bf16),
        halv=((2, 2, 16, 256), bf16), hald=((2, 2, 16, 256), bf16), rhv=((2, 2, 16, 256), bf16), rhd=((2, 2, 16, 256), bf16),
        ps=((SWEEPS, 2, 256, 256), bf16), ts=((SWEEPS, 2, 256, 256), bf16), xs=((SWEEPS, 64, 256), f32),
        res=((BLK, MARKS), bf16), resall=((4, BLK, MARKS), bf16), dqz=((2, 64, MARKS), f32),
        tm=((2, 4, 2, rows, rows), bf16), th=((2, 4, 2, 32, rows), bf16), hv=((2, 256, 32), bf16), hdt=((2, 256, 32), bf16),
        hvr=((2, 256, 32), bf16), vr=((2, 256, rows), bf16), conv=((256, wide), f32), dconv=((256, wide), f32),
        gsum=((4, 8, 256), f32), gtaps=((8, 256), f32), att=((256, wide), bf16), dp=((3, 256, wide), bf16),
        dlm=((2, 256, MARKS), bf16), po=((2, rows, 512), bf16), dn=((2, rows, 512), bf16), ep=((MARKS, 512), bf16),
        wpart=((4, 512, 256), bf16), er=((MARKS, 256), bf16), es=((MARKS, 256), bf16), erv=((size, mb, 256), bf16),
        em=((mb, 256), bf16), eall=((MARKS, 512), bf16), por=(half2, bf16), pos=(half2, bf16), psr=((rows, 256), bf16),
        dnr=((2, rows, 512), bf16), hid=(half2, f32), z=(half2, bf16), zhalo=((2, 2, 192, 256), bf16),
        lnr=((rows, 512), bf16), lns=((rows, 256), bf16), wrv=((size, 2, 4, wr, 256), bf16), wsum=((4, wr, 256), bf16),
        wone=((4, wr, 256), bf16), gacc=((49, 8, 256), f32), outh=(half2, bf16), gk=((56, 256), f32),
        gkr=((n, 8, 256), f32), gkm=((8, 256), f32), small=((8, 512), f32), smr=((n, 8, 128), f32), smx=((8, 128), f32),
    )


SEMS = ("s_w", "s_v", "s_t", "s_h", "s_x", "s_g", "s_p", "s_d", "s_b", "s_c", "s_r", "s_q", "s_a", "s_e", "s_f", "s_o",
        "s_z", "s_l", "s_y", "s_u", "s_k", "s_m", "s_s")


def layer_kernel(n, names, *refs):
    r = Refs(names, refs)
    half, g, partner = place(n)
    me = lax.axis_index("seq")
    hd = lax.axis_index("head")
    other = 1 - half
    size = n // 2
    rows = r.tok.shape[1]
    mb, wr = MARKS // size, r.wts.shape[1]
    mine = my_half()
    theirs = pl.ds(pl.multiple_of((1 - hd) * 256, 256), 256)
    count = r.cnt[half]
    near, far = cube(n), everyone(n)
    core = 1 - hd

    def wrow(device):
        return pl.ds(pl.multiple_of(device * wr, wr), wr)

    def marks(i):
        return pl.ds(pl.multiple_of(lax.rem(g + i, size) * mb, mb), mb)

    r.wts[0:3] = r.wqkv[...]
    r.wts[3] = r.woutt[...]
    greet(far[1:])
    c_t = go([remote(r.tok.at[other, :, mine], r.xblk.at[half, :, mine], r.s_t, 0, seq=partner)])
    c_w = go([remote(r.wts, r.wall.at[:, wrow(me)], r.s_w, 0, seq=partner)])
    c_v = go([remote(r.wts, r.wall.at[:, wrow(me)], r.s_v, i, seq=near[i]) for i in range(1, size)])
    c_h = go([
        remote(r.cot.at[:, pl.ds(rows - 192, 192), mine], r.halo.at[0], r.s_h, 0, seq=far[1]),
        remote(r.cot.at[:, pl.ds(0, 192), mine], r.halo.at[1], r.s_h, 1, seq=far[n - 1]),
    ])
    r.wall[:, wrow(me)] = r.wts[...]
    r.xblk[half] = r.tok[half]
    r.normed[half] = norm_rows(r.tok[half], r.gain[...], r.bias[...])
    join_taps(r.kc, r.k7, r.k5, r.k3)
    make_bands(r.taps, rows, r.tm, r.th)

    got(c_t)
    c_p = go([remote(r.xblk.at[other, :, mine], r.xblk.at[other, :, mine], r.s_p, 0, head=core)])
    got(c_p)
    r.normed[other] = norm_rows(r.xblk[other], r.gain[...], r.bias[...])
    r.xp[...] = segment_sums(n, g, count, r.normed).astype(bf16)
    c_x = go([remote(r.xp.at[marks(i)], r.xr.at[g], r.s_x, i, seq=near[i]) for i in range(1, size)])
    row = marks(0)
    r.xr[pl.ds(g, 1)] = r.xp[row][None]
    got(c_w)
    c_v += go([
        remote(r.wall.at[:, wrow(partner)], r.wall.at[:, wrow(partner)], r.s_v, size + i, seq=near[i]) for i in range(1, size)
    ])
    got(c_h)
    back_conv(n, r.cnt[other], other, r.cot, r.halo, r.kc, r.dh, r.zs, r.pad)
    r.dhs[...] = r.dh[other].astype(bf16)
    c_d = go([remote(r.dhs, r.dhrb.at[half, :, mine], r.s_d, 0, seq=partner)])
    got(c_x)
    total = r.xr[0].astype(f32)
    for d in range(1, size):
        total = total + r.xr[d].astype(f32)
    low, high = edges(count, iota((mb, 256), 0) + g * mb)
    r.xm[...] = (total / (high - low).astype(f32)).astype(bf16)
    r.xbar[row, mine] = r.xm[...]
    c_g = go([remote(r.xm, r.xbar.at[row, mine], r.s_g, i, seq=near[i]) for i in range(1, size)])
    back_conv(n, count, half, r.cot, r.halo, r.kc, r.dh, r.zs, r.pad)
    r.dhrb[half, :, mine] = r.dh[half].astype(bf16)
    c_p += go([remote(r.dh, r.dhf.at[:, :, mine], r.s_p, 1, head=core)])
    r.dhf[:, :, mine] = r.dh[...]
    got(c_g)
    c_p += go([remote(r.xbar.at[:, mine], r.xbar.at[:, mine], r.s_p, 2, head=core)])
    got(c_v)

    project(n, count, r.normed, r.wall, r.qt, r.kt, r.vt)
    value_edges(n, count, r.normed, r.wall, r.halv)
    c_q = go([
        remote(r.halv.at[1], r.rhv.at[0], r.s_q, 0, seq=near[1]),
        remote(r.halv.at[0], r.rhv.at[1], r.s_q, 1, seq=near[size - 1]),
    ])
    got(c_p[2:3])
    landmarks(r.xbar, r.wall, r.qlt, r.klt)
    key_scores(n, count, r.kt, r.qlt, r.vt, r.e3, r.blkb)

    def to_owner(blk, recv, sems, h, d):
        return pltpu.make_async_remote_copy(
            src_ref=blk.at[h], dst_ref=recv.at[d], send_sem=sems.at[0, h], recv_sem=sems.at[1, d],
            device_id={"seq": half * size + OWNERS[h]}, device_id_type=MESH,
        )

    def give(blk, recv, sems):
        for h, o in enumerate(OWNERS):

            @pl.when(g != o)
            def _():
                to_owner(blk, recv, sems, h, g).start()

            @pl.when(g == o)
            def _():
                recv[pl.ds(g, 1)] = blk[h:h + 1]

    def given(blk, recv, sems, h):
        for d in range(size):
            if d != OWNERS[h]:
                to_owner(blk, recv, sems, h, d).wait_recv()

    give(r.blkb, r.recvb, r.s_b)
    query_scores(r.qt, r.klt, r.a1)
    r.wback[...] = r.wall[3].astype(f32).T.astype(bf16)
    got(c_d)
    c_p += go([remote(r.dhrb.at[:, :, mine], r.dhrb.at[:, :, mine], r.s_p, 3, head=core)])
    got(c_p[3:4])
    out_grads(r.dhrb, r.wback, r.dot, r.hald)
    c_q += go([
        remote(r.hald.at[1], r.rhd.at[0], r.s_q, 2, seq=near[1]),
        remote(r.hald.at[0], r.rhd.at[1], r.s_q, 3, seq=near[size - 1]),
    ])
    partial_dc(r.dot, r.a1, r.blkd)
    give(r.blkd, r.recvd, r.s_c)

    r.dqz[...] = jnp.zeros_like(r.dqz)

    def spread(h, i):
        return pltpu.make_async_remote_copy(
            src_ref=r.res, dst_ref=r.resall.at[h], send_sem=r.s_r.at[0, i], recv_sem=r.s_r.at[1, h],
            device_id={"seq": near[i]}, device_id_type=MESH,
        )

    @pl.when(is_owner(g))
    def _():
        here = head_rows(head_of(g))

        def wait_for(blk, recv, sems):
            def wait():
                for d in range(size):

                    @pl.when(g != d)
                    def _():
                        to_owner(blk, recv, sems, 0, d).wait_recv()

            return wait

        rest = chain(
            r.qlt[here], r.klt[here], r.recvb, r.recvd, r.res, r.dqz, r.ps, r.ts, r.xs,
            wait_for(r.blkb, r.recvb, r.s_b), wait_for(r.blkd, r.recvd, r.s_c),
        )
        for h, o in enumerate(OWNERS):

            @pl.when(g == o)
            def _():
                for i in range(1, size):
                    spread(h, i).start()
                r.resall[h] = r.res[...]

        rest()

    got(c_q)
    value_conv(n, r.vt, r.rhv, r.tm, r.th, r.hv, r.vr, r.hvr, r.conv)
    value_conv_back(n, r.dot, r.rhd, r.tm, r.th, r.hdt, r.vr, r.hvr, r.dconv, r.gsum, r.gtaps)
    r.small[...] = jnp.zeros_like(r.small)
    r.gacc[...] = jnp.zeros_like(r.gacc)
    for h, o in enumerate(OWNERS):

        @pl.when(g != o)
        def _():
            spread(h, 1).wait_recv()

    attend(r.resall, r.a1, r.conv, r.att)
    output_rows(r.att, r.wback, r.po)
    c_a = go([remote(r.po.at[:, :, theirs], r.por, r.s_a, 0, head=core)])
    score_grads(n, count, r.qt, r.kt, r.vt, r.qlt, r.klt, r.dot, r.a1, r.e3, r.blkb, r.resall, r.dqz, r.dconv, r.dp, r.dlm)
    got(c_a)
    r.pos[...] = (r.po[:, :, mine].astype(f32) + r.por[...].astype(f32)).astype(bf16)
    c_o = go([remote(r.pos.at[other], r.psr, r.s_o, 0, seq=partner)])
    mark_rows(r.wall, r.dlm, r.ep)
    c_a += go([remote(r.ep.at[:, theirs], r.er, r.s_a, 1, head=core)])
    input_rows(r.wall, r.dp, r.dn)
    c_a += go([remote(r.dn, r.dnr, r.s_a, 2, head=core)])
    got(c_a[1:2])
    r.es[...] = (r.ep[:, mine].astype(f32) + r.er[...].astype(f32)).astype(bf16)
    c_e = go([remote(r.es.at[marks(i)], r.erv.at[g], r.s_e, i, seq=near[i]) for i in range(1, size)])
    r.erv[pl.ds(g, 1)] = r.es[row][None]
    r.z[half] = hidden_rows(count, half, r.tok, r.obias, r.pos[half], r.hid).astype(bf16)
    got(c_o)
    r.z[other] = hidden_rows(r.cnt[other], other, r.tok, r.obias, r.psr[...], r.hid).astype(bf16)
    got(c_e)
    total = r.erv[0].astype(f32)
    for d in range(1, size):
        total = total + r.erv[d].astype(f32)
    r.em[...] = total.astype(bf16)
    r.eall[row, mine] = r.em[...]
    c_f = go([remote(r.em, r.eall.at[row, mine], r.s_f, i, seq=near[i]) for i in range(1, size)])
    c_z = go([
        remote(r.z.at[:, pl.ds(rows - 192, 192)], r.zhalo.at[0], r.s_z, 0, seq=far[1]),
        remote(r.z.at[:, pl.ds(0, 192)], r.zhalo.at[1], r.s_z, 1, seq=far[n - 1]),
    ])
    weight_grads(r.normed, r.xbar, r.dhrb, r.att, r.dp, r.dlm, r.wpart)
    c_y = []
    for i in range(1, size):
        for k, device in enumerate((near[i], lax.rem(near[i] + size, n))):
            c_y += go([remote(r.wpart.at[:, wrow(device)], r.wrv.at[g, k], r.s_y, 2 * i + k, seq=near[i])])
    r.wrv[pl.ds(g, 1), 0] = r.wpart[:, wrow(me)][None]
    r.wrv[pl.ds(g, 1), 1] = r.wpart[:, wrow(partner)][None]

    got(c_f)
    c_a += go([remote(r.eall.at[:, mine], r.eall.at[:, mine], r.s_a, 3, head=core)])
    got(c_a[2:4])
    r.lnf[other] = norm_back(n, g, count, other, r.xblk, r.dn, r.dnr, r.eall, r.gain, r.small)
    r.lns[...] = r.lnf[other, :, mine].astype(bf16)
    c_l = go([remote(r.lns, r.lnr.at[:, mine], r.s_l, 0, seq=partner)])
    r.lnf[half] = norm_back(n, g, count, half, r.xblk, r.dn, r.dnr, r.eall, r.gain, r.small)
    for a in range(2):
        for b in range(4):
            r.smx[4 * a + b:4 * a + b + 1] = r.small[a:a + 1, 128 * b:128 * b + 128]
    c_s = go([remote(r.smx, r.smr.at[me], r.s_s, i, seq=far[i]) for i in range(1, n)])
    r.smr[pl.ds(me, 1)] = r.smx[...][None]

    got(c_z)
    for s in range(2):
        grid_forward(n, r.cnt[s], s, r.hid, r.zhalo, r.cot, r.kc, r.pbias, r.outh, r.zs, r.pad, r.gacc)
    c_l += go([remote(r.outh, r.outf.at[:, :, mine], r.s_l, 1, head=core)])
    r.outf[:, :, mine] = r.outh[...]
    grid_sums(r.gacc, r.dh, r.cot, r.gtaps, r.gk)
    blocks = r.gk.shape[0] // 8

    def to(b, d):
        return pltpu.make_async_remote_copy(
            src_ref=r.gk.at[pl.ds(8 * b, 8)], dst_ref=r.gkr.at[d], send_sem=r.s_k.at[0, b], recv_sem=r.s_k.at[1, d],
            device_id={"seq": b}, device_id_type=MESH,
        )

    def back(b, i):
        return pltpu.make_async_remote_copy(
            src_ref=r.gkm, dst_ref=r.gkall.at[pl.ds(8 * b, 8), mine], send_sem=r.s_m.at[0, i], recv_sem=r.s_m.at[1, b],
            device_id={"seq": far[i]}, device_id_type=MESH,
        )

    for b in range(blocks):

        @pl.when(me != b)
        def _():
            to(b, me).start()

    got(c_l[0:1])
    c_l += go([remote(r.lnr.at[:, mine], r.lnr.at[:, mine], r.s_l, 2, head=core)])
    got(c_y)
    c_u = []
    for k in (1, 0):
        total = r.wrv[0, k].astype(f32)
        for d in range(1, size):
            total = total + r.wrv[d, k].astype(f32)
        if k == 1:
            r.wsum[...] = total.astype(bf16)
            c_u = go([remote(r.wsum, r.wone, r.s_u, 0, seq=partner)])
    for b in range(blocks):

        @pl.when(me == b)
        def _():
            r.gkr[pl.ds(me, 1)] = r.gk[pl.ds(8 * b, 8)][None]
            for d in range(n):
                if d != b:
                    to(b, d).wait_recv()
            gsum = r.gkr[0]
            for d in range(1, n):
                gsum = gsum + r.gkr[d]
            r.gkm[...] = gsum
            r.gkall[pl.ds(8 * b, 8), mine] = gsum
            for i in range(1, n):
                back(b, i).start()

    got(c_l[2:3])
    r.lnf[other] = r.lnr[...].astype(f32)
    got(c_s)
    acc = r.smr[0]
    for d in range(1, n):
        acc = acc + r.smr[d]
    r.sums[...] = acc
    for b in range(blocks):

        @pl.when(me != b)
        def _():
            back(b, 0).wait_recv()

    c_k = go([remote(r.gkall.at[:, mine], r.gkall.at[:, mine], r.s_l, 3, head=core)])
    got(c_u)
    r.gw[...] = total + r.wone[...].astype(f32)
    got(c_k + c_l[1:2] + c_p[1:2])

    sent(c_t + c_w + c_v + c_h + c_p + c_x + c_d + c_g + c_q + c_a + c_o + c_e + c_f + c_z + c_y + c_l + c_s + c_u + c_k)
    for h, o in enumerate(OWNERS):

        @pl.when(g != o)
        def _():
            to_owner(r.blkb, r.recvb, r.s_b, h, g).wait_send()
            to_owner(r.blkd, r.recvd, r.s_c, h, g).wait_send()

        @pl.when(g == o)
        def _():
            for i in range(1, size):
                spread(h, i).wait_send()

    for b in range(blocks):

        @pl.when(me != b)
        def _():
            to(b, me).wait_send()

        @pl.when(me == b)
        def _():
            for i in range(1, n):
                back(b, i).wait_send()


def result_kernel(outf, lnf, dhf, gw, sums, gkall, out, gx, gwqkv, gwoutt, ggain, gbias, gtaps, gob, k7o, k5o, k3o, gpb):
    out[...] = outf[...]
    gx[...] = dhf[...] + lnf[...]
    gwqkv[...] = gw[0:3]
    gwoutt[...] = gw[3]
    for i in range(4):
        ggain[:, 128 * i:128 * i + 128] = sums[i:i + 1]
        gbias[:, 128 * i:128 * i + 128] = sums[4 + i:5 + i]
    rows = gkall[51:55, my_half()]
    li, lt = iota((256, 33), 0), iota((256, 33), 1)
    spot = jnp.where(((li + lt) & 255) == 16, 1.0, 0.0).astype(bf16)
    parts = [mm(piece.astype(bf16), spot) for piece in split3(rows)]
    gtaps[...] = parts[0] + parts[1] + parts[2]
    gob[...] = gkall[49:50]
    gpb[...] = gkall[50:51]
    spill_kernels(gkall, k7o, k5o, k3o)


def ring(rows_up, rows_down):
    count = lax.axis_size("seq")
    up = lax.ppermute(rows_up, "seq", [(i, (i + 1) % count) for i in range(count)])
    down = lax.ppermute(rows_down, "seq", [((i + 1) % count, i) for i in range(count)])
    return jnp.stack([up, down])


def half_of(full, axis):
    return lax.dynamic_slice_in_dim(full, lax.axis_index("head") * 256, 256, axis)


def swap(n, blocks):
    half, _, _ = place(n)
    theirs = lax.ppermute(jnp.where(half == 0, blocks[1], blocks[0]), "seq", [(i, (i + n // 2) % n) for i in range(n)])
    own = jnp.where(half == 0, blocks[0], blocks[1])
    return jnp.where(half == 0, jnp.stack([own, theirs]), jnp.stack([theirs, own]))


def half_sum(n, value):
    half, _, _ = place(n)
    pair = lax.psum(jnp.stack([jnp.where(half == s, value, 0.0) for s in range(2)]), "seq")
    return jnp.where(half == 0, pair[0], pair[1])


def half_max(n, value):
    half, _, _ = place(n)
    pair = lax.pmax(jnp.stack([jnp.where(half == s, value, -jnp.inf) for s in range(2)]), "seq")
    return jnp.where(half == 0, pair[0], pair[1])


def norm_kernel(n, cnt, xblk, gain, bias, normed, xp):
    half, g, _ = place(n)
    for b in range(2):
        normed[b] = norm_rows(xblk[b], gain[...], bias[...])
    xp[...] = segment_sums(n, g, cnt[half], normed)


def back_conv_kernel(n, cnt, cot, halo, k7, k5, k3, dh, kc, zs, pad):
    join_taps(kc, k7, k5, k3)
    for s in range(2):
        back_conv(n, cnt[s], s, cot, halo, kc, dh, zs, pad)


def start_plain(n, counts, tok, cot, gain, bias, wqkv, woutt, k7, k5, k3, scratch):
    half, _, _ = place(n)
    rows = tok.shape[1]
    count = counts[half]
    xblk = swap(n, tok)
    normed, xp = call(
        functools.partial(norm_kernel, n), [sds((2, rows, 512), bf16), sds((MARKS, 256))], [SMEM] + [VMEM] * 3
    )(counts, xblk, gain, bias)
    low, high = edges(count, jnp.arange(MARKS, dtype=jnp.int32))
    xbar = (half_sum(n, xp) / (high - low).astype(f32)[:, None]).astype(bf16)
    xbar = lax.all_gather(xbar, "head", axis=1, tiled=True)
    wts = jnp.concatenate([wqkv, woutt[None]], axis=0)
    wall = lax.all_gather(wts, "seq", axis=1, tiled=True)
    mine = half_of(cot, 2)
    dh = call(functools.partial(back_conv_kernel, n), sds((2, rows, 256)), [SMEM] + [VMEM] * 5, scratch)(
        counts, cot, ring(mine[:, -192:], mine[:, :192]), k7, k5, k3
    )
    dhrb = swap(n, lax.all_gather(dh.astype(bf16), "head", axis=2, tiled=True))
    return xblk, normed, xbar, wall, dh, dhrb


def half_ring(n, hal):
    size = n // 2
    up = [(i, i // size * size + (i + 1) % size) for i in range(n)]
    return jnp.stack([lax.ppermute(hal[1], "seq", up), lax.ppermute(hal[0], "seq", [(j, i) for i, j in up])])


def three_rows(stat, first):
    return (stat[:, first:first + 1] + stat[:, first + 1:first + 2]) + stat[:, first + 2:first + 3]


def reduce_plain(n, blkb, blkd, halv, hald):
    _, g, _ = place(n)
    stat = blkb[:, 64:].astype(f32)
    top, total = three_rows(stat, 0), three_rows(stat, 3)
    best = half_max(n, top)
    w = jnp.exp(top - best)
    total = half_sum(n, total * w)
    value = half_sum(n, blkb[:, 0:64].astype(f32) * w)
    dct = half_sum(n, blkd.astype(f32)).astype(bf16)
    stat = jnp.concatenate(split3(best) + split3(total) + [jnp.zeros((4, 10, MARKS), f32)], axis=1)
    whole = jnp.concatenate([value, stat], axis=1).astype(bf16)
    h = head_of(g)
    recvb, recvd = lax.dynamic_slice_in_dim(whole, h, 1, 0), lax.dynamic_slice_in_dim(dct, h, 1, 0)
    return recvb, recvd, half_ring(n, halv), half_ring(n, hald)


def spread_plain(n, res):
    _, g, _ = place(n)
    held = ((jnp.arange(4) == head_of(g)) & is_owner(g))[:, None, None]
    return half_sum(n, jnp.where(held, res[None].astype(f32), 0.0)).astype(bf16)


def scores_kernel(n, cnt, normed, xbar, wall, dhrb, qt, kt, vt, qlt, klt, dot, wback, a1, e3, blkb, blkd, halv, hald):
    half, _, _ = place(n)
    count = cnt[half]
    wback[...] = wall[3].astype(f32).T.astype(bf16)
    project(n, count, normed, wall, qt, kt, vt)
    value_edges(n, count, normed, wall, halv)
    landmarks(xbar, wall, qlt, klt)
    key_scores(n, count, kt, qlt, vt, e3, blkb)
    query_scores(qt, klt, a1)
    out_grads(dhrb, wback, dot, hald)
    partial_dc(dot, a1, blkd)


def chain_kernel(n, recvb, recvd, qlt, klt, res, dqz, ps, ts, xs):
    _, g, _ = place(n)
    here = head_rows(head_of(g))
    dqz[...] = jnp.zeros_like(dqz)

    @pl.when(is_owner(g))
    def _():
        chain(qlt[here], klt[here], recvb, recvd, res, dqz, ps, ts, xs)()


def grads_kernel(n, cnt, normed, xbar, wall, wback, dhrb, qt, kt, vt, qlt, klt, dot, a1, e3, blkb, resall, rhv, rhd, taps,
                 dqz, po, dn, ep, wpart, gtaps, tm, th, hv, hdt, hvr, vr, conv, dconv, gsum, att, dp, dlm):
    half, _, _ = place(n)
    make_bands(taps, normed.shape[1], tm, th)
    value_conv(n, vt, rhv, tm, th, hv, vr, hvr, conv)
    value_conv_back(n, dot, rhd, tm, th, hdt, vr, hvr, dconv, gsum, gtaps)
    attend(resall, a1, conv, att)
    output_rows(att, wback, po)
    score_grads(n, cnt[half], qt, kt, vt, qlt, klt, dot, a1, e3, blkb, resall, dqz, dconv, dp, dlm)
    mark_rows(wall, dlm, ep)
    input_rows(wall, dp, dn)
    weight_grads(normed, xbar, dhrb, att, dp, dlm, wpart)


def hidden_kernel(cnt, tok, obias, part, hid, z):
    for s in range(2):
        z[s] = hidden_rows(cnt[s], s, tok, obias, part[s], hid).astype(bf16)


def final_kernel(n, cnt, hid, halo, cot, k7, k5, k3, pbias, xblk, dn, dnr, eall, gain, dh, gtaps,
                 outh, lnb, gk, small, kc, zs, pad, gacc):
    half, g, _ = place(n)
    join_taps(kc, k7, k5, k3)
    gacc[...] = jnp.zeros_like(gacc)
    small[...] = jnp.zeros_like(small)
    for s in range(2):
        grid_forward(n, cnt[s], s, hid, halo, cot, kc, pbias, outh, zs, pad, gacc)
    grid_sums(gacc, dh, cot, gtaps, gk)
    for b in range(2):
        lnb[b] = norm_back(n, g, cnt[half], b, xblk, dn, dnr, eall, gain, small)


def late_plain(n, counts, tok, cot, xblk, dh, po, ep, dn, wpart, gtaps, gain, obias, pbias, k7, k5, k3, scratch):
    rows = tok.shape[1]
    part = half_of(swap(n, lax.psum(po.astype(f32), "head").astype(bf16)), 2)
    hid, z = call(hidden_kernel, [sds((2, rows, 256)), sds((2, rows, 256), bf16)], [SMEM] + [VMEM] * 3)(
        counts, tok, obias, part
    )
    dnr = lax.ppermute(dn, "head", [(0, 1), (1, 0)])
    eall = half_sum(n, lax.psum(ep.astype(f32), "head")).astype(bf16)
    outh, lnb, gk, small = call(
        functools.partial(final_kernel, n),
        [sds((2, rows, 256), bf16), sds((2, rows, 512)), sds((56, 256)), sds((8, 512))],
        [SMEM] + [VMEM] * 14,
        scratch + [pltpu.VMEM((49, 8, 256), f32)],
    )(counts, hid, ring(z[:, -192:], z[:, :192]), cot, k7, k5, k3, pbias, xblk, dn, dnr, eall, gain, dh, gtaps)
    out = lax.all_gather(outh, "head", axis=2, tiled=True)
    dhf = lax.all_gather(dh, "head", axis=2, tiled=True)
    gw = lax.psum_scatter(wpart.astype(f32), "seq", scatter_dimension=1, tiled=True)
    gk, small = lax.psum((gk, small), "seq")
    gkall = lax.all_gather(gk, "head", axis=1, tiled=True)
    return out, swap(n, lnb), dhf, gw, small[0:2].reshape(8, 128), gkall


def layer_plain(n, counts, tok, cot, gain, bias, wqkv, woutt, taps, obias, pbias, k7, k5, k3):
    rows = tok.shape[1]
    made = layer_buffers(n, rows, wqkv.shape[1])

    def out(*names):
        return [sds(*made[name]) for name in names]

    def tmp(*names):
        return [pltpu.VMEM(*made[name]) for name in names]

    conv_tmp = tmp("kc", "zs", "pad")
    xblk, normed, xbar, wall, dh, dhrb = start_plain(
        n, counts, tok, cot, gain, bias, wqkv, woutt, k7, k5, k3, conv_tmp
    )
    qt, kt, vt, qlt, klt, dot, wback, a1, e3, blkb, blkd, halv, hald = call(
        functools.partial(scores_kernel, n),
        out("qt", "kt", "vt", "qlt", "klt", "dot", "wback", "a1", "e3", "blkb", "blkd", "halv", "hald"),
        [SMEM] + [VMEM] * 4,
    )(counts, normed, xbar, wall, dhrb)
    recvb, recvd, rhv, rhd = reduce_plain(n, blkb, blkd, halv, hald)
    res, dqz = call(
        functools.partial(chain_kernel, n), out("res", "dqz"), [VMEM] * 4, tmp("ps", "ts", "xs")
    )(recvb, recvd, qlt, klt)
    resall = spread_plain(n, res)
    po, dn, ep, wpart, gtaps = call(
        functools.partial(grads_kernel, n),
        out("po", "dn", "ep", "wpart", "gtaps"),
        [SMEM] + [VMEM] * 19,
        tmp("tm", "th", "hv", "hdt", "hvr", "vr", "conv", "dconv", "gsum", "att", "dp", "dlm"),
    )(counts, normed, xbar, wall, wback, dhrb, qt, kt, vt, qlt, klt, dot, a1, e3, blkb, resall, rhv, rhd, taps, dqz)
    return late_plain(
        n, counts, tok, cot, xblk, dh, po, ep, dn, wpart, gtaps, gain, obias, pbias, k7, k5, k3, conv_tmp
    )


def shards(n, tokens, counts, ln_gain, ln_bias, w_qkv, conv_taps, w_out, out_bias, kernel7, kernel5, kernel3, ppeg_bias, cotangent):
    rows, wr = tokens.shape[1], w_qkv.shape[1]
    gain, bias, obias, pbias = (v[None, :] for v in (ln_gain, ln_bias, out_bias, ppeg_bias))
    args = (counts, tokens, cotangent, gain, bias, w_qkv, w_out.T, conv_taps, obias, pbias, kernel7, kernel5, kernel3)
    if n == 16:
        results, buffers = layer_results(n, rows, wr), layer_buffers(n, rows, wr)
        names = INPUTS + tuple(results) + tuple(buffers) + SEMS
        made = call(
            functools.partial(layer_kernel, n, names),
            [sds(*v) for v in results.values()],
            [SMEM] + [VMEM] * 12,
            [pltpu.VMEM(*v) for v in buffers.values()] + [DMA((2, n)) for _ in SEMS],
            cid=0,
            vmem=60,
        )(*args)
    else:
        made = layer_plain(n, *args)
    vec = sds((1, 512))
    out, gx, gwqkv, gwoutt, ggain, gbias, gtaps, gob, k7o, k5o, k3o, gpb = call(
        result_kernel,
        [sds((2, rows, 512), bf16), sds((2, rows, 512)), sds((3, wr, 256)), sds((wr, 256)), vec, vec, sds((4, 33)), vec,
         sds((7, 7, 512)), sds((5, 5, 512)), sds((3, 3, 512)), vec],
        [VMEM] * 6,
    )(*made)
    return out, gx, ggain[0], gbias[0], gwqkv, gtaps, gwoutt.T, gob[0], k7o, k5o, k3o, gpb[0]


def solution(mesh):
    rows, cols = P(None, "seq", None), P(None, "seq", "head")
    return jax.shard_map(
        functools.partial(shards, mesh.shape["seq"]),
        mesh=mesh,
        in_specs=(rows, P(), P(), P(), cols, P("head", None), P("head", "seq"), P(), P(), P(), P(), P(), rows),
        out_specs=(rows, rows, P(), P(), cols, P("head", None), P("head", "seq"), P(), P(), P(), P(), P()),
        check_vma=False,
    )
```

```python
import functools

import jax
import jax.numpy as jnp
from jax import lax
from jax.experimental import pallas as pl
from jax.experimental.pallas import tpu as pltpu
from jax.sharding import PartitionSpec as P

MESH = pl.DeviceIdType.MESH
GRID_W = 64
MARKS = 256
SWEEPS = 6
EPSILON = 1e-05
f32, bf16 = jnp.float32, jnp.bfloat16
VMEM = pl.BlockSpec(memory_space=pltpu.VMEM)
SMEM = pl.BlockSpec(memory_space=pltpu.SMEM)
DMA = pltpu.SemaphoreType.DMA
SCALE = 64 ** -0.5
BLK = 144
PART = 80


def sds(shape, dtype=f32):
    return jax.ShapeDtypeStruct(shape, dtype)


def call(kernel, outs, specs, scratch=(), cid=None, vmem=56):
    extra = {} if cid is None else dict(collective_id=cid, has_side_effects=True)
    return pl.pallas_call(
        kernel,
        out_shape=outs,
        in_specs=specs,
        out_specs=jax.tree.map(lambda _: VMEM, outs),
        scratch_shapes=list(scratch),
        compiler_params=pltpu.CompilerParams(vmem_limit_bytes=vmem * 2**20, **extra),
    )


def mm(left, right, cl=1, cr=0):
    return lax.dot_general(left, right, (((cl,), (cr,)), ((), ())), preferred_element_type=f32)


def split(value):
    high = value.astype(bf16)
    return high, (value - high.astype(f32)).astype(bf16)


def split3(row):
    high = row.astype(bf16).astype(f32)
    rest = row - high
    mid = rest.astype(bf16).astype(f32)
    return [high, mid, rest - mid]


def mm3(left, right, cl=1, cr=0):
    (lh, ll), (rh, rl) = left, right
    return mm(lh, rh, cl, cr) + (mm(lh, rl, cl, cr) + mm(ll, rh, cl, cr))


def iota(shape, dim):
    return lax.broadcasted_iota(jnp.int32, shape, dim)


def edges(count, marks):
    return (marks * count + (MARKS - 1)) >> 8, ((marks + 1) * count + (MARKS - 1)) >> 8


def member(count, start, rows):
    low, high = edges(count, iota((MARKS, rows), 0))
    slot = iota((MARKS, rows), 1) + start
    return jnp.where((slot >= low) & (slot < high), 1.0, 0.0).astype(bf16)

OWNERS = (0, 3, 5, 6)


def place(n):
    me = lax.axis_index("seq")
    return me // (n // 2), lax.rem(me, n // 2), lax.rem(me + n // 2, n)


def head_of(g):
    return jnp.where(g == 0, 0, jnp.where(g == 3, 1, jnp.where(g == 5, 2, 3)))


def is_owner(g):
    return (g == 0) | (g == 3) | (g == 5) | (g == 6)


def my_half():
    return pl.ds(pl.multiple_of(lax.axis_index("head") * 256, 256), 256)


def block_start(n, g, b, rows):
    return (g + b * (n // 2)) * rows


def places(n, g, rows, shape, dim):
    at = iota(shape, dim)
    return at + g * rows + jnp.where(at >= rows, (n // 2 - 1) * rows, 0)


def norm_rows(x, gain, bias):
    x = x.astype(f32)
    xc = x - jnp.mean(x, axis=-1, keepdims=True)
    inv = lax.rsqrt(jnp.mean(xc * xc, axis=-1, keepdims=True) + EPSILON)
    return (xc * inv * gain + bias).astype(bf16)


def segment_sums(n, g, count, normed):
    rows = normed.shape[1]
    mine = my_half()
    return sum(mm(member(count, block_start(n, g, b, rows), rows), normed[b, :, mine]) for b in range(2))


def join_taps(kc, k7, k5, k3):
    mine = my_half()
    kc[...] = jnp.zeros_like(kc)
    for a in range(7):
        kc[a, 0:7] = k7[a, :, mine]
    for a in range(5):
        kc[a + 1, 1:6] = kc[a + 1, 1:6] + k5[a, :, mine]
    for a in range(3):
        kc[a + 2, 2:5] = kc[a + 2, 2:5] + k3[a, :, mine]


def load_grid(zs, pad, body, top, bottom):
    grid = body.shape[0] // GRID_W
    pad[...] = jnp.zeros_like(pad)
    pad[0:3, 8:8 + GRID_W] = top.reshape(3, GRID_W, 256)
    pad[3:3 + grid, 8:8 + GRID_W] = body.reshape(grid, GRID_W, 256)
    pad[3 + grid:6 + grid, 8:8 + GRID_W] = bottom.reshape(3, GRID_W, 256)
    for b in range(7):
        zs[b] = pad[:, 5 + b:5 + b + GRID_W, :]


def conv_row(zs, kc, i, flip):
    acc = jnp.zeros((GRID_W, 256), f32)
    for a in range(7):
        for b in range(7):
            ka, kb = (6 - a, 6 - b) if flip else (a, b)
            acc = acc + kc[ka, kb:kb + 1, :] * zs[b, i + a]
    return acc


def load_cot(n, b, cotb, top, bottom, zs, pad):
    at = block_start(n, place(n)[1], b, cotb.shape[1])
    top = jnp.where(at > 0, top.astype(f32), 0.0)
    bottom = jnp.where(at < (n - 1) * cotb.shape[1], bottom.astype(f32), 0.0)
    load_grid(zs, pad, cotb[b].astype(f32), top, bottom)


def back_conv(n, count, b, cotb, zs, kc, dh):
    _, g, _ = place(n)
    rows = cotb.shape[1]

    @pl.loop(0, rows // GRID_W)
    def _(i):
        acc = conv_row(zs, kc, i, True)
        here = pl.ds(pl.multiple_of(i * GRID_W, GRID_W), GRID_W)
        slot = iota((GRID_W, 256), 0) + (block_start(n, g, b, rows) + i * GRID_W)
        dh[b, here] = cotb[b, here].astype(f32) + jnp.where(slot < count, acc, 0.0)


def kernel_grads(n, count, b, i, hid, zs, gacc):
    _, g, _ = place(n)
    rows = hid.shape[1]
    here = pl.ds(pl.multiple_of(i * GRID_W, GRID_W), GRID_W)
    slot = iota((GRID_W, 256), 0) + (block_start(n, g, b, rows) + i * GRID_W)
    z = jnp.where(slot < count, hid[b, here], 0.0)
    for ka in range(7):
        for kb in range(7):
            part = (z * zs[6 - kb, i + 6 - ka]).reshape(GRID_W // 8, 8, 256)
            gacc[ka * 7 + kb] = gacc[ka * 7 + kb] + jnp.sum(part, axis=0)


def hidden_rows(n, count, b, x, obias, part, hid):
    _, g, _ = place(n)
    rows = x.shape[1]
    mine = my_half()
    hid[b] = x[b, :, mine].astype(f32) + part.astype(f32) + obias[:, mine]
    slot = iota((rows, 256), 0) + block_start(n, g, b, rows)
    return jnp.where(slot < count, hid[b], 0.0)


def ring_ends(n, g, b, recv):
    top = jnp.where(g > 0, recv[0, b].astype(f32), recv[0, 0].astype(f32) * b)
    bottom = jnp.where(g < n // 2 - 1, recv[1, b].astype(f32), recv[1, 1].astype(f32) * (1 - b))
    return top, bottom


def grid_forward(n, count, b, hid, halo, kc, pbias, outh, zs, pad):
    _, g, _ = place(n)
    rows = hid.shape[1]
    mine = my_half()
    slot = iota((rows, 256), 0) + block_start(n, g, b, rows)
    top, bottom = ring_ends(n, g, b, halo)
    load_grid(zs, pad, jnp.where(slot < count, hid[b], 0.0), top, bottom)

    @pl.loop(0, rows // GRID_W)
    def _(i):
        here = pl.ds(pl.multiple_of(i * GRID_W, GRID_W), GRID_W)
        acc = conv_row(zs, kc, i, False)
        outh[b, here] = (hid[b, here] + acc + pbias[:, mine]).astype(bf16)


def grid_sums(gacc, dh, cotb, gtaps, gk):
    for t in range(49):
        gk[t:t + 1] = jnp.sum(gacc[t], axis=0, keepdims=True)
    gk[49:50] = jnp.sum(dh[0], axis=0, keepdims=True) + jnp.sum(dh[1], axis=0, keepdims=True)
    g = cotb[0].astype(f32) + cotb[1].astype(f32)
    gk[50:51] = jnp.sum(g, axis=0, keepdims=True)
    gk[51:55] = gtaps[0:4]
    gk[55:56] = jnp.zeros((1, 256), f32)


def norm_back(n, g, count, b, x, dn, dnr, eall, gain, small):
    rows = x.shape[1]
    low, high = edges(count, iota((MARKS, 512), 0))
    e = (eall[...].astype(f32) / (high - low).astype(f32)).astype(bf16)
    mem = member(count, block_start(n, g, b, rows), rows)
    total = (dn[b].astype(f32) + dnr[b].astype(f32)) + mm(mem, e, 0, 0)
    x = x[b].astype(f32)
    xc = x - jnp.mean(x, axis=-1, keepdims=True)
    inv = lax.rsqrt(jnp.mean(xc * xc, axis=-1, keepdims=True) + EPSILON)
    xh = xc * inv
    dg = total * gain[...]
    m1 = jnp.mean(dg, axis=-1, keepdims=True)
    m2 = jnp.mean(dg * xh, axis=-1, keepdims=True)
    small[0:1] = small[0:1] + jnp.sum(total * xh, axis=0, keepdims=True)
    small[1:2] = small[1:2] + jnp.sum(total, axis=0, keepdims=True)
    return (dg - m1 - xh * m2) * inv


def spill_kernels(gkall, k7o, k5o, k3o):
    for a in range(7):
        k7o[a] = gkall[7 * a:7 * a + 7]
    for a in range(5):
        k5o[a] = gkall[7 * a + 8:7 * a + 13]
    for a in range(3):
        k3o[a] = gkall[7 * a + 16:7 * a + 19]


def greet(peers, pair=True):
    sem = pltpu.get_barrier_semaphore()
    for peer in peers:
        pl.semaphore_signal(sem, inc=1, device_id={"seq": peer}, device_id_type=MESH)
    if pair:
        hd = lax.axis_index("head")
        pl.semaphore_signal(sem, inc=1, device_id={"head": 1 - hd}, device_id_type=MESH)
    pl.semaphore_wait(sem, len(peers) + (1 if pair else 0))


def everyone(n):
    me = lax.axis_index("seq")
    return [lax.rem(me + i, n) for i in range(n)]


def cube(n):
    half, g, _ = place(n)
    return [half * (n // 2) + lax.rem(g + i, n // 2) for i in range(n // 2)]


def remote(src, dst, sems, i, **where):
    return pltpu.make_async_remote_copy(
        src_ref=src, dst_ref=dst, send_sem=sems.at[0, i], recv_sem=sems.at[1, i], device_id=where, device_id_type=MESH
    )


def go(copies):
    for c in copies:
        c.start()
    return copies


def got(copies):
    for c in copies:
        c.wait_recv()


def sent(copies):
    for c in copies:
        c.wait_send()


def project(n, count, normed, wall, wt, qt, kt, vt):
    _, g, _ = place(n)
    for j in range(3):
        wt[j] = wall[j].T
    rows = normed.shape[1]
    nr = normed[...].reshape(2 * rows, 512)
    qt[...] = mm(wt[0], nr, 1, 1).astype(bf16)
    kt[...] = mm(wt[1], nr, 1, 1).astype(bf16)
    slots = places(n, g, rows, (256, 2 * rows), 1)
    vt[...] = jnp.where(slots < count, mm(wt[2], nr, 1, 1), 0.0).astype(bf16)


def value_edges(n, count, normed, wall, halv):
    _, g, _ = place(n)
    rows = normed.shape[1]
    for b in range(2):
        for side, first in ((0, 0), (1, rows - 16)):
            slot = iota((16, 256), 0) + (block_start(n, g, b, rows) + first)
            v = mm(normed[b, first:first + 16], wall[2])
            halv[side, b] = jnp.where(slot < count, v, 0.0).astype(bf16)


def landmarks(xbar, wt, qlt, klt):
    qlt[...] = mm(wt[0], xbar[...], 1, 1).astype(bf16)
    klt[...] = mm(wt[1], xbar[...], 1, 1).astype(bf16)


def head_rows(h):
    return pl.ds(pl.multiple_of(h * 64, 64), 64)


def key_scores(n, count, kt, qlt, vt, e3, blkb, beside=None):
    _, g, _ = place(n)
    wide = kt.shape[1]
    ok = places(n, g, wide // 2, (wide, MARKS), 0) < count
    for h in range(4):
        here = slice(64 * h, 64 * h + 64)
        s3 = jnp.where(ok, mm(kt[here] * SCALE, qlt[here], 0, 0), -1e30)
        top = jnp.max(s3, axis=0, keepdims=True)
        e = jnp.where(ok, jnp.exp(s3 - top), 0.0)
        total = jnp.sum(e, axis=0, keepdims=True)
        er = e.astype(bf16)
        e3[h] = er
        blkb[h, 0:64] = mm(vt[here], er).astype(bf16)
        stat = jnp.concatenate(split3(top) + split3(total) + [jnp.zeros((10, MARKS), f32)], axis=0)
        blkb[h, 64:80] = stat.astype(bf16)
        if beside:
            beside(h)


def query_scores(qt, klt, a1, beside=None):
    for h in range(4):
        here = slice(64 * h, 64 * h + 64)
        s1 = mm(klt[here] * SCALE, qt[here], 0, 0)
        e1 = jnp.exp(s1 - jnp.max(s1, axis=0, keepdims=True))
        a1[h] = (e1 / jnp.sum(e1, axis=0, keepdims=True)).astype(bf16)
        if beside:
            beside(h)


def out_grads(dhrb, wback, dot, hald):
    rows = dhrb.shape[1]
    dot[...] = mm(wback[...], dhrb[...].reshape(2 * rows, 512), 1, 1).astype(bf16)
    for b in range(2):
        for side, first in ((0, 0), (1, rows - 16)):
            hald[side, b] = mm(dhrb[b, first:first + 16], wback[...], 1, 1).astype(bf16)


def partial_dc(dot, a1, blkd):
    @pl.loop(0, 4, unroll=4)
    def _(h):
        blkd[h] = mm(dot[head_rows(h)], a1[h], 1, 1).astype(bf16)


def three(stat, first):
    return (stat[first:first + 1] + stat[first + 1:first + 2]) + stat[first + 2:first + 3]


class Chain:
    def __init__(self, ql, kl, r):
        self.ql, self.kl, self.r = ql, kl, r

    def begin(self):
        r = self.r
        s2 = mm(self.ql[...] * SCALE, self.kl[...], 0, 0)
        e2 = jnp.exp(s2 - jnp.max(s2, axis=1, keepdims=True))
        a = e2 / jnp.sum(e2, axis=1, keepdims=True)
        r.amat[...] = a
        asp = split(a)
        r.asp[0], r.asp[1] = asp
        inv = self.sums()[4]
        r.pcur[...] = mm3(asp, asp, 1, 1) * inv

    def sums(self):
        a = self.r.amat[...]
        cs, rs = jnp.sum(a, axis=0, keepdims=True), jnp.sum(a, axis=1, keepdims=True)
        cm, rm = jnp.max(cs, axis=1, keepdims=True), jnp.max(rs, axis=0, keepdims=True)
        return cs, rs, cm, rm, 1.0 / (cm * rm)

    def sweep(self, k):
        r = self.r
        p = r.pcur[...]
        psp = split(p)
        t = mm3(psp, psp)
        tsp = split(t)
        r.ps[k, 0], r.ps[k, 1] = psp
        r.ts[k, 0], r.ts[k, 1] = tsp
        if k < SWEEPS - 1:
            r.pcur[...] = 0.25 * (13.0 * p - 15.0 * t + mm3(tsp, split(7.0 * p - t)))

    def powers(self, k):
        r = self.r
        return (r.ps[k, 0], r.ps[k, 1]), (r.ts[k, 0], r.ts[k, 1])

    def apply(self, x, k):
        psp, tsp = self.powers(k)
        xt = mm3(split(x), tsp)
        return 0.25 * (13.0 * x + 7.0 * xt - mm3(split(15.0 * x + xt), psp))

    def forward(self):
        r = self.r
        parts = r.recvb.shape[0]
        tops = [three(r.recvb[d, 64:80].astype(f32), 0) for d in range(parts)]
        top = functools.reduce(jnp.maximum, tops)
        total, value = 0.0, 0.0
        for d in range(parts):
            w = jnp.exp(tops[d] - top)
            total = total + three(r.recvb[d, 64:80].astype(f32), 3) * w
            value = value + r.recvb[d, 0:64].astype(f32) * w
        value = value / total
        x = value
        for k in range(SWEEPS):
            r.xs[k] = x
            x = self.apply(x, k)
        r.xs[SWEEPS] = x
        ct = mm3(split(x), (r.asp[0], r.asp[1])) * self.sums()[4]
        r.res[0:64] = ct.astype(bf16)
        r.ctf[...] = ct
        self.top, self.total, self.value = top, total, value

    def backward(self):
        r = self.r
        dct = r.recvd[0].astype(f32)
        for d in range(1, r.recvd.shape[0]):
            dct = dct + r.recvd[d].astype(f32)
        r.dctf[...] = dct
        y = mm3(split(dct), (r.asp[0], r.asp[1]), 1, 1) * self.sums()[4]
        for k in range(SWEEPS - 1, -1, -1):
            r.ys[k] = y
            y = self.apply(y, k)
        dbr = y.astype(bf16)
        r.res[64:128] = dbr
        rt = jnp.sum(dbr.astype(f32) * self.value, axis=0, keepdims=True)
        stat = split3(self.top) + split3(self.total) + split3(rt) + [jnp.zeros((7, MARKS), f32)]
        r.res[128:144] = jnp.concatenate(stat, axis=0).astype(bf16)

    def power_grad(self, k):
        r = self.r
        psp, tsp = self.powers(k)
        outer = mm3(split(r.ys[k]), split(r.xs[k]), 0, 0) * 0.125
        d = outer + outer.T
        eq = 0.25 * r.ecur[...]
        pd = mm3(psp, split(d))
        pe = mm3(psp, split(eq))
        new = 13.0 * eq - 15.0 * d + mm3(split(7.0 * pe - pd), psp)
        left = 7.0 * pd - 15.0 * pe + mm3(tsp, split(7.0 * eq - d - (pe + pe.T)))
        r.ecur[...] = new + (left + left.T)

    def finish(self):
        r = self.r
        ql, kl, a, dct, e = self.ql[...], self.kl[...], r.amat[...], r.dctf[...], r.ecur[...]
        cs, rs, cm, rm, inv = self.sums()
        grad = mm3(split(r.xs[SWEEPS]), split(dct), 0, 0) * inv + mm3(split(e), (r.asp[0], r.asp[1])) * (2.0 * inv)
        p0 = r.ps[0, 0].astype(f32) + r.ps[0, 1].astype(f32)
        slope = jnp.sum(jnp.sum(dct * r.ctf[...], axis=0, keepdims=True), axis=1, keepdims=True)
        slope = -inv * (slope + jnp.sum(jnp.sum(e * p0, axis=0, keepdims=True), axis=1, keepdims=True))
        eqc, eqr = jnp.where(cs == cm, 1.0, 0.0), jnp.where(rs == rm, 1.0, 0.0)
        grad = grad + (slope * rm) * (eqc / jnp.sum(eqc, axis=1, keepdims=True))
        grad = grad + (slope * cm) * (eqr / jnp.sum(eqr, axis=0, keepdims=True))
        dsc = a * (grad - jnp.sum(a * grad, axis=1, keepdims=True)) * SCALE
        dh, dl = split(dsc)
        return mm(kl, dh, 1, 1) + mm(kl, dl, 1, 1), mm(ql, dh) + mm(ql, dl)


def add_chain(here, dlm, grads):
    for j in range(2):
        dlm[j, here] = (dlm[j, here].astype(f32) + grads[j]).astype(bf16)


def band(base, shift, rows):
    wide = jnp.broadcast_to(base, (rows, 256))
    return pltpu.roll(wide, shift, 1, stride=1, stride_axis=0)


def diagonals(g, shift):
    return jnp.sum(pltpu.roll(g, shift, 1, stride=1, stride_axis=0), axis=0, keepdims=True)


def make_bands(taps, rows, tm, th):
    pi, pj = iota((rows, rows), 0), iota((rows, rows), 1)
    inside = (pi - pj <= 16) & (pj - pi <= 16)
    hi, hj = iota((32, rows), 0), iota((32, rows), 1)
    far = jnp.where(hi < 16, hi - hj, hj - hi - (rows - 32)) >= 0
    ti, tl = iota((33, 256), 0), iota((33, 256), 1)
    spots = [jnp.where(((ti + tl if f == 0 else tl - ti + 32) & 255) == 16, 1.0, 0.0).astype(bf16) for f in range(2)]
    pieces = [piece.astype(bf16) for piece in split3(taps[...])]
    for f in range(2):
        lines = mm(pieces[0], spots[f]) + mm(pieces[1], spots[f]) + mm(pieces[2], spots[f])
        for h in range(4):
            line = lines[h:h + 1, :]
            full = jnp.where(inside, band(line, 0, rows), 0.0)
            tm[f, h, 0], tm[f, h, 1] = split(full)
            both = jnp.concatenate([band(line, 240, 16), band(line, 0, 16)], axis=0)
            th[f, h, 0], th[f, h, 1] = split(jnp.where(far, both, 0.0))


def value_conv(n, vt, recvv, tm, th, hv, vr, hvr, conv):
    _, g, _ = place(n)
    rows = vt.shape[1] // 2
    pi, pj = iota((rows, rows), 0), iota((rows, rows), 1)
    mirror = jnp.where(pi + pj == rows - 1, 1.0, 0.0).astype(bf16)
    si, sj = iota((32, 32), 0), iota((32, 32), 1)
    mirror32 = jnp.where(si + sj == jnp.where(si < 16, 15, 47), 1.0, 0.0).astype(bf16)
    for b in range(2):
        part = slice(b * rows, (b + 1) * rows)
        hv[b] = jnp.concatenate(ring_ends(n, g, b, recvv), axis=0).T.astype(bf16)
        vr[b] = mm(vt[:, part], mirror).astype(bf16)
        hvr[b] = mm(hv[b], mirror32).astype(bf16)

        @pl.loop(0, 4, unroll=4)
        def _(h):
            here = head_rows(h)
            v, vh = vt[here, part], hv[b, here]
            conv[here, part] = mm(v, tm[0, h, 0]) + mm(v, tm[0, h, 1]) + mm(vh, th[0, h, 0]) + mm(vh, th[0, h, 1])


def value_conv_back(n, dot, recvd, tm, th, hd, vr, hvr, dconv, gsum, gtaps):
    _, g, _ = place(n)
    rows = dot.shape[1] // 2
    pi, pj = iota((rows, rows), 0), iota((rows, rows), 1)
    hi, hj = iota((32, rows), 0), iota((32, rows), 1)
    near = (pi + pj >= rows - 17) & (pi + pj <= rows + 15)
    beyond = jnp.where(hi < 16, 15 - hi - hj, hi + hj - (rows + 15)) >= 0
    for b in range(2):
        hd[b] = jnp.concatenate(ring_ends(n, g, b, recvd), axis=0).T.astype(bf16)

    @pl.loop(0, 4, unroll=4)
    def _(h):
        here = head_rows(h)
        s, sh = 0.0, 0.0
        for b in range(2):
            part = slice(b * rows, (b + 1) * rows)
            d, dh = dot[here, part], hd[b, here]
            dconv[here, part] = mm(d, tm[1, h, 0]) + mm(d, tm[1, h, 1]) + mm(dh, th[1, h, 0]) + mm(dh, th[1, h, 1])
            s = s + mm(vr[b, here], d, 0, 0)
            sh = sh + mm(hvr[b, here], d, 0, 0)
        s, sh = jnp.where(near, s, 0.0), jnp.where(beyond, sh, 0.0)
        gsum[h] = jnp.broadcast_to(diagonals(s, 1) + diagonals(sh[0:16], 1) + diagonals(sh[16:32], 241), (8, 256))

    for h in range(4):
        gtaps[h:h + 1, :] = gsum[h, 0:1]
    gtaps[4:8, :] = jnp.zeros((4, 256), f32)


def attend(res, a1, conv, att):
    @pl.loop(0, 4, unroll=4)
    def _(h):
        here = head_rows(h)
        att[here] = (mm(res[h, 0:64], a1[h]) + conv[here]).astype(bf16)


def score_grads(n, count, qt, kt, vt, qlt, klt, dot, a1, e3, blkb, res, dconv, dp, dlm):
    _, g, _ = place(n)
    wide = qt.shape[1]
    slots = places(n, g, wide // 2, (64, wide), 1)

    @pl.loop(0, 4, unroll=4)
    def _(h):
        here = head_rows(h)
        ct, dbt = res[h, 0:64], res[h, 64:128]
        stat = res[h, 128:144].astype(f32)
        own = three(blkb[h, 64:80].astype(f32), 0)
        factor = jnp.exp(own - three(stat, 0)) / three(stat, 3)
        rt = three(stat, 6)
        do, v = dot[here], vt[here]
        a = a1[h].astype(f32)
        da = mm(ct, do, 0, 0)
        d1 = (a * (da - jnp.sum(a * da, axis=0, keepdims=True))).astype(bf16)
        dp[0, here] = mm(klt[here] * SCALE, d1).astype(bf16)
        dlm[1, here] = mm(qt[here] * SCALE, d1, 1, 1).astype(bf16)
        a3 = e3[h].astype(f32) * factor
        d3 = (a3 * (mm(v, dbt, 0, 0) - rt)).astype(bf16)
        dlm[0, here] = mm(kt[here] * SCALE, d3).astype(bf16)
        dp[1, here] = mm(qlt[here] * SCALE, d3, 1, 1).astype(bf16)
        dv = mm(dbt, a3.astype(bf16), 1, 1) + dconv[here]
        dp[2, here] = jnp.where(slots < count, dv, 0.0).astype(bf16)


def mark_rows(wall, dlm, ep):
    ep[...] = (mm(wall[0], dlm[0]) + mm(wall[1], dlm[1])).T.astype(bf16)


def input_rows(wall, dp, dn):
    rows = dn.shape[1]
    d = mm(wall[0], dp[0]) + mm(wall[1], dp[1]) + mm(wall[2], dp[2])
    dn[...] = d.T.astype(bf16).reshape(2, rows, 512)


def output_rows(att, wback, po):
    rows = po.shape[1]
    po[...] = mm(att[...], wback[...], 0, 0).astype(bf16).reshape(2, rows, 512)


def weight_grad(j, normed, xbar, dhrb, att, dp, dlm, wpart):
    rows = normed.shape[1]
    if j == 3:
        grad = mm(att[...], dhrb[...].reshape(2 * rows, 512))
    else:
        grad = mm(dp[j], normed[...].reshape(2 * rows, 512))
        if j < 2:
            grad = grad + mm(dlm[j], xbar[...])
    wpart[j] = grad.T.astype(bf16)


class Refs:
    def __init__(self, names, refs):
        self.__dict__.update(zip(names, refs))


INPUTS = ("cnt", "tok", "cot", "gain", "bias", "wqkv", "woutt", "taps", "obias", "pbias", "k7", "k5", "k3")


def layer_results(n, rows, wr):
    return dict(
        outf=((2, rows, 512), bf16), gxf=((2, rows, 512), f32), gw=((4, wr, 256), f32),
        sums=((8, 128), f32), gkall=((56, 512), f32),
    )


def layer_buffers(n, rows, wr):
    size = n // 2
    mb, wide, grid = MARKS // size, 2 * rows, rows // GRID_W
    half2 = (2, rows, 256)
    return dict(
        wts=((4, wr, 256), bf16), wall=((4, 512, 256), bf16), wback=((256, 512), bf16), wt=((3, 256, 512), bf16),
        xblk=((2, rows, 512), bf16), normed=((2, rows, 512), bf16), xbar=((MARKS, 512), bf16),
        xp=((MARKS, 256), bf16), xr=((size, mb, 256), bf16), xm=((mb, 256), bf16),
        halo=((2, 2, 192, 256), bf16), dh=(half2, f32), dhrb=((2, rows, 512), bf16),
        kc=((7, 8, 256), f32), zs=((7, grid + 6, GRID_W, 256), f32), zc=((2, 7, grid + 6, GRID_W, 256), f32), pad=((grid + 6, GRID_W + 16, 256), f32),
        qt=((256, wide), bf16), kt=((256, wide), bf16), vt=((256, wide), bf16), dot=((256, wide), bf16),
        qlt=((256, MARKS), bf16), klt=((256, MARKS), bf16), a1=((4, MARKS, wide), bf16), e3=((4, wide, MARKS), bf16),
        blkb=((4, PART, MARKS), bf16), blkd=((4, 64, MARKS), bf16),
        recvb=((size, PART, MARKS), bf16), recvd=((size, 64, MARKS), bf16),
        halv=((2, 2, 16, 256), bf16), hald=((2, 2, 16, 256), bf16), rhv=((2, 2, 16, 256), bf16), rhd=((2, 2, 16, 256), bf16),
        ps=((SWEEPS, 2, 256, 256), bf16), ts=((SWEEPS, 2, 256, 256), bf16), xs=((SWEEPS + 1, 64, 256), f32), ys=((SWEEPS, 64, 256), f32), ctf=((64, 256), f32), dctf=((64, 256), f32),
        amat=((256, 256), f32), asp=((2, 256, 256), bf16), pcur=((256, 256), f32), ecur=((256, 256), f32),
        res=((BLK, MARKS), bf16), resall=((8, BLK, MARKS), bf16),
        tm=((2, 4, 2, rows, rows), bf16), th=((2, 4, 2, 32, rows), bf16), hv=((2, 256, 32), bf16), hdt=((2, 256, 32), bf16),
        hvr=((2, 256, 32), bf16), vr=((2, 256, rows), bf16), conv=((256, wide), f32), dconv=((256, wide), f32),
        gsum=((4, 8, 256), f32), gtaps=((8, 256), f32), att=((256, wide), bf16), dp=((3, 256, wide), bf16),
        dlm=((2, 256, MARKS), bf16), po=((2, rows, 512), bf16), dn=((2, rows, 512), bf16), ep=((MARKS, 512), bf16),
        wpart=((4, 512, 256), bf16), er=((MARKS, 256), bf16), es=((MARKS, 256), bf16), erv=((size, mb, 256), bf16),
        em=((mb, 256), bf16), eall=((MARKS, 512), bf16), por=(half2, bf16),
        dnr=((2, rows, 512), bf16), hid=(half2, f32), z=(half2, bf16), cotb=(half2, bf16), lnf=((rows, 512), f32), dhf=((rows, 512), f32), zhalo=((2, 2, 192, 256), bf16),
        lnr=((rows, 512), bf16), lns=((rows, 256), bf16), wrv=((size, 2, 4, wr, 256), bf16), wsum=((4, wr, 256), bf16),
        wone=((4, wr, 256), bf16), gacc=((49, 8, 256), f32), outh=(half2, bf16), gk=((56, 256), f32),
        gkr=((n, 8, 256), f32), gkm=((8, 256), f32), small=((8, 512), f32), smr=((n, 8, 128), f32), smx=((8, 128), f32),
    )


SEMS = dict(
    s_w=2, s_v=2, s_n=2, s_t=1, s_h=4, s_x=1, s_g=1, s_p=4, s_d=1, s_b=1, s_c=1, s_r=1, s_q=4, s_a=4, s_e=1, s_f=1, s_z=2, s_l=5,
    s_y=1, s_u=1, s_k=1, s_m=1, s_s=1,
)


class Many:
    def __init__(self, total, sems, i, **where):
        self.sems, self.i, self.all = sems, i, remote(total, total, sems, i, **where)

    def add(self, src, dst, **where):
        remote(src, dst, self.sems, self.i, **where).start()

    def wait_recv(self):
        self.all.wait_recv()

    def wait_send(self):
        self.all.wait_send()


def layer_kernel(n, names, *refs):
    r = Refs(names, refs)
    half, g, partner = place(n)
    me = lax.axis_index("seq")
    hd = lax.axis_index("head")
    other = 1 - half
    size = n // 2
    rows = r.tok.shape[1]
    mb, wr = MARKS // size, r.wts.shape[1]
    mine = my_half()
    theirs = pl.ds(pl.multiple_of((1 - hd) * 256, 256), 256)
    count = r.cnt[half]
    near, far = cube(n), everyone(n)
    core = 1 - hd

    def wrow(device):
        return pl.ds(pl.multiple_of(device * wr, wr), wr)

    def marks(i):
        return pl.ds(pl.multiple_of(lax.rem(g + i, size) * mb, mb), mb)

    cube_rows = pl.ds(0, (size - 1) * wr)
    cube_marks = pl.ds(0, (size - 1) * mb)

    def fan(total, sems, i, pieces):
        group = Many(total, sems, i, seq=near[1])
        for j, (src, dst) in enumerate(pieces, 1):
            group.add(src, dst, seq=near[j])
        return [group]

    r.wts[0:3] = r.wqkv[...]
    r.wts[3] = r.woutt[...]
    greet(far[1:])
    qkv = slice(0, 3)
    c_w = go([remote(r.wts.at[qkv], r.wall.at[qkv, wrow(me)], r.s_w, 0, seq=partner)])
    c_t = go([remote(r.tok.at[other, :, mine], r.xblk.at[half, :, mine], r.s_t, 0, seq=partner)])
    c_v = fan(r.wall.at[qkv, cube_rows], r.s_v, 0, [(r.wts.at[qkv], r.wall.at[qkv, wrow(me)])] * (size - 1))
    up, down = far[1], far[n - 1]
    first, final = pl.ds(0, 192), pl.ds(rows - 192, 192)
    c_h = go([
        remote(r.cot.at[up // size, final, mine], r.halo.at[0, up // size], r.s_h, 0, seq=up),
        remote(r.cot.at[down // size, first, mine], r.halo.at[1, down // size], r.s_h, 1, seq=down),
    ])
    r.wall[:, wrow(me)] = r.wts[...]
    r.cotb[half] = r.cot[half, :, mine]
    r.xblk[half] = r.tok[half]
    r.normed[half] = norm_rows(r.tok[half], r.gain[...], r.bias[...])
    join_taps(r.kc, r.k7, r.k5, r.k3)
    got(c_w)
    pair_rows = (r.wall.at[qkv, wrow(partner)],) * 2
    c_v += fan(r.wall.at[qkv, cube_rows], r.s_v, 1, [pair_rows] * (size - 1))
    make_bands(r.taps, rows, r.tm, r.th)

    got(c_t)
    c_p = go([remote(r.xblk.at[other, :, mine], r.xblk.at[other, :, mine], r.s_p, 0, head=core)])
    c_d = go([remote(r.cot.at[other, :, mine], r.cotb.at[half], r.s_d, 0, seq=partner)])
    got(c_p)
    r.normed[other] = norm_rows(r.xblk[other], r.gain[...], r.bias[...])
    r.xp[...] = segment_sums(n, g, count, r.normed).astype(bf16)
    c_x = fan(r.xr.at[pl.ds(0, size - 1)], r.s_x, 0, [(r.xp.at[marks(i)], r.xr.at[g]) for i in range(1, size)])
    row = marks(0)
    r.xr[pl.ds(g, 1)] = r.xp[row][None]
    c_w += go([remote(r.wts.at[3], r.wall.at[3, wrow(me)], r.s_w, 1, seq=partner)])
    got(c_h)
    load_cot(n, half, r.cotb, r.halo[0, half], r.halo[1, half], r.zc.at[half], r.pad)
    back_conv(n, count, half, r.cotb, r.zc.at[half], r.kc, r.dh)
    c_p += go([remote(r.dh.at[half], r.dhf.at[:, mine], r.s_p, 2, head=core)])
    r.dhf[:, mine] = r.dh[half]
    got(c_x)
    total = r.xr[0].astype(f32)
    for d in range(1, size):
        total = total + r.xr[d].astype(f32)
    low, high = edges(count, iota((mb, 256), 0) + g * mb)
    r.xm[...] = (total / (high - low).astype(f32)).astype(bf16)
    r.xbar[row, mine] = r.xm[...]
    c_g = fan(r.xbar.at[cube_marks, mine], r.s_g, 0, [(r.xm, r.xbar.at[row, mine])] * (size - 1))
    got(c_d)
    above = jnp.where((g == size - 1) & (half == 0), half, other)
    below = jnp.where((g == 0) & (half == 1), half, other)
    c_h += go([
        remote(r.cotb.at[above, final], r.halo.at[0, other], r.s_h, 2, seq=near[1]),
        remote(r.cotb.at[below, first], r.halo.at[1, other], r.s_h, 3, seq=near[size - 1]),
    ])
    got(c_v)
    project(n, count, r.normed, r.wall, r.wt, r.qt, r.kt, r.vt)
    c_n = fan(r.wall.at[3, cube_rows], r.s_n, 0, [(r.wts.at[3], r.wall.at[3, wrow(me)])] * (size - 1))
    got(c_w[1:])
    pair_row = (r.wall.at[3, wrow(partner)],) * 2
    c_n += fan(r.wall.at[3, cube_rows], r.s_n, 1, [pair_row] * (size - 1))
    got(c_g)
    c_p += go([remote(r.xbar.at[:, mine], r.xbar.at[:, mine], r.s_p, 1, head=core)])
    value_edges(n, count, r.normed, r.wall, r.halv)
    c_q = go([
        remote(r.halv.at[1], r.rhv.at[0], r.s_q, 0, seq=near[1]),
        remote(r.halv.at[0], r.rhv.at[1], r.s_q, 1, seq=near[size - 1]),
    ])
    got(c_h[2:])
    load_cot(n, other, r.cotb, r.halo[0, other], r.halo[1, other], r.zc.at[other], r.pad)
    back_conv(n, count, other, r.cotb, r.zc.at[other], r.kc, r.dh)
    r.dhrb[:, :, mine] = r.dh[...].astype(bf16)
    c_p += go([remote(r.dhrb.at[:, :, mine], r.dhrb.at[:, :, mine], r.s_p, 3, head=core)])

    got(c_p[2:3])
    landmarks(r.xbar, r.wt, r.qlt, r.klt)
    here = head_rows(head_of(g))
    one = Chain(r.qlt.at[here], r.klt.at[here], r)
    one.begin()
    key_scores(n, count, r.kt, r.qlt, r.vt, r.e3, r.blkb, one.sweep)

    def give(blk, recv, sems):
        for h, o in enumerate(OWNERS):

            @pl.when(g != o)
            def _():
                remote(blk.at[h], recv.at[g], sems, 0, seq=half * size + o).start()

            @pl.when(g == o)
            def _():
                recv[pl.ds(g, 1)] = blk[h:h + 1]

    def gave(blk, sems):
        remote(blk, blk, sems, 0, seq=near[1]).wait_send()

    give(r.blkb, r.recvb, r.s_b)
    query_scores(r.qt, r.klt, r.a1, lambda h: one.sweep(4 + h) if h < 2 else None)
    got(c_n)
    r.wback[...] = r.wall[3].T
    got(c_p[3:4])
    out_grads(r.dhrb, r.wback, r.dot, r.hald)
    c_q += go([
        remote(r.hald.at[1], r.rhd.at[0], r.s_q, 2, seq=near[1]),
        remote(r.hald.at[0], r.rhd.at[1], r.s_q, 3, seq=near[size - 1]),
    ])
    partial_dc(r.dot, r.a1, r.blkd)
    give(r.blkd, r.recvd, r.s_c)

    @pl.when(is_owner(g))
    def _():
        def wait_for(recv, sems):
            remote(recv.at[pl.ds(0, size - 1)], recv.at[pl.ds(0, size - 1)], sems, 0, seq=near[1]).wait_recv()

        wait_for(r.recvb, r.s_b)
        one.forward()
        wait_for(r.recvd, r.s_c)
        one.backward()
        for h, o in enumerate(OWNERS):

            @pl.when(g == o)
            def _():
                for i in range(1, size):
                    remote(r.res, r.resall.at[h], r.s_r, 0, seq=near[i]).start()
                r.resall[h] = r.res[...]

    got(c_q)
    value_conv(n, r.vt, r.rhv, r.tm, r.th, r.hv, r.vr, r.hvr, r.conv)
    value_conv_back(n, r.dot, r.rhd, r.tm, r.th, r.hdt, r.vr, r.hvr, r.dconv, r.gsum, r.gtaps)
    r.small[...] = jnp.zeros_like(r.small)
    r.gacc[...] = jnp.zeros_like(r.gacc)

    def results(count):
        return remote(r.resall.at[pl.ds(0, count)], r.resall.at[pl.ds(0, count)], r.s_r, 0, seq=near[1])

    @pl.when(is_owner(g))
    def _():
        results(3).wait_recv()

    @pl.when(jnp.logical_not(is_owner(g)))
    def _():
        results(4).wait_recv()

    attend(r.resall, r.a1, r.conv, r.att)
    output_rows(r.att, r.wback, r.po)
    c_a = go([remote(r.po.at[:, :, theirs], r.por, r.s_a, 0, head=core)])
    weights = (r.normed, r.xbar, r.dhrb, r.att, r.dp, r.dlm, r.wpart)
    c_y = [Many(r.wrv.at[pl.ds(0, size - 1)], r.s_y, 0, seq=near[1])]

    def send_weights(j):
        for i in range(1, size):
            for k, device in enumerate((near[i], lax.rem(near[i] + size, n))):
                c_y[0].add(r.wpart.at[j, wrow(device)], r.wrv.at[g, k, j], seq=near[i])

    score_grads(n, count, r.qt, r.kt, r.vt, r.qlt, r.klt, r.dot, r.a1, r.e3, r.blkb, r.resall, r.dconv, r.dp, r.dlm)
    got(c_a[0:1])
    for b in range(2):
        part = r.po[b, :, mine].astype(f32) + r.por[b].astype(f32)
        r.z[b] = hidden_rows(n, count, b, r.xblk, r.obias, part, r.hid).astype(bf16)
    c_z = go([
        remote(r.z.at[:, final], r.zhalo.at[0], r.s_z, 0, seq=near[1]),
        remote(r.z.at[:, first], r.zhalo.at[1], r.s_z, 1, seq=near[size - 1]),
    ])
    r.ecur[...] = jnp.zeros_like(r.ecur)
    lines = rows // GRID_W

    @pl.loop(0, 2 * lines)
    def _(i):
        kernel_grads(n, count, i // lines, lax.rem(i, lines), r.hid, r.zc.at[i // lines], r.gacc)

        @pl.when(i < SWEEPS)
        def _():
            one.power_grad(jnp.maximum(SWEEPS - 1 - i, 0))

    @pl.when(is_owner(g))
    def _():
        add_chain(here, r.dlm, one.finish())

    mark_rows(r.wall, r.dlm, r.ep)
    c_a += go([remote(r.ep.at[:, theirs], r.er, r.s_a, 1, head=core)])
    grid_sums(r.gacc, r.dh, r.cotb, r.gtaps, r.gk)
    blocks = r.gk.shape[0] // 8

    def block(b):
        return r.gk.at[pl.ds(8 * b, 8)]

    def on_block_owner(inside, outside):
        pl.when(me < blocks)(inside)
        pl.when(me >= blocks)(outside)

    for b in range(blocks):

        @pl.when(me != b)
        def _():
            remote(block(b), r.gkr.at[me], r.s_k, 0, seq=b).start()

        @pl.when(me == b)
        def _():
            r.gkr[pl.ds(me, 1)] = block(b)[...][None]

    got(c_a[1:2])
    r.es[...] = (r.ep[:, mine].astype(f32) + r.er[...].astype(f32)).astype(bf16)
    c_e = fan(r.erv.at[pl.ds(0, size - 1)], r.s_e, 0, [(r.es.at[marks(i)], r.erv.at[g]) for i in range(1, size)])
    r.erv[pl.ds(g, 1)] = r.es[row][None]
    input_rows(r.wall, r.dp, r.dn)
    c_a += go([remote(r.dn, r.dnr, r.s_a, 2, head=core)])
    weight_grad(3, *weights)
    weight_grad(2, *weights)
    got(c_e)
    total = r.erv[0].astype(f32)
    for d in range(1, size):
        total = total + r.erv[d].astype(f32)
    r.em[...] = total.astype(bf16)
    r.eall[row, mine] = r.em[...]
    c_f = fan(r.eall.at[cube_marks, mine], r.s_f, 0, [(r.em, r.eall.at[row, mine])] * (size - 1))
    send_weights(3)
    send_weights(2)
    for j in range(2):
        weight_grad(j, *weights)
        send_weights(j)
    r.wrv[pl.ds(g, 1), 0] = r.wpart[:, wrow(me)][None]
    r.wrv[pl.ds(g, 1), 1] = r.wpart[:, wrow(partner)][None]

    got(c_f)
    c_a += go([remote(r.eall.at[:, mine], r.eall.at[:, mine], r.s_a, 3, head=core)])
    everything = r.gkr.at[pl.ds(0, n - 1)]

    @pl.when(me < blocks)
    def _():
        remote(everything, everything, r.s_k, 0, seq=partner).wait_recv()
        gsum = r.gkr[0]
        for d in range(1, n):
            gsum = gsum + r.gkr[d]
        r.gkm[...] = gsum
        here = pl.ds(pl.multiple_of(8 * me, 8), 8)
        r.gkall[here, mine] = gsum
        for i in range(1, n):
            remote(r.gkm, r.gkall.at[here, mine], r.s_m, 0, seq=far[i]).start()

    got(c_a[2:4])
    back = norm_back(n, g, count, other, r.xblk, r.dn, r.dnr, r.eall, r.gain, r.small)
    r.lnf[...] = back
    r.lns[...] = (r.lnf[:, mine] + r.dh[other]).astype(bf16)
    c_l = go([remote(r.lns, r.lnr.at[:, mine], r.s_l, 0, seq=partner)])
    got(c_p[1:2])
    r.gxf[half] = r.dhf[...] + norm_back(n, g, count, half, r.xblk, r.dn, r.dnr, r.eall, r.gain, r.small)
    for a in range(2):
        for b in range(4):
            r.smx[4 * a + b:4 * a + b + 1] = r.small[a:a + 1, 128 * b:128 * b + 128]
    c_s = [Many(r.smr.at[pl.ds(0, n - 1)], r.s_s, 0, seq=partner)]
    for i in range(1, n):
        c_s[0].add(r.smx, r.smr.at[me], seq=far[i])
    r.smr[pl.ds(me, 1)] = r.smx[...][None]

    got(c_z)
    grid_forward(n, count, other, r.hid, r.zhalo, r.kc, r.pbias, r.outh, r.zs, r.pad)
    c_l += go([remote(r.outh.at[other], r.outf.at[half, :, mine], r.s_l, 1, seq=partner)])
    grid_forward(n, count, half, r.hid, r.zhalo, r.kc, r.pbias, r.outh, r.zs, r.pad)
    r.outf[half, :, mine] = r.outh[half]
    got(c_l[0:1])
    c_l += go([remote(r.lnr.at[:, mine], r.lnr.at[:, mine], r.s_l, 2, head=core)])
    got(c_y)
    c_u = []
    for k in (1, 0):
        total = r.wrv[0, k].astype(f32)
        for d in range(1, size):
            total = total + r.wrv[d, k].astype(f32)
        if k == 1:
            r.wsum[...] = total.astype(bf16)
            c_u = go([remote(r.wsum, r.wone, r.s_u, 0, seq=partner)])

    def blocks_back(count):
        part = r.gkall.at[pl.ds(0, 8 * count), mine]
        return remote(part, part, r.s_m, 0, seq=partner)

    on_block_owner(blocks_back(blocks - 1).wait_recv, blocks_back(blocks).wait_recv)
    c_l += go([remote(r.gkall.at[:, mine], r.gkall.at[:, mine], r.s_l, 4, head=core)])
    got(c_s)
    acc = r.smr[0]
    for d in range(1, n):
        acc = acc + r.smr[d]
    r.sums[...] = acc
    got(c_l[1:2])
    c_l += go([remote(r.outf.at[:, :, mine], r.outf.at[:, :, mine], r.s_l, 3, head=core)])
    got(c_l[2:3])
    r.gxf[other] = r.lnr[...].astype(f32)
    got(c_u)
    r.gw[...] = total + r.wone[...].astype(f32)
    got(c_l[3:])

    sent(c_t + c_w + c_v + c_n + c_h + c_p + c_x + c_d + c_g + c_q + c_a + c_e + c_f + c_z + c_y + c_l + c_s + c_u)

    @pl.when(is_owner(g))
    def _():
        gave(r.blkb.at[pl.ds(0, 3)], r.s_b)
        gave(r.blkd.at[pl.ds(0, 3)], r.s_c)
        gave(r.resall.at[pl.ds(0, size - 1)], r.s_r)

    @pl.when(jnp.logical_not(is_owner(g)))
    def _():
        gave(r.blkb, r.s_b)
        gave(r.blkd, r.s_c)

    def blocks_left(count):
        part = r.gk.at[pl.ds(0, 8 * count)]
        return remote(part, part, r.s_k, 0, seq=partner)

    on_block_owner(blocks_left(blocks - 1).wait_send, blocks_left(blocks).wait_send)

    @pl.when(me < blocks)
    def _():
        remote(everything, everything, r.s_m, 0, seq=partner).wait_send()


def result_kernel(outf, gxf, gw, sums, gkall, out, gx, gwqkv, gwoutt, ggain, gbias, gtaps, gob, k7o, k5o, k3o, gpb):
    out[...] = outf[...]
    gx[...] = gxf[...]
    gwqkv[...] = gw[0:3]
    gwoutt[...] = gw[3]
    for i in range(4):
        ggain[:, 128 * i:128 * i + 128] = sums[i:i + 1]
        gbias[:, 128 * i:128 * i + 128] = sums[4 + i:5 + i]
    rows = gkall[51:55, my_half()]
    li, lt = iota((256, 33), 0), iota((256, 33), 1)
    spot = jnp.where(((li + lt) & 255) == 16, 1.0, 0.0).astype(bf16)
    parts = [mm(piece.astype(bf16), spot) for piece in split3(rows)]
    gtaps[...] = parts[0] + parts[1] + parts[2]
    gob[...] = gkall[49:50]
    gpb[...] = gkall[50:51]
    spill_kernels(gkall, k7o, k5o, k3o)


def half_of(full, axis):
    return lax.dynamic_slice_in_dim(full, lax.axis_index("head") * 256, 256, axis)


def swap(n, blocks):
    half, _, _ = place(n)
    theirs = lax.ppermute(jnp.where(half == 0, blocks[1], blocks[0]), "seq", [(i, (i + n // 2) % n) for i in range(n)])
    own = jnp.where(half == 0, blocks[0], blocks[1])
    return jnp.where(half == 0, jnp.stack([own, theirs]), jnp.stack([theirs, own]))


def half_sum(n, value):
    half, _, _ = place(n)
    pair = lax.psum(jnp.stack([jnp.where(half == s, value, 0.0) for s in range(2)]), "seq")
    return jnp.where(half == 0, pair[0], pair[1])


def half_max(n, value):
    half, _, _ = place(n)
    pair = lax.pmax(jnp.stack([jnp.where(half == s, value, -jnp.inf) for s in range(2)]), "seq")
    return jnp.where(half == 0, pair[0], pair[1])


def norm_kernel(n, cnt, xblk, gain, bias, normed, xp):
    half, g, _ = place(n)
    for b in range(2):
        normed[b] = norm_rows(xblk[b], gain[...], bias[...])
    xp[...] = segment_sums(n, g, cnt[half], normed)


def back_conv_kernel(n, cnt, cotb, halo, k7, k5, k3, dh, kc, zs, pad):
    half, _, _ = place(n)
    join_taps(kc, k7, k5, k3)
    for b in range(2):
        load_cot(n, b, cotb, *ring_ends(n, place(n)[1], b, halo), zs, pad)
        back_conv(n, cnt[half], b, cotb, zs, kc, dh)


def start_plain(n, counts, tok, cot, gain, bias, wqkv, woutt, k7, k5, k3, scratch):
    half, _, _ = place(n)
    rows = tok.shape[1]
    count = counts[half]
    xblk = swap(n, tok)
    normed, xp = call(
        functools.partial(norm_kernel, n), [sds((2, rows, 512), bf16), sds((MARKS, 256))], [SMEM] + [VMEM] * 3
    )(counts, xblk, gain, bias)
    low, high = edges(count, jnp.arange(MARKS, dtype=jnp.int32))
    xbar = (half_sum(n, xp) / (high - low).astype(f32)[:, None]).astype(bf16)
    xbar = lax.all_gather(xbar, "head", axis=1, tiled=True)
    wts = jnp.concatenate([wqkv, woutt[None]], axis=0)
    wall = lax.all_gather(wts, "seq", axis=1, tiled=True)
    cotb = half_of(swap(n, cot), 2)
    halo = half_ring(n, jnp.stack([cotb[:, :192], cotb[:, -192:]]))
    dh = call(functools.partial(back_conv_kernel, n), sds((2, rows, 256)), [SMEM] + [VMEM] * 5, scratch)(
        counts, cotb, halo, k7, k5, k3
    )
    dhrb = lax.all_gather(dh.astype(bf16), "head", axis=2, tiled=True)
    return xblk, normed, xbar, wall, cotb, halo, dh, dhrb


def half_ring(n, hal):
    size = n // 2
    up = [(i, i // size * size + (i + 1) % size) for i in range(n)]
    return jnp.stack([lax.ppermute(hal[1], "seq", up), lax.ppermute(hal[0], "seq", [(j, i) for i, j in up])])


def three_rows(stat, first):
    return (stat[:, first:first + 1] + stat[:, first + 1:first + 2]) + stat[:, first + 2:first + 3]


def reduce_plain(n, blkb, blkd, halv, hald):
    _, g, _ = place(n)
    stat = blkb[:, 64:].astype(f32)
    top, total = three_rows(stat, 0), three_rows(stat, 3)
    best = half_max(n, top)
    w = jnp.exp(top - best)
    total = half_sum(n, total * w)
    value = half_sum(n, blkb[:, 0:64].astype(f32) * w)
    dct = half_sum(n, blkd.astype(f32)).astype(bf16)
    stat = jnp.concatenate(split3(best) + split3(total) + [jnp.zeros((4, 10, MARKS), f32)], axis=1)
    whole = jnp.concatenate([value, stat], axis=1).astype(bf16)
    h = head_of(g)
    recvb, recvd = lax.dynamic_slice_in_dim(whole, h, 1, 0), lax.dynamic_slice_in_dim(dct, h, 1, 0)
    return recvb, recvd, half_ring(n, halv), half_ring(n, hald)


def spread_plain(n, res):
    _, g, _ = place(n)
    held = ((jnp.arange(4) == head_of(g)) & is_owner(g))[:, None, None]
    return half_sum(n, jnp.where(held, res[None].astype(f32), 0.0)).astype(bf16)


def scores_kernel(n, cnt, normed, xbar, wall, dhrb, qt, kt, vt, qlt, klt, dot, wback, a1, e3, blkb, blkd, halv, hald, wt):
    half, _, _ = place(n)
    count = cnt[half]
    wback[...] = wall[3].T
    project(n, count, normed, wall, wt, qt, kt, vt)
    value_edges(n, count, normed, wall, halv)
    landmarks(xbar, wt, qlt, klt)
    key_scores(n, count, kt, qlt, vt, e3, blkb)
    query_scores(qt, klt, a1)
    out_grads(dhrb, wback, dot, hald)
    partial_dc(dot, a1, blkd)


CHAIN = ("res", "amat", "asp", "pcur", "ps", "ts", "xs", "ys", "ctf", "dctf", "ecur")


def chain_kernel(n, recvb, recvd, qlt, klt, dqz, *refs):
    _, g, _ = place(n)
    here = head_rows(head_of(g))
    dqz[...] = jnp.zeros_like(dqz)
    refs[0][...] = jnp.zeros_like(refs[0])

    @pl.when(is_owner(g))
    def _():
        one = Chain(qlt.at[here], klt.at[here], Refs(("recvb", "recvd") + CHAIN, (recvb, recvd) + refs))
        one.begin()
        for k in range(SWEEPS):
            one.sweep(k)
        one.forward()
        one.backward()
        one.r.ecur[...] = jnp.zeros_like(one.r.ecur)
        for k in range(SWEEPS):
            one.power_grad(SWEEPS - 1 - k)
        dqz[0], dqz[1] = one.finish()


def grads_kernel(n, cnt, normed, xbar, wall, wback, dhrb, qt, kt, vt, qlt, klt, dot, a1, e3, blkb, resall, rhv, rhd, taps,
                 dqz, po, dn, ep, wpart, gtaps, tm, th, hv, hdt, hvr, vr, conv, dconv, gsum, att, dp, dlm):
    half, _, _ = place(n)
    make_bands(taps, normed.shape[1], tm, th)
    value_conv(n, vt, rhv, tm, th, hv, vr, hvr, conv)
    value_conv_back(n, dot, rhd, tm, th, hdt, vr, hvr, dconv, gsum, gtaps)
    attend(resall, a1, conv, att)
    output_rows(att, wback, po)
    score_grads(n, cnt[half], qt, kt, vt, qlt, klt, dot, a1, e3, blkb, resall, dconv, dp, dlm)
    add_chain(head_rows(head_of(place(n)[1])), dlm, dqz)
    mark_rows(wall, dlm, ep)
    input_rows(wall, dp, dn)
    for j in range(4):
        weight_grad(j, normed, xbar, dhrb, att, dp, dlm, wpart)


def hidden_kernel(n, cnt, x, obias, part, hid, z):
    half, _, _ = place(n)
    for b in range(2):
        z[b] = hidden_rows(n, cnt[half], b, x, obias, part[b], hid).astype(bf16)


def final_kernel(n, cnt, hid, halo, cotb, chalo, k7, k5, k3, pbias, xblk, dn, dnr, eall, gain, dh, gtaps,
                 outh, lnb, gk, small, kc, zs, pad, gacc):
    half, g, _ = place(n)
    join_taps(kc, k7, k5, k3)
    gacc[...] = jnp.zeros_like(gacc)
    small[...] = jnp.zeros_like(small)
    for b in range(2):
        grid_forward(n, cnt[half], b, hid, halo, kc, pbias, outh, zs, pad)
        load_cot(n, b, cotb, *ring_ends(n, g, b, chalo), zs, pad)
        pl.loop(0, hid.shape[1] // GRID_W)(lambda i: kernel_grads(n, cnt[half], b, i, hid, zs, gacc))
    grid_sums(gacc, dh, cotb, gtaps, gk)
    for b in range(2):
        lnb[b] = norm_back(n, g, cnt[half], b, xblk, dn, dnr, eall, gain, small)


def late_plain(n, counts, cotb, chalo, xblk, dh, po, ep, dn, wpart, gtaps, gain, obias, pbias, k7, k5, k3, scratch):
    rows = xblk.shape[1]
    part = half_of(lax.psum(po.astype(f32), "head").astype(bf16), 2)
    hid, z = call(functools.partial(hidden_kernel, n), [sds((2, rows, 256)), sds((2, rows, 256), bf16)], [SMEM] + [VMEM] * 3)(
        counts, xblk, obias, part
    )
    halo = half_ring(n, jnp.stack([z[:, :192], z[:, -192:]]))
    dnr = lax.ppermute(dn, "head", [(0, 1), (1, 0)])
    eall = half_sum(n, lax.psum(ep.astype(f32), "head")).astype(bf16)
    outh, lnb, gk, small = call(
        functools.partial(final_kernel, n),
        [sds((2, rows, 256), bf16), sds((2, rows, 512)), sds((56, 256)), sds((8, 512))],
        [SMEM] + [VMEM] * 15,
        scratch + [pltpu.VMEM((49, 8, 256), f32)],
    )(counts, hid, halo, cotb, chalo, k7, k5, k3, pbias, xblk, dn, dnr, eall, gain, dh, gtaps)
    out = swap(n, lax.all_gather(outh, "head", axis=2, tiled=True))
    gx = swap(n, lax.all_gather(dh, "head", axis=2, tiled=True) + lnb)
    gw = lax.psum_scatter(wpart.astype(f32), "seq", scatter_dimension=1, tiled=True)
    gk, small = lax.psum((gk, small), "seq")
    gkall = lax.all_gather(gk, "head", axis=1, tiled=True)
    return out, gx, gw, small[0:2].reshape(8, 128), gkall


def layer_plain(n, counts, tok, cot, gain, bias, wqkv, woutt, taps, obias, pbias, k7, k5, k3):
    rows = tok.shape[1]
    made = layer_buffers(n, rows, wqkv.shape[1])

    def out(*names):
        return [sds(*made[name]) for name in names]

    def tmp(*names):
        return [pltpu.VMEM(*made[name]) for name in names]

    conv_tmp = tmp("kc", "zs", "pad")
    xblk, normed, xbar, wall, cotb, chalo, dh, dhrb = start_plain(
        n, counts, tok, cot, gain, bias, wqkv, woutt, k7, k5, k3, conv_tmp
    )
    qt, kt, vt, qlt, klt, dot, wback, a1, e3, blkb, blkd, halv, hald = call(
        functools.partial(scores_kernel, n),
        out("qt", "kt", "vt", "qlt", "klt", "dot", "wback", "a1", "e3", "blkb", "blkd", "halv", "hald"),
        [SMEM] + [VMEM] * 4,
        tmp("wt"),
    )(counts, normed, xbar, wall, dhrb)
    recvb, recvd, rhv, rhd = reduce_plain(n, blkb, blkd, halv, hald)
    dqz, res = call(
        functools.partial(chain_kernel, n), [sds((2, 64, MARKS)), sds((BLK, MARKS), bf16)], [VMEM] * 4, tmp(*CHAIN[1:])
    )(recvb, recvd, qlt, klt)
    resall = spread_plain(n, res)
    po, dn, ep, wpart, gtaps = call(
        functools.partial(grads_kernel, n),
        out("po", "dn", "ep", "wpart", "gtaps"),
        [SMEM] + [VMEM] * 19,
        tmp("tm", "th", "hv", "hdt", "hvr", "vr", "conv", "dconv", "gsum", "att", "dp", "dlm"),
    )(counts, normed, xbar, wall, wback, dhrb, qt, kt, vt, qlt, klt, dot, a1, e3, blkb, resall, rhv, rhd, taps, dqz)
    return late_plain(
        n, counts, cotb, chalo, xblk, dh, po, ep, dn, wpart, gtaps, gain, obias, pbias, k7, k5, k3, conv_tmp
    )


def shards(n, tokens, counts, ln_gain, ln_bias, w_qkv, conv_taps, w_out, out_bias, kernel7, kernel5, kernel3, ppeg_bias, cotangent):
    rows, wr = tokens.shape[1], w_qkv.shape[1]
    gain, bias, obias, pbias = (v[None, :] for v in (ln_gain, ln_bias, out_bias, ppeg_bias))
    args = (counts, tokens, cotangent, gain, bias, w_qkv, w_out.T, conv_taps, obias, pbias, kernel7, kernel5, kernel3)
    if n == 16:
        results, buffers = layer_results(n, rows, wr), layer_buffers(n, rows, wr)
        names = INPUTS + tuple(results) + tuple(buffers) + tuple(SEMS)
        made = call(
            functools.partial(layer_kernel, n, names),
            [sds(*v) for v in results.values()],
            [SMEM] + [VMEM] * 12,
            [pltpu.VMEM(*v) for v in buffers.values()] + [DMA((2, k)) for k in SEMS.values()],
            cid=0,
            vmem=60,
        )(*args)
    else:
        made = layer_plain(n, *args)
    vec = sds((1, 512))
    out, gx, gwqkv, gwoutt, ggain, gbias, gtaps, gob, k7o, k5o, k3o, gpb = call(
        result_kernel,
        [sds((2, rows, 512), bf16), sds((2, rows, 512)), sds((3, wr, 256)), sds((wr, 256)), vec, vec, sds((4, 33)), vec,
         sds((7, 7, 512)), sds((5, 5, 512)), sds((3, 3, 512)), vec],
        [VMEM] * 5,
    )(*made)
    return out, gx, ggain[0], gbias[0], gwqkv, gtaps, gwoutt.T, gob[0], k7o, k5o, k3o, gpb[0]


def solution(mesh):
    rows, cols = P(None, "seq", None), P(None, "seq", "head")
    return jax.shard_map(
        functools.partial(shards, mesh.shape["seq"]),
        mesh=mesh,
        in_specs=(rows, P(), P(), P(), cols, P("head", None), P("head", "seq"), P(), P(), P(), P(), P(), rows),
        out_specs=(rows, rows, P(), P(), cols, P("head", None), P("head", "seq"), P(), P(), P(), P(), P()),
        check_vma=False,
    )
```

```python
import functools

import jax
import jax.numpy as jnp
from jax import lax
from jax.experimental import pallas as pl
from jax.experimental.pallas import tpu as pltpu
from jax.sharding import PartitionSpec as P

MESH = pl.DeviceIdType.MESH
GRID_W = 64
MARKS = 256
SWEEPS = 6
EPSILON = 1e-05
f32, bf16 = jnp.float32, jnp.bfloat16
VMEM = pl.BlockSpec(memory_space=pltpu.VMEM)
SMEM = pl.BlockSpec(memory_space=pltpu.SMEM)
DMA = pltpu.SemaphoreType.DMA
SCALE = 64 ** -0.5
PART = 80


def sds(shape, dtype=f32):
    return jax.ShapeDtypeStruct(shape, dtype)


def call(kernel, outs, specs, scratch=(), cid=None, vmem=56):
    extra = {} if cid is None else dict(collective_id=cid, has_side_effects=True)
    return pl.pallas_call(
        kernel,
        out_shape=outs,
        in_specs=specs,
        out_specs=jax.tree.map(lambda _: VMEM, outs),
        scratch_shapes=list(scratch),
        compiler_params=pltpu.CompilerParams(vmem_limit_bytes=vmem * 2**20, **extra),
    )


def mm(left, right, cl=1, cr=0):
    return lax.dot_general(left, right, (((cl,), (cr,)), ((), ())), preferred_element_type=f32)


def split(value):
    high = value.astype(bf16)
    return high, (value - high.astype(f32)).astype(bf16)


def split3(row):
    high = row.astype(bf16).astype(f32)
    rest = row - high
    mid = rest.astype(bf16).astype(f32)
    return [high, mid, rest - mid]


def mm3(left, right, cl=1, cr=0):
    (lh, ll), (rh, rl) = left, right
    return mm(lh, rh, cl, cr) + (mm(lh, rl, cl, cr) + mm(ll, rh, cl, cr))


def iota(shape, dim):
    return lax.broadcasted_iota(jnp.int32, shape, dim)


def edges(count, marks):
    return (marks * count + (MARKS - 1)) >> 8, ((marks + 1) * count + (MARKS - 1)) >> 8


def member(count, start, rows):
    low, high = edges(count, iota((MARKS, rows), 0))
    slot = iota((MARKS, rows), 1) + start
    return jnp.where((slot >= low) & (slot < high), 1.0, 0.0).astype(bf16)

OWNERS = (0, 3, 5, 6)


def place(n):
    me = lax.axis_index("seq")
    return me // (n // 2), lax.rem(me, n // 2), lax.rem(me + n // 2, n)


def head_of(g):
    return jnp.where(g == 0, 0, jnp.where(g == 3, 1, jnp.where(g == 5, 2, 3)))


def is_owner(g):
    return (g == 0) | (g == 3) | (g == 5) | (g == 6)


def my_half():
    return pl.ds(pl.multiple_of(lax.axis_index("head") * 256, 256), 256)


def block_start(n, g, b, rows):
    return (g + b * (n // 2)) * rows


def places(n, g, rows, shape, dim):
    at = iota(shape, dim)
    return at + g * rows + jnp.where(at >= rows, (n // 2 - 1) * rows, 0)


CHUNK = 64


def norm_rows(x, gain, bias, out):
    @pl.loop(0, x.shape[0] // CHUNK)
    def _(i):
        here = pl.ds(pl.multiple_of(i * CHUNK, CHUNK), CHUNK)
        v = x[here].astype(f32)
        vc = v - jnp.mean(v, axis=-1, keepdims=True)
        inv = lax.rsqrt(jnp.mean(vc * vc, axis=-1, keepdims=True) + EPSILON)
        out[here] = (vc * inv * gain[...] + bias[...]).astype(bf16)


def segment_sums(n, g, count, normed):
    rows = normed.shape[1]
    mine = my_half()
    return sum(mm(member(count, block_start(n, g, b, rows), rows), normed[b, :, mine]) for b in range(2))


def join_taps(kc, k7, k5, k3):
    mine = my_half()
    kc[...] = jnp.zeros_like(kc)
    for a in range(7):
        kc[a, 0:7] = k7[a, :, mine]
    for a in range(5):
        kc[a + 1, 1:6] = kc[a + 1, 1:6] + k5[a, :, mine]
    for a in range(3):
        kc[a + 2, 2:5] = kc[a + 2, 2:5] + k3[a, :, mine]


def load_grid(zs, pad, body, top, bottom):
    grid = body.shape[0] // GRID_W
    side = jnp.zeros((grid + 6, 8, 256), f32)
    pad[:, 0:8], pad[:, 8 + GRID_W:16 + GRID_W] = side, side
    pad[0:3, 8:8 + GRID_W] = top.reshape(3, GRID_W, 256)
    pad[3:3 + grid, 8:8 + GRID_W] = body.reshape(grid, GRID_W, 256)
    pad[3 + grid:6 + grid, 8:8 + GRID_W] = bottom.reshape(3, GRID_W, 256)

    @pl.loop(0, grid + 6)
    def _(i):
        for b in range(7):
            zs[b, i] = pad[i, 5 + b:5 + b + GRID_W, :]


def conv_row(zs, kc, i, flip):
    acc = jnp.zeros((GRID_W, 256), f32)
    for a in range(7):
        for b in range(7):
            ka, kb = (6 - a, 6 - b) if flip else (a, b)
            acc = acc + kc[ka, kb:kb + 1, :] * zs[b, i + a]
    return acc


def load_cot(n, b, cotb, top, bottom, zs, pad):
    at = block_start(n, place(n)[1], b, cotb.shape[1])
    top = jnp.where(at > 0, top.astype(f32), 0.0)
    bottom = jnp.where(at < (n - 1) * cotb.shape[1], bottom.astype(f32), 0.0)
    load_grid(zs, pad, cotb[b].astype(f32), top, bottom)


def back_conv(n, count, b, cotb, zs, kc, dh):
    _, g, _ = place(n)
    rows = cotb.shape[1]

    @pl.loop(0, rows // GRID_W)
    def _(i):
        acc = conv_row(zs, kc, i, True)
        here = pl.ds(pl.multiple_of(i * GRID_W, GRID_W), GRID_W)
        slot = iota((GRID_W, 256), 0) + (block_start(n, g, b, rows) + i * GRID_W)
        dh[b, here] = cotb[b, here].astype(f32) + jnp.where(slot < count, acc, 0.0)


def kernel_grads(n, count, b, i, hid, zs, gacc):
    _, g, _ = place(n)
    rows = hid.shape[1]
    here = pl.ds(pl.multiple_of(i * GRID_W, GRID_W), GRID_W)
    slot = iota((GRID_W, 256), 0) + (block_start(n, g, b, rows) + i * GRID_W)
    z = jnp.where(slot < count, hid[b, here], 0.0)
    for ka in range(7):
        for kb in range(7):
            part = (z * zs[6 - kb, i + 6 - ka]).reshape(GRID_W // 8, 8, 256)
            gacc[ka * 7 + kb] = gacc[ka * 7 + kb] + jnp.sum(part, axis=0)


def hidden_rows(n, count, b, x, obias, part, hid):
    _, g, _ = place(n)
    rows = x.shape[1]
    mine = my_half()
    hid[b] = x[b, :, mine].astype(f32) + part.astype(f32) + obias[:, mine]
    slot = iota((rows, 256), 0) + block_start(n, g, b, rows)
    return jnp.where(slot < count, hid[b], 0.0)


def ring_ends(n, g, b, recv):
    top = jnp.where(g > 0, recv[0, b].astype(f32), recv[0, 0].astype(f32) * b)
    bottom = jnp.where(g < n // 2 - 1, recv[1, b].astype(f32), recv[1, 1].astype(f32) * (1 - b))
    return top, bottom


def grid_forward(n, count, b, hid, halo, kc, pbias, outh, zs, pad):
    _, g, _ = place(n)
    rows = hid.shape[1]
    mine = my_half()
    slot = iota((rows, 256), 0) + block_start(n, g, b, rows)
    top, bottom = ring_ends(n, g, b, halo)
    load_grid(zs, pad, jnp.where(slot < count, hid[b], 0.0), top, bottom)

    @pl.loop(0, rows // GRID_W)
    def _(i):
        here = pl.ds(pl.multiple_of(i * GRID_W, GRID_W), GRID_W)
        acc = conv_row(zs, kc, i, False)
        outh[b, here] = (hid[b, here] + acc + pbias[:, mine]).astype(bf16)


def grid_sums(gacc, dh, cotb, gtaps, gk):
    for t in range(49):
        gk[t:t + 1] = jnp.sum(gacc[t], axis=0, keepdims=True)
    gk[49:50] = jnp.sum(dh[0], axis=0, keepdims=True) + jnp.sum(dh[1], axis=0, keepdims=True)
    g = cotb[0].astype(f32) + cotb[1].astype(f32)
    gk[50:51] = jnp.sum(g, axis=0, keepdims=True)
    gk[51:55] = gtaps[0:4]
    gk[55:56] = jnp.zeros((1, 256), f32)


def norm_back(n, g, count, b, x, dn, dnr, eall, gain, small, out):
    rows = x.shape[1]
    low, high = edges(count, iota((MARKS, 512), 0))
    e = (eall[...].astype(f32) / (high - low).astype(f32)).astype(bf16)
    mem = member(count, block_start(n, g, b, rows), rows)
    out[...] = mm(mem, e, 0, 0)

    @pl.loop(0, rows // CHUNK)
    def _(i):
        here = pl.ds(pl.multiple_of(i * CHUNK, CHUNK), CHUNK)
        total = (dn[b, here].astype(f32) + dnr[b, here].astype(f32)) + out[here]
        v = x[b, here].astype(f32)
        vc = v - jnp.mean(v, axis=-1, keepdims=True)
        inv = lax.rsqrt(jnp.mean(vc * vc, axis=-1, keepdims=True) + EPSILON)
        vh = vc * inv
        dg = total * gain[...]
        m1 = jnp.mean(dg, axis=-1, keepdims=True)
        m2 = jnp.mean(dg * vh, axis=-1, keepdims=True)
        small[0:1] = small[0:1] + jnp.sum(total * vh, axis=0, keepdims=True)
        small[1:2] = small[1:2] + jnp.sum(total, axis=0, keepdims=True)
        out[here] = (dg - m1 - vh * m2) * inv


def spill_kernels(gkall, k7o, k5o, k3o):
    for a in range(7):
        k7o[a] = gkall[7 * a:7 * a + 7]
    for a in range(5):
        k5o[a] = gkall[7 * a + 8:7 * a + 13]
    for a in range(3):
        k3o[a] = gkall[7 * a + 16:7 * a + 19]


def hail(peers):
    sem = pltpu.get_barrier_semaphore()
    for peer in peers:
        pl.semaphore_signal(sem, inc=1, device_id={"seq": peer}, device_id_type=MESH)
    pl.semaphore_signal(sem, inc=1, device_id={"head": 1 - lax.axis_index("head")}, device_id_type=MESH)


def heard(peers):
    pl.semaphore_wait(pltpu.get_barrier_semaphore(), len(peers) + 1)


def everyone(n):
    me = lax.axis_index("seq")
    return [lax.rem(me + i, n) for i in range(n)]


def cube(n):
    half, g, _ = place(n)
    return [half * (n // 2) + lax.rem(g + i, n // 2) for i in range(n // 2)]


def remote(src, dst, sems, i, **where):
    return pltpu.make_async_remote_copy(
        src_ref=src, dst_ref=dst, send_sem=sems.at[0, i], recv_sem=sems.at[1, i], device_id=where, device_id_type=MESH
    )


def go(copies):
    for c in copies:
        c.start()
    return copies


def got(copies):
    for c in copies:
        c.wait_recv()


def sent(copies):
    for c in copies:
        c.wait_send()


def matrix(wall, j):
    n, _, wr, cols = wall.shape
    return wall[:, j].reshape(n * wr, cols)


def project(n, count, normed, wall, wt, qt, kt, vt):
    _, g, _ = place(n)
    for j in range(3):
        wt[j] = matrix(wall, j).T
    rows = normed.shape[1]
    nr = normed[...].reshape(2 * rows, 512)
    qt[...] = mm(wt[0], nr, 1, 1).astype(bf16)
    kt[...] = mm(wt[1], nr, 1, 1).astype(bf16)
    slots = places(n, g, rows, (256, 2 * rows), 1)
    vt[...] = jnp.where(slots < count, mm(wt[2], nr, 1, 1), 0.0).astype(bf16)


def value_edges(n, count, normed, wall, halv):
    _, g, _ = place(n)
    rows = normed.shape[1]
    for b in range(2):
        for side, first in ((0, 0), (1, rows - 16)):
            slot = iota((16, 256), 0) + (block_start(n, g, b, rows) + first)
            v = mm(normed[b, first:first + 16], matrix(wall, 2))
            halv[side, b] = jnp.where(slot < count, v, 0.0).astype(bf16)


def landmarks(xbar, wt, qlt, klt):
    qlt[...] = mm(wt[0], xbar[...], 1, 1).astype(bf16)
    klt[...] = mm(wt[1], xbar[...], 1, 1).astype(bf16)


def head_rows(h):
    return pl.ds(pl.multiple_of(h * 64, 64), 64)


def key_scores(n, count, kt, qlt, vt, e3, blkb):
    _, g, _ = place(n)
    wide = kt.shape[1]

    @pl.loop(0, 4, unroll=4)
    def _(h):
        here = head_rows(h)
        ok = places(n, g, wide // 2, (wide, MARKS), 0) < count
        s3 = jnp.where(ok, mm(kt[here] * SCALE, qlt[here], 0, 0), -1e30)
        top = jnp.max(s3, axis=0, keepdims=True)
        e = jnp.where(ok, jnp.exp(s3 - top), 0.0)
        total = jnp.sum(e, axis=0, keepdims=True)
        er = e.astype(bf16)
        e3[h] = er
        blkb[h, 0:64] = mm(vt[here], er).astype(bf16)
        stat = jnp.concatenate(split3(top) + split3(total) + [jnp.zeros((10, MARKS), f32)], axis=0)
        blkb[h, 64:80] = stat.astype(bf16)


def query_scores(qt, klt, a1):
    @pl.loop(0, 4, unroll=4)
    def _(h):
        here = head_rows(h)
        s1 = mm(klt[here] * SCALE, qt[here], 0, 0)
        e1 = jnp.exp(s1 - jnp.max(s1, axis=0, keepdims=True))
        a1[h] = (e1 / jnp.sum(e1, axis=0, keepdims=True)).astype(bf16)


def out_grads(dhrb, wback, dot, hald):
    rows = dhrb.shape[1]
    dot[...] = mm(wback[...], dhrb[...].reshape(2 * rows, 512), 1, 1).astype(bf16)
    for b in range(2):
        for side, first in ((0, 0), (1, rows - 16)):
            hald[side, b] = mm(dhrb[b, first:first + 16], wback[...], 1, 1).astype(bf16)


def partial_dc(dot, a1, blkd):
    @pl.loop(0, 4, unroll=4)
    def _(h):
        blkd[h] = mm(dot[head_rows(h)], a1[h], 1, 1).astype(bf16)


def three(stat, first):
    return (stat[first:first + 1] + stat[first + 1:first + 2]) + stat[first + 2:first + 3]


class Chain:
    def __init__(self, ql, kl, r):
        self.ql, self.kl, self.r = ql, kl, r

    def begin(self):
        r = self.r
        s2 = mm(self.ql[...] * SCALE, self.kl[...], 0, 0)
        e2 = jnp.exp(s2 - jnp.max(s2, axis=1, keepdims=True))
        a = e2 / jnp.sum(e2, axis=1, keepdims=True)
        r.amat[...] = a
        asp = split(a)
        r.asp[0], r.asp[1] = asp
        inv = self.sums()[4]
        r.pcur[...] = mm3(asp, asp, 1, 1) * inv

    def sums(self):
        a = self.r.amat[...]
        cs, rs = jnp.sum(a, axis=0, keepdims=True), jnp.sum(a, axis=1, keepdims=True)
        cm, rm = jnp.max(cs, axis=1, keepdims=True), jnp.max(rs, axis=0, keepdims=True)
        return cs, rs, cm, rm, 1.0 / (cm * rm)

    def sweep(self, k):
        r = self.r
        p = r.pcur[...]
        psp = split(p)
        t = mm3(psp, psp)
        tsp = split(t)
        r.ps[k, 0], r.ps[k, 1] = psp
        r.ts[k, 0], r.ts[k, 1] = tsp
        r.pcur[...] = 0.25 * (13.0 * p - 15.0 * t + mm3(tsp, split(7.0 * p - t)))

    def powers(self, k):
        r = self.r
        return (r.ps[k, 0], r.ps[k, 1]), (r.ts[k, 0], r.ts[k, 1])

    def apply(self, x, k):
        psp, tsp = self.powers(k)
        xt = mm3(split(x), tsp)
        return 0.25 * (13.0 * x + 7.0 * xt - mm3(split(15.0 * x + xt), psp))

    def forward(self):
        r = self.r
        parts = r.recvb.shape[0]
        tops = [three(r.recvb[d, 64:80].astype(f32), 0) for d in range(parts)]
        top = functools.reduce(jnp.maximum, tops)
        total, value = 0.0, 0.0
        for d in range(parts):
            w = jnp.exp(tops[d] - top)
            total = total + three(r.recvb[d, 64:80].astype(f32), 3) * w
            value = value + r.recvb[d, 0:64].astype(f32) * w
        value = value / total
        r.xs[0] = value

        @pl.loop(0, SWEEPS)
        def _(k):
            r.xs[k + 1] = self.apply(r.xs[k], k)

        ct = mm3(split(r.xs[SWEEPS]), (r.asp[0], r.asp[1])) * self.sums()[4]
        r.res[0, 0:64] = ct.astype(bf16)
        stat = split3(top) + split3(total) + [jnp.zeros((10, MARKS), f32)]
        r.res[0, 64:80] = jnp.concatenate(stat, axis=0).astype(bf16)
        r.ctf[...] = ct

    def backward(self):
        r = self.r
        dct = r.recvd[0].astype(f32)
        for d in range(1, r.recvd.shape[0]):
            dct = dct + r.recvd[d].astype(f32)
        r.dctf[...] = dct
        r.ys[SWEEPS] = mm3(split(dct), (r.asp[0], r.asp[1]), 1, 1) * self.sums()[4]

        @pl.loop(0, SWEEPS)
        def _(i):
            r.ys[SWEEPS - 1 - i] = self.apply(r.ys[SWEEPS - i], SWEEPS - 1 - i)

        dbr = r.ys[0].astype(bf16)
        r.res[1, 0:64] = dbr
        rt = jnp.sum(dbr.astype(f32) * r.xs[0], axis=0, keepdims=True)
        r.res[1, 64:80] = jnp.concatenate(split3(rt) + [jnp.zeros((13, MARKS), f32)], axis=0).astype(bf16)

    def power_grad(self, k):
        r = self.r
        psp, tsp = self.powers(k)
        outer = mm3(split(r.ys[k + 1]), split(r.xs[k]), 0, 0) * 0.125
        d = outer + outer.T
        eq = 0.25 * r.ecur[...]
        pd = mm3(psp, split(d))
        pe = mm3(psp, split(eq))
        new = 13.0 * eq - 15.0 * d + mm3(split(7.0 * pe - pd), psp)
        left = 7.0 * pd - 15.0 * pe + mm3(tsp, split(7.0 * eq - d - (pe + pe.T)))
        r.ecur[...] = new + (left + left.T)

    def finish(self):
        r = self.r
        ql, kl, a, dct, e = self.ql[...], self.kl[...], r.amat[...], r.dctf[...], r.ecur[...]
        cs, rs, cm, rm, inv = self.sums()
        grad = mm3(split(r.xs[SWEEPS]), split(dct), 0, 0) * inv + mm3(split(e), (r.asp[0], r.asp[1])) * (2.0 * inv)
        p0 = r.ps[0, 0].astype(f32) + r.ps[0, 1].astype(f32)
        slope = jnp.sum(jnp.sum(dct * r.ctf[...], axis=0, keepdims=True), axis=1, keepdims=True)
        slope = -inv * (slope + jnp.sum(jnp.sum(e * p0, axis=0, keepdims=True), axis=1, keepdims=True))
        eqc, eqr = jnp.where(cs == cm, 1.0, 0.0), jnp.where(rs == rm, 1.0, 0.0)
        grad = grad + (slope * rm) * (eqc / jnp.sum(eqc, axis=1, keepdims=True))
        grad = grad + (slope * cm) * (eqr / jnp.sum(eqr, axis=0, keepdims=True))
        dsc = a * (grad - jnp.sum(a * grad, axis=1, keepdims=True)) * SCALE
        dh, dl = split(dsc)
        return mm(kl, dh, 1, 1) + mm(kl, dl, 1, 1), mm(ql, dh) + mm(ql, dl)


def add_chain(here, dlm, grads):
    for j in range(2):
        dlm[j, here] = (dlm[j, here].astype(f32) + grads[j]).astype(bf16)


def band(base, shift, rows):
    wide = jnp.broadcast_to(base, (rows, 256))
    return pltpu.roll(wide, shift, 1, stride=1, stride_axis=0)


def diagonals(g, shift):
    return jnp.sum(pltpu.roll(g, shift, 1, stride=1, stride_axis=0), axis=0, keepdims=True)


def make_bands(taps, rows, base, tm, th):
    pi, pj = iota((rows, rows), 0), iota((rows, rows), 1)
    inside = (pi - pj <= 16) & (pj - pi <= 16)
    hi, hj = iota((32, rows), 0), iota((32, rows), 1)
    far = jnp.where(hi < 16, hi - hj, hj - hi - (rows - 32)) >= 0
    ti, tl = iota((33, 256), 0), iota((33, 256), 1)
    spots = [jnp.where(((ti + tl if f == 0 else tl - ti + 32) & 255) == 16, 1.0, 0.0).astype(bf16) for f in range(2)]
    pieces = [piece.astype(bf16) for piece in split3(taps[...])]
    for f in range(2):
        lines = mm(pieces[0], spots[f]) + mm(pieces[1], spots[f]) + mm(pieces[2], spots[f])
        for h in range(4):
            base[4 * f + h] = jnp.broadcast_to(lines[h:h + 1, :], (8, 256))

    @pl.loop(0, 8)
    def _(i):
        f, h = i // 4, lax.rem(i, 4)
        line = base[i, 0:1]
        tm[f, h, 0], tm[f, h, 1] = split(jnp.where(inside, band(line, 0, rows), 0.0))
        both = jnp.concatenate([band(line, 240, 16), band(line, 0, 16)], axis=0)
        th[f, h, 0], th[f, h, 1] = split(jnp.where(far, both, 0.0))


def value_conv(n, vt, recvv, tm, th, hv, vr, hvr, conv):
    _, g, _ = place(n)
    rows = vt.shape[1] // 2
    pi, pj = iota((rows, rows), 0), iota((rows, rows), 1)
    mirror = jnp.where(pi + pj == rows - 1, 1.0, 0.0).astype(bf16)
    si, sj = iota((32, 32), 0), iota((32, 32), 1)
    mirror32 = jnp.where(si + sj == jnp.where(si < 16, 15, 47), 1.0, 0.0).astype(bf16)
    for b in range(2):
        part = slice(b * rows, (b + 1) * rows)
        hv[b] = jnp.concatenate(ring_ends(n, g, b, recvv), axis=0).T.astype(bf16)
        vr[b] = mm(vt[:, part], mirror).astype(bf16)
        hvr[b] = mm(hv[b], mirror32).astype(bf16)

        @pl.loop(0, 4, unroll=4)
        def _(h):
            here = head_rows(h)
            v, vh = vt[here, part], hv[b, here]
            conv[here, part] = mm(v, tm[0, h, 0]) + mm(v, tm[0, h, 1]) + mm(vh, th[0, h, 0]) + mm(vh, th[0, h, 1])


def value_conv_back(n, dot, recvd, tm, th, hd, vr, hvr, dconv, gsum, gtaps):
    _, g, _ = place(n)
    rows = dot.shape[1] // 2
    pi, pj = iota((rows, rows), 0), iota((rows, rows), 1)
    hi, hj = iota((32, rows), 0), iota((32, rows), 1)
    near = (pi + pj >= rows - 17) & (pi + pj <= rows + 15)
    beyond = jnp.where(hi < 16, 15 - hi - hj, hi + hj - (rows + 15)) >= 0
    for b in range(2):
        hd[b] = jnp.concatenate(ring_ends(n, g, b, recvd), axis=0).T.astype(bf16)

    @pl.loop(0, 4, unroll=4)
    def _(h):
        here = head_rows(h)
        s, sh = 0.0, 0.0
        for b in range(2):
            part = slice(b * rows, (b + 1) * rows)
            d, dh = dot[here, part], hd[b, here]
            dconv[here, part] = mm(d, tm[1, h, 0]) + mm(d, tm[1, h, 1]) + mm(dh, th[1, h, 0]) + mm(dh, th[1, h, 1])
            s = s + mm(vr[b, here], d, 0, 0)
            sh = sh + mm(hvr[b, here], d, 0, 0)
        s, sh = jnp.where(near, s, 0.0), jnp.where(beyond, sh, 0.0)
        gsum[h] = jnp.broadcast_to(diagonals(s, 1) + diagonals(sh[0:16], 1) + diagonals(sh[16:32], 241), (8, 256))

    for h in range(4):
        gtaps[h:h + 1, :] = gsum[h, 0:1]
    gtaps[4:8, :] = jnp.zeros((4, 256), f32)


def attend(res, a1, conv, att):
    @pl.loop(0, 4, unroll=4)
    def _(h):
        here = head_rows(h)
        att[here] = (mm(res[0, h, 0:64], a1[h]) + conv[here]).astype(bf16)


def score_grads(n, count, qt, kt, vt, qlt, klt, dot, a1, e3, blkb, res, dconv, dp, dlm):
    _, g, _ = place(n)
    wide = qt.shape[1]
    slots = places(n, g, wide // 2, (64, wide), 1)

    @pl.loop(0, 4, unroll=4)
    def _(h):
        here = head_rows(h)
        ct, dbt = res[0, h, 0:64], res[1, h, 0:64]
        stat = res[0, h, 64:80].astype(f32)
        own = three(blkb[h, 64:80].astype(f32), 0)
        factor = jnp.exp(own - three(stat, 0)) / three(stat, 3)
        rt = three(res[1, h, 64:80].astype(f32), 0)
        do, v = dot[here], vt[here]
        a = a1[h].astype(f32)
        da = mm(ct, do, 0, 0)
        d1 = (a * (da - jnp.sum(a * da, axis=0, keepdims=True))).astype(bf16)
        dp[0, here] = mm(klt[here] * SCALE, d1).astype(bf16)
        dlm[1, here] = mm(qt[here] * SCALE, d1, 1, 1).astype(bf16)
        a3 = e3[h].astype(f32) * factor
        d3 = (a3 * (mm(v, dbt, 0, 0) - rt)).astype(bf16)
        dlm[0, here] = mm(kt[here] * SCALE, d3).astype(bf16)
        dp[1, here] = mm(qlt[here] * SCALE, d3, 1, 1).astype(bf16)
        dv = mm(dbt, a3.astype(bf16), 1, 1) + dconv[here]
        dp[2, here] = jnp.where(slots < count, dv, 0.0).astype(bf16)


def mark_rows(wall, dlm, ep):
    ep[...] = (mm(matrix(wall, 0), dlm[0]) + mm(matrix(wall, 1), dlm[1])).T.astype(bf16)


def input_rows(wall, dp, dn):
    rows = dn.shape[1]
    d = mm(matrix(wall, 0), dp[0]) + mm(matrix(wall, 1), dp[1]) + mm(matrix(wall, 2), dp[2])
    dn[...] = d.T.astype(bf16).reshape(2, rows, 512)


def output_rows(att, wback, po):
    rows = po.shape[1]
    po[...] = mm(att[...], wback[...], 0, 0).astype(bf16).reshape(2, rows, 512)


def weight_grad(j, normed, xbar, dhrb, att, dp, dlm, wpart):
    rows = normed.shape[1]
    if j == 3:
        grad = mm(att[...], dhrb[...].reshape(2 * rows, 512))
    else:
        grad = mm(dp[j], normed[...].reshape(2 * rows, 512))
        if j < 2:
            grad = grad + mm(dlm[j], xbar[...])
    low = grad.T.astype(bf16)
    size, _, _, wr, _ = wpart.shape
    for half in range(2):
        for g in range(size):
            first = (half * size + g) * wr
            wpart[g, half, j] = low[first:first + wr]


class Refs:
    def __init__(self, names, refs):
        self.__dict__.update(zip(names, refs))


INPUTS = ("cnt", "tok", "cot", "gain", "bias", "wqkv", "woutt", "taps", "obias", "pbias", "k7", "k5", "k3")


def layer_results(n, rows, wr):
    return dict(
        outf=((2, rows, 512), bf16), gxf=((2, rows, 512), f32), gw=((4, wr, 256), f32),
        sums=((8, 128), f32), gkall=((56, 512), f32),
    )


def layer_buffers(n, rows, wr):
    size = n // 2
    mb, wide, grid = MARKS // size, 2 * rows, rows // GRID_W
    half2 = (2, rows, 256)
    return dict(
        wts=((4, wr, 256), bf16), wall=((n, 4, wr, 256), bf16), wback=((256, 512), bf16), wt=((3, 256, 512), bf16),
        xblk=((2, rows, 512), bf16), normed=((2, rows, 512), bf16), xbar=((MARKS, 512), bf16),
        nown=((2, rows, 512), bf16), xp=((2, MARKS, 256), bf16), xr=((n, mb, 256), bf16), xm=((mb, 256), bf16),
        halo=((2, 2, 192, 256), bf16), dh=(half2, f32), dhrb=((2, rows, 512), bf16),
        kc=((7, 8, 256), f32), zs=((7, grid + 6, GRID_W, 256), f32), zc=((2, 7, grid + 6, GRID_W, 256), f32), pad=((grid + 6, GRID_W + 16, 256), f32),
        qt=((256, wide), bf16), kt=((256, wide), bf16), vt=((256, wide), bf16), dot=((256, wide), bf16),
        qlt=((256, MARKS), bf16), klt=((256, MARKS), bf16), a1=((4, MARKS, wide), bf16), e3=((4, wide, MARKS), bf16),
        blkb=((4, PART, MARKS), bf16), blkd=((4, 64, MARKS), bf16),
        recvb=((size, PART, MARKS), bf16), recvd=((size, 64, MARKS), bf16),
        halv=((2, 2, 16, 256), bf16), hald=((2, 2, 16, 256), bf16), rhv=((2, 2, 16, 256), bf16), rhd=((2, 2, 16, 256), bf16),
        ps=((SWEEPS, 2, 256, 256), bf16), ts=((SWEEPS, 2, 256, 256), bf16), xs=((SWEEPS + 1, 64, 256), f32), ys=((SWEEPS + 1, 64, 256), f32), ctf=((64, 256), f32), dctf=((64, 256), f32),
        amat=((256, 256), f32), asp=((2, 256, 256), bf16), pcur=((256, 256), f32), ecur=((256, 256), f32),
        res=((2, PART, MARKS), bf16), resall=((2, 8, PART, MARKS), bf16),
        tm=((2, 4, 2, rows, rows), bf16), th=((2, 4, 2, 32, rows), bf16), hv=((2, 256, 32), bf16), hdt=((2, 256, 32), bf16),
        hvr=((2, 256, 32), bf16), vr=((2, 256, rows), bf16), conv=((256, wide), f32), dconv=((256, wide), f32),
        base=((8, 8, 256), f32), gsum=((4, 8, 256), f32), gtaps=((8, 256), f32), att=((256, wide), bf16), dp=((3, 256, wide), bf16),
        dlm=((2, 256, MARKS), bf16), po=((2, rows, 512), bf16), dn=((2, rows, 512), bf16), ep=((MARKS, 512), bf16),
        wpart=((size, 2, 4, wr, 256), bf16), er=((MARKS, 256), bf16), es=((MARKS, 256), bf16), erv=((size, mb, 256), bf16),
        em=((mb, 256), bf16), eall=((MARKS, 512), bf16), por=(half2, bf16),
        dnr=((2, rows, 512), bf16), hid=(half2, f32), z=(half2, bf16), cotb=(half2, bf16), lnf=((rows, 512), f32), dhf=((rows, 512), f32), zhalo=((2, 2, 192, 256), bf16),
        lnr=((rows, 512), bf16), lns=((rows, 256), bf16), wrv=((size, 2, 4, wr, 256), bf16), wsum=((4, wr, 256), bf16),
        wone=((4, wr, 256), bf16), gacc=((49, 8, 256), f32), outh=(half2, bf16), gk=((56, 256), f32),
        gkr=((n, 8, 256), f32), gkm=((8, 256), f32), small=((8, 512), f32), smr=((n, 8, 128), f32), smx=((8, 128), f32),
    )


SEMS = dict(
    s_w=2, s_v=4, s_t=1, s_h=4, s_x=1, s_g=1, s_p=4, s_d=1, s_b=1, s_c=1, s_r=2, s_q=4, s_a=4, s_e=1, s_f=1, s_z=2, s_l=5,
    s_y=1, s_u=1, s_k=1, s_m=1, s_s=1,
)


class Many:
    def __init__(self, total, sems, i, **where):
        self.sems, self.i, self.all = sems, i, remote(total, total, sems, i, **where)

    def add(self, src, dst, **where):
        remote(src, dst, self.sems, self.i, **where).start()

    def wait_recv(self):
        self.all.wait_recv()

    def wait_send(self):
        self.all.wait_send()


def layer_kernel(n, names, *refs):
    r = Refs(names, refs)
    half, g, partner = place(n)
    me = lax.axis_index("seq")
    hd = lax.axis_index("head")
    other = 1 - half
    size = n // 2
    rows = r.tok.shape[1]
    mb, wr = MARKS // size, r.wts.shape[1]
    mine = my_half()
    theirs = pl.ds(pl.multiple_of((1 - hd) * 256, 256), 256)
    count = r.cnt[half]
    near, far = cube(n), everyone(n)
    core = 1 - hd

    def marks(i):
        return pl.ds(pl.multiple_of(lax.rem(g + i, size) * mb, mb), mb)

    cube_marks = pl.ds(0, (size - 1) * mb)

    def fan(total, sems, i, pieces):
        group = Many(total, sems, i, seq=near[1])
        for j, (src, dst) in enumerate(pieces, 1):
            group.add(src, dst, seq=near[j])
        return [group]

    hail(far[1:])
    r.wts[0:3] = r.wqkv[...]
    r.wts[3] = r.woutt[...]
    for k in range(2):
        norm_rows(r.tok.at[k], r.gain, r.bias, r.nown.at[k])
        mem = member(r.cnt[k], me * rows, rows)
        r.xp[k] = mm(mem, r.nown[k, :, mine]).astype(bf16)
    heard(far[1:])
    c_x = [Many(r.xr.at[pl.ds(0, n - 1)], r.s_x, 0, seq=partner)]
    for i in range(1, n):
        at = pl.ds(pl.multiple_of(lax.rem(far[i], size) * mb, mb), mb)
        c_x[0].add(r.xp.at[far[i] // size, at], r.xr.at[me], seq=far[i])
    row = marks(0)
    r.xr[pl.ds(me, 1)] = r.xp[half, row][None]
    first3 = pl.ds(0, 3)
    others = r.wall.at[pl.ds(0, size - 1), first3]
    others_out = r.wall.at[pl.ds(0, size - 1), 3]
    c_w = go([remote(r.wts.at[first3], r.wall.at[me, first3], r.s_w, 0, seq=partner)])
    c_t = go([remote(r.tok.at[other, :, mine], r.xblk.at[half, :, mine], r.s_t, 0, seq=partner)])
    c_v = fan(others, r.s_v, 0, [(r.wts.at[first3], r.wall.at[me, first3])] * (size - 1))
    up, down = far[1], far[n - 1]
    first, final = pl.ds(0, 192), pl.ds(rows - 192, 192)
    c_h = go([
        remote(r.cot.at[up // size, final, mine], r.halo.at[0, up // size], r.s_h, 0, seq=up),
        remote(r.cot.at[down // size, first, mine], r.halo.at[1, down // size], r.s_h, 1, seq=down),
    ])
    r.wall[pl.ds(me, 1)] = r.wts[...][None]
    r.cotb[half] = r.cot[half, :, mine]
    r.xblk[half] = r.tok[half]
    r.normed[half] = r.nown[half]
    join_taps(r.kc, r.k7, r.k5, r.k3)
    got(c_w)
    c_v += fan(others, r.s_v, 1, [(r.wall.at[partner, first3],) * 2] * (size - 1))
    make_bands(r.taps, rows, r.base, r.tm, r.th)

    got(c_x)
    total = r.xr[0].astype(f32)
    for d in range(1, n):
        total = total + r.xr[d].astype(f32)
    low, high = edges(count, iota((mb, 256), 0) + g * mb)
    r.xm[...] = (total / (high - low).astype(f32)).astype(bf16)
    r.xbar[row, mine] = r.xm[...]
    c_g = fan(r.xbar.at[cube_marks, mine], r.s_g, 0, [(r.xm, r.xbar.at[row, mine])] * (size - 1))
    got(c_t)
    c_p = go([remote(r.xblk.at[other, :, mine], r.xblk.at[other, :, mine], r.s_p, 0, head=core)])
    c_d = go([remote(r.cot.at[other, :, mine], r.cotb.at[half], r.s_d, 0, seq=partner)])
    c_w += go([remote(r.wts.at[3], r.wall.at[me, 3], r.s_w, 1, seq=partner)])
    got(c_h)
    load_cot(n, half, r.cotb, r.halo[0, half], r.halo[1, half], r.zc.at[half], r.pad)
    back_conv(n, count, half, r.cotb, r.zc.at[half], r.kc, r.dh)
    c_p += go([remote(r.dh.at[half], r.dhf.at[:, mine], r.s_p, 2, head=core)])
    r.dhf[:, mine] = r.dh[half]
    got(c_g)
    c_p += go([remote(r.xbar.at[:, mine], r.xbar.at[:, mine], r.s_p, 1, head=core)])
    got(c_p[0:1])
    norm_rows(r.xblk.at[other], r.gain, r.bias, r.normed.at[other])
    got(c_v[0:2])
    project(n, count, r.normed, r.wall, r.wt, r.qt, r.kt, r.vt)
    got(c_w[1:])
    c_v += fan(others_out, r.s_v, 2, [(r.wts.at[3], r.wall.at[me, 3])] * (size - 1))
    c_v += fan(others_out, r.s_v, 3, [(r.wall.at[partner, 3],) * 2] * (size - 1))
    value_edges(n, count, r.normed, r.wall, r.halv)
    c_q = go([
        remote(r.halv.at[1], r.rhv.at[0], r.s_q, 0, seq=near[1]),
        remote(r.halv.at[0], r.rhv.at[1], r.s_q, 1, seq=near[size - 1]),
    ])

    got(c_p[2:3])
    landmarks(r.xbar, r.wt, r.qlt, r.klt)
    here = head_rows(head_of(g))
    one = Chain(r.qlt.at[here], r.klt.at[here], r)
    key_scores(n, count, r.kt, r.qlt, r.vt, r.e3, r.blkb)

    def give(blk, recv, sems):
        for h, o in enumerate(OWNERS):

            @pl.when(g != o)
            def _():
                remote(blk.at[h], recv.at[g], sems, 0, seq=half * size + o).start()

            @pl.when(g == o)
            def _():
                recv[pl.ds(g, 1)] = blk[h:h + 1]

    def gave(blk, sems):
        remote(blk, blk, sems, 0, seq=near[1]).wait_send()

    give(r.blkb, r.recvb, r.s_b)
    got(c_d)
    above = jnp.where((g == size - 1) & (half == 0), half, other)
    below = jnp.where((g == 0) & (half == 1), half, other)
    c_h += go([
        remote(r.cotb.at[above, final], r.halo.at[0, other], r.s_h, 2, seq=near[1]),
        remote(r.cotb.at[below, first], r.halo.at[1, other], r.s_h, 3, seq=near[size - 1]),
    ])
    one.begin()
    pl.loop(0, SWEEPS, unroll=SWEEPS)(one.sweep)

    def spread(k):
        for h, o in enumerate(OWNERS):

            @pl.when(g == o)
            def _():
                for i in range(1, size):
                    remote(r.res.at[k], r.resall.at[k, h], r.s_r, k, seq=near[i]).start()
                r.resall[k, h] = r.res[k]

    def results(k):
        def arrive(count):
            part = r.resall.at[k, pl.ds(0, count)]
            remote(part, part, r.s_r, k, seq=near[1]).wait_recv()

        @pl.when(is_owner(g))
        def _():
            arrive(3)

        @pl.when(jnp.logical_not(is_owner(g)))
        def _():
            arrive(4)

    def wait_for(recv, sems):
        part = recv.at[pl.ds(0, size - 1)]
        remote(part, part, sems, 0, seq=near[1]).wait_recv()

    @pl.when(is_owner(g))
    def _():
        wait_for(r.recvb, r.s_b)
        one.forward()
        spread(0)

    got(c_h[2:])
    load_cot(n, other, r.cotb, r.halo[0, other], r.halo[1, other], r.zc.at[other], r.pad)
    back_conv(n, count, other, r.cotb, r.zc.at[other], r.kc, r.dh)
    r.dhrb[:, :, mine] = r.dh[...].astype(bf16)
    c_p += go([remote(r.dhrb.at[:, :, mine], r.dhrb.at[:, :, mine], r.s_p, 3, head=core)])
    query_scores(r.qt, r.klt, r.a1)
    got(c_v[2:4])
    r.wback[...] = matrix(r.wall, 3).T
    got(c_p[3:4])
    out_grads(r.dhrb, r.wback, r.dot, r.hald)
    c_q += go([
        remote(r.hald.at[1], r.rhd.at[0], r.s_q, 2, seq=near[1]),
        remote(r.hald.at[0], r.rhd.at[1], r.s_q, 3, seq=near[size - 1]),
    ])
    partial_dc(r.dot, r.a1, r.blkd)
    give(r.blkd, r.recvd, r.s_c)

    got(c_q)
    value_conv(n, r.vt, r.rhv, r.tm, r.th, r.hv, r.vr, r.hvr, r.conv)
    results(0)
    attend(r.resall, r.a1, r.conv, r.att)
    output_rows(r.att, r.wback, r.po)
    c_a = go([remote(r.po.at[:, :, theirs], r.por, r.s_a, 0, head=core)])

    @pl.when(is_owner(g))
    def _():
        wait_for(r.recvd, r.s_c)
        one.backward()
        spread(1)

    value_conv_back(n, r.dot, r.rhd, r.tm, r.th, r.hdt, r.vr, r.hvr, r.dconv, r.gsum, r.gtaps)
    r.small[...] = jnp.zeros_like(r.small)
    r.gacc[...] = jnp.zeros_like(r.gacc)
    got(c_a[0:1])
    for b in range(2):
        part = r.po[b, :, mine].astype(f32) + r.por[b].astype(f32)
        r.z[b] = hidden_rows(n, count, b, r.xblk, r.obias, part, r.hid).astype(bf16)
    c_z = go([
        remote(r.z.at[:, final], r.zhalo.at[0], r.s_z, 0, seq=near[1]),
        remote(r.z.at[:, first], r.zhalo.at[1], r.s_z, 1, seq=near[size - 1]),
    ])

    @pl.when(is_owner(g))
    def _():
        r.ecur[...] = jnp.zeros_like(r.ecur)
        pl.loop(0, SWEEPS, unroll=SWEEPS)(lambda i: one.power_grad(SWEEPS - 1 - i))

    results(1)
    weights = (r.normed, r.xbar, r.dhrb, r.att, r.dp, r.dlm, r.wpart)
    c_y = [Many(r.wrv.at[pl.ds(0, size - 1)], r.s_y, 0, seq=near[1])]

    score_grads(n, count, r.qt, r.kt, r.vt, r.qlt, r.klt, r.dot, r.a1, r.e3, r.blkb, r.resall, r.dconv, r.dp, r.dlm)
    @pl.when(is_owner(g))
    def _():
        add_chain(here, r.dlm, one.finish())

    mark_rows(r.wall, r.dlm, r.ep)
    c_a += go([remote(r.ep.at[:, theirs], r.er, r.s_a, 1, head=core)])
    got(c_a[1:2])
    r.es[...] = (r.ep[:, mine].astype(f32) + r.er[...].astype(f32)).astype(bf16)
    c_e = fan(r.erv.at[pl.ds(0, size - 1)], r.s_e, 0, [(r.es.at[marks(i)], r.erv.at[g]) for i in range(1, size)])
    r.erv[pl.ds(g, 1)] = r.es[row][None]
    lines = rows // GRID_W

    @pl.loop(0, 2 * lines)
    def _(i):
        kernel_grads(n, count, i // lines, lax.rem(i, lines), r.hid, r.zc.at[i // lines], r.gacc)

    grid_sums(r.gacc, r.dh, r.cotb, r.gtaps, r.gk)
    blocks = r.gk.shape[0] // 8

    def block(b):
        return r.gk.at[pl.ds(8 * b, 8)]

    def on_block_owner(inside, outside):
        pl.when(me < blocks)(inside)
        pl.when(me >= blocks)(outside)

    for b in range(blocks):

        @pl.when(me != b)
        def _():
            remote(block(b), r.gkr.at[me], r.s_k, 0, seq=b).start()

        @pl.when(me == b)
        def _():
            r.gkr[pl.ds(me, 1)] = block(b)[...][None]

    input_rows(r.wall, r.dp, r.dn)
    c_a += go([remote(r.dn, r.dnr, r.s_a, 2, head=core)])
    weight_grad(3, *weights)
    weight_grad(2, *weights)
    got(c_e)
    total = r.erv[0].astype(f32)
    for d in range(1, size):
        total = total + r.erv[d].astype(f32)
    r.em[...] = total.astype(bf16)
    r.eall[row, mine] = r.em[...]
    c_f = fan(r.eall.at[cube_marks, mine], r.s_f, 0, [(r.em, r.eall.at[row, mine])] * (size - 1))
    def send_weights(j):
        for i in range(1, size):
            c_y[0].add(r.wpart.at[lax.rem(g + i, size), :, j], r.wrv.at[g, :, j], seq=near[i])

    send_weights(3)
    send_weights(2)
    for j in range(2):
        weight_grad(j, *weights)
        send_weights(j)
    r.wrv[pl.ds(g, 1)] = r.wpart[pl.ds(g, 1)]

    got(c_f)
    c_a += go([remote(r.eall.at[:, mine], r.eall.at[:, mine], r.s_a, 3, head=core)])
    everything = r.gkr.at[pl.ds(0, n - 1)]

    @pl.when(me < blocks)
    def _():
        remote(everything, everything, r.s_k, 0, seq=partner).wait_recv()
        gsum = r.gkr[0]
        for d in range(1, n):
            gsum = gsum + r.gkr[d]
        r.gkm[...] = gsum
        here = pl.ds(pl.multiple_of(8 * me, 8), 8)
        r.gkall[here, mine] = gsum
        for i in range(1, n):
            remote(r.gkm, r.gkall.at[here, mine], r.s_m, 0, seq=far[i]).start()

    got(c_a[2:4])
    norm_back(n, g, count, other, r.xblk, r.dn, r.dnr, r.eall, r.gain, r.small, r.lnf)
    r.lns[...] = (r.lnf[:, mine] + r.dh[other]).astype(bf16)
    c_l = go([remote(r.lns, r.lnr.at[:, mine], r.s_l, 0, seq=partner)])
    got(c_p[1:2])
    norm_back(n, g, count, half, r.xblk, r.dn, r.dnr, r.eall, r.gain, r.small, r.lnf)
    r.gxf[half] = r.dhf[...] + r.lnf[...]
    for a in range(2):
        for b in range(4):
            r.smx[4 * a + b:4 * a + b + 1] = r.small[a:a + 1, 128 * b:128 * b + 128]
    c_s = [Many(r.smr.at[pl.ds(0, n - 1)], r.s_s, 0, seq=partner)]
    for i in range(1, n):
        c_s[0].add(r.smx, r.smr.at[me], seq=far[i])
    r.smr[pl.ds(me, 1)] = r.smx[...][None]

    got(c_z)
    grid_forward(n, count, other, r.hid, r.zhalo, r.kc, r.pbias, r.outh, r.zs, r.pad)
    c_l += go([remote(r.outh.at[other], r.outf.at[half, :, mine], r.s_l, 1, seq=partner)])
    grid_forward(n, count, half, r.hid, r.zhalo, r.kc, r.pbias, r.outh, r.zs, r.pad)
    r.outf[half, :, mine] = r.outh[half]
    got(c_l[0:1])
    c_l += go([remote(r.lnr.at[:, mine], r.lnr.at[:, mine], r.s_l, 2, head=core)])
    got(c_y)
    c_u = []
    for k in (other, half):
        total = r.wrv[0, k].astype(f32)
        for d in range(1, size):
            total = total + r.wrv[d, k].astype(f32)
        if k is other:
            r.wsum[...] = total.astype(bf16)
            c_u = go([remote(r.wsum, r.wone, r.s_u, 0, seq=partner)])

    def blocks_back(count):
        part = r.gkall.at[pl.ds(0, 8 * count), mine]
        return remote(part, part, r.s_m, 0, seq=partner)

    on_block_owner(blocks_back(blocks - 1).wait_recv, blocks_back(blocks).wait_recv)
    c_l += go([remote(r.gkall.at[:, mine], r.gkall.at[:, mine], r.s_l, 4, head=core)])
    got(c_s)
    acc = r.smr[0]
    for d in range(1, n):
        acc = acc + r.smr[d]
    r.sums[...] = acc
    got(c_l[1:2])
    c_l += go([remote(r.outf.at[:, :, mine], r.outf.at[:, :, mine], r.s_l, 3, head=core)])
    got(c_l[2:3])
    r.gxf[other] = r.lnr[...].astype(f32)
    got(c_u)
    r.gw[...] = total + r.wone[...].astype(f32)
    got(c_l[3:])

    sent(c_t + c_w + c_v + c_h + c_p + c_x + c_d + c_g + c_q + c_a + c_e + c_f + c_z + c_y + c_l + c_s + c_u)

    @pl.when(is_owner(g))
    def _():
        gave(r.blkb.at[pl.ds(0, 3)], r.s_b)
        gave(r.blkd.at[pl.ds(0, 3)], r.s_c)
        for k in range(2):
            part = r.resall.at[k, pl.ds(0, size - 1)]
            remote(part, part, r.s_r, k, seq=near[1]).wait_send()

    @pl.when(jnp.logical_not(is_owner(g)))
    def _():
        gave(r.blkb, r.s_b)
        gave(r.blkd, r.s_c)

    def blocks_left(count):
        part = r.gk.at[pl.ds(0, 8 * count)]
        return remote(part, part, r.s_k, 0, seq=partner)

    on_block_owner(blocks_left(blocks - 1).wait_send, blocks_left(blocks).wait_send)

    @pl.when(me < blocks)
    def _():
        remote(everything, everything, r.s_m, 0, seq=partner).wait_send()


def result_kernel(outf, gxf, gw, sums, gkall, out, gx, gwqkv, gwoutt, ggain, gbias, gtaps, gob, k7o, k5o, k3o, gpb):
    out[...] = outf[...]
    gx[...] = gxf[...]
    gwqkv[...] = gw[0:3]
    gwoutt[...] = gw[3]
    for i in range(4):
        ggain[:, 128 * i:128 * i + 128] = sums[i:i + 1]
        gbias[:, 128 * i:128 * i + 128] = sums[4 + i:5 + i]
    rows = gkall[51:55, my_half()]
    li, lt = iota((256, 33), 0), iota((256, 33), 1)
    spot = jnp.where(((li + lt) & 255) == 16, 1.0, 0.0).astype(bf16)
    parts = [mm(piece.astype(bf16), spot) for piece in split3(rows)]
    gtaps[...] = parts[0] + parts[1] + parts[2]
    gob[...] = gkall[49:50]
    gpb[...] = gkall[50:51]
    spill_kernels(gkall, k7o, k5o, k3o)


def half_of(full, axis):
    return lax.dynamic_slice_in_dim(full, lax.axis_index("head") * 256, 256, axis)


def swap(n, blocks):
    half, _, _ = place(n)
    theirs = lax.ppermute(jnp.where(half == 0, blocks[1], blocks[0]), "seq", [(i, (i + n // 2) % n) for i in range(n)])
    own = jnp.where(half == 0, blocks[0], blocks[1])
    return jnp.where(half == 0, jnp.stack([own, theirs]), jnp.stack([theirs, own]))


def half_sum(n, value):
    half, _, _ = place(n)
    pair = lax.psum(jnp.stack([jnp.where(half == s, value, 0.0) for s in range(2)]), "seq")
    return jnp.where(half == 0, pair[0], pair[1])


def half_max(n, value):
    half, _, _ = place(n)
    pair = lax.pmax(jnp.stack([jnp.where(half == s, value, -jnp.inf) for s in range(2)]), "seq")
    return jnp.where(half == 0, pair[0], pair[1])


def norm_kernel(n, cnt, xblk, gain, bias, normed, xp):
    half, g, _ = place(n)
    for b in range(2):
        norm_rows(xblk.at[b], gain, bias, normed.at[b])
    xp[...] = segment_sums(n, g, cnt[half], normed)


def back_conv_kernel(n, cnt, cotb, halo, k7, k5, k3, dh, kc, zs, pad):
    half, _, _ = place(n)
    join_taps(kc, k7, k5, k3)
    for b in range(2):
        load_cot(n, b, cotb, *ring_ends(n, place(n)[1], b, halo), zs, pad)
        back_conv(n, cnt[half], b, cotb, zs, kc, dh)


def start_plain(n, counts, tok, cot, gain, bias, wqkv, woutt, k7, k5, k3, scratch):
    half, _, _ = place(n)
    rows = tok.shape[1]
    count = counts[half]
    xblk = swap(n, tok)
    normed, xp = call(
        functools.partial(norm_kernel, n), [sds((2, rows, 512), bf16), sds((MARKS, 256))], [SMEM] + [VMEM] * 3
    )(counts, xblk, gain, bias)
    low, high = edges(count, jnp.arange(MARKS, dtype=jnp.int32))
    xbar = (half_sum(n, xp) / (high - low).astype(f32)[:, None]).astype(bf16)
    xbar = lax.all_gather(xbar, "head", axis=1, tiled=True)
    wts = jnp.concatenate([wqkv, woutt[None]], axis=0)
    wall = lax.all_gather(wts, "seq", axis=1, tiled=True).reshape(4, 16, 32, 256).swapaxes(0, 1)
    cotb = half_of(swap(n, cot), 2)
    halo = half_ring(n, jnp.stack([cotb[:, :192], cotb[:, -192:]]))
    dh = call(functools.partial(back_conv_kernel, n), sds((2, rows, 256)), [SMEM] + [VMEM] * 5, scratch)(
        counts, cotb, halo, k7, k5, k3
    )
    dhrb = lax.all_gather(dh.astype(bf16), "head", axis=2, tiled=True)
    return xblk, normed, xbar, wall, cotb, halo, dh, dhrb


def half_ring(n, hal):
    size = n // 2
    up = [(i, i // size * size + (i + 1) % size) for i in range(n)]
    return jnp.stack([lax.ppermute(hal[1], "seq", up), lax.ppermute(hal[0], "seq", [(j, i) for i, j in up])])


def three_rows(stat, first):
    return (stat[:, first:first + 1] + stat[:, first + 1:first + 2]) + stat[:, first + 2:first + 3]


def reduce_plain(n, blkb, blkd, halv, hald):
    _, g, _ = place(n)
    stat = blkb[:, 64:].astype(f32)
    top, total = three_rows(stat, 0), three_rows(stat, 3)
    best = half_max(n, top)
    w = jnp.exp(top - best)
    total = half_sum(n, total * w)
    value = half_sum(n, blkb[:, 0:64].astype(f32) * w)
    dct = half_sum(n, blkd.astype(f32)).astype(bf16)
    stat = jnp.concatenate(split3(best) + split3(total) + [jnp.zeros((4, 10, MARKS), f32)], axis=1)
    whole = jnp.concatenate([value, stat], axis=1).astype(bf16)
    h = head_of(g)
    recvb, recvd = lax.dynamic_slice_in_dim(whole, h, 1, 0), lax.dynamic_slice_in_dim(dct, h, 1, 0)
    return recvb, recvd, half_ring(n, halv), half_ring(n, hald)


def spread_plain(n, res):
    _, g, _ = place(n)
    held = ((jnp.arange(4) == head_of(g)) & is_owner(g))[None, :, None, None]
    return half_sum(n, jnp.where(held, res[:, None].astype(f32), 0.0)).astype(bf16)


def scores_kernel(n, cnt, normed, xbar, wall, dhrb, qt, kt, vt, qlt, klt, dot, wback, a1, e3, blkb, blkd, halv, hald, wt):
    half, _, _ = place(n)
    count = cnt[half]
    wback[...] = matrix(wall, 3).T
    project(n, count, normed, wall, wt, qt, kt, vt)
    value_edges(n, count, normed, wall, halv)
    landmarks(xbar, wt, qlt, klt)
    key_scores(n, count, kt, qlt, vt, e3, blkb)
    query_scores(qt, klt, a1)
    out_grads(dhrb, wback, dot, hald)
    partial_dc(dot, a1, blkd)


CHAIN = ("res", "amat", "asp", "pcur", "ps", "ts", "xs", "ys", "ctf", "dctf", "ecur")


def chain_kernel(n, recvb, recvd, qlt, klt, dqz, *refs):
    _, g, _ = place(n)
    here = head_rows(head_of(g))
    dqz[...] = jnp.zeros_like(dqz)
    refs[0][...] = jnp.zeros_like(refs[0])

    @pl.when(is_owner(g))
    def _():
        one = Chain(qlt.at[here], klt.at[here], Refs(("recvb", "recvd") + CHAIN, (recvb, recvd) + refs))
        one.begin()
        pl.loop(0, SWEEPS)(one.sweep)
        one.forward()
        one.backward()
        one.r.ecur[...] = jnp.zeros_like(one.r.ecur)
        pl.loop(0, SWEEPS)(lambda i: one.power_grad(SWEEPS - 1 - i))
        dqz[0], dqz[1] = one.finish()


def grads_kernel(n, cnt, normed, xbar, wall, wback, dhrb, qt, kt, vt, qlt, klt, dot, a1, e3, blkb, resall, rhv, rhd, taps,
                 dqz, po, dn, ep, wpart, gtaps, base, tm, th, hv, hdt, hvr, vr, conv, dconv, gsum, att, dp, dlm):
    half, _, _ = place(n)
    make_bands(taps, normed.shape[1], base, tm, th)
    value_conv(n, vt, rhv, tm, th, hv, vr, hvr, conv)
    value_conv_back(n, dot, rhd, tm, th, hdt, vr, hvr, dconv, gsum, gtaps)
    attend(resall, a1, conv, att)
    output_rows(att, wback, po)
    score_grads(n, cnt[half], qt, kt, vt, qlt, klt, dot, a1, e3, blkb, resall, dconv, dp, dlm)
    add_chain(head_rows(head_of(place(n)[1])), dlm, dqz)
    mark_rows(wall, dlm, ep)
    input_rows(wall, dp, dn)
    for j in range(4):
        weight_grad(j, normed, xbar, dhrb, att, dp, dlm, wpart)


def hidden_kernel(n, cnt, x, obias, part, hid, z):
    half, _, _ = place(n)
    for b in range(2):
        z[b] = hidden_rows(n, cnt[half], b, x, obias, part[b], hid).astype(bf16)


def final_kernel(n, cnt, hid, halo, cotb, chalo, k7, k5, k3, pbias, xblk, dn, dnr, eall, gain, dh, gtaps,
                 outh, lnb, gk, small, kc, zs, pad, gacc):
    half, g, _ = place(n)
    join_taps(kc, k7, k5, k3)
    gacc[...] = jnp.zeros_like(gacc)
    small[...] = jnp.zeros_like(small)
    for b in range(2):
        grid_forward(n, cnt[half], b, hid, halo, kc, pbias, outh, zs, pad)
        load_cot(n, b, cotb, *ring_ends(n, g, b, chalo), zs, pad)
        pl.loop(0, hid.shape[1] // GRID_W)(lambda i: kernel_grads(n, cnt[half], b, i, hid, zs, gacc))
    grid_sums(gacc, dh, cotb, gtaps, gk)
    for b in range(2):
        norm_back(n, g, cnt[half], b, xblk, dn, dnr, eall, gain, small, lnb.at[b])


def late_plain(n, counts, cotb, chalo, xblk, dh, po, ep, dn, wpart, gtaps, gain, obias, pbias, k7, k5, k3, scratch):
    rows = xblk.shape[1]
    part = half_of(lax.psum(po.astype(f32), "head").astype(bf16), 2)
    hid, z = call(functools.partial(hidden_kernel, n), [sds((2, rows, 256)), sds((2, rows, 256), bf16)], [SMEM] + [VMEM] * 3)(
        counts, xblk, obias, part
    )
    halo = half_ring(n, jnp.stack([z[:, :192], z[:, -192:]]))
    dnr = lax.ppermute(dn, "head", [(0, 1), (1, 0)])
    eall = half_sum(n, lax.psum(ep.astype(f32), "head")).astype(bf16)
    outh, lnb, gk, small = call(
        functools.partial(final_kernel, n),
        [sds((2, rows, 256), bf16), sds((2, rows, 512)), sds((56, 256)), sds((8, 512))],
        [SMEM] + [VMEM] * 15,
        scratch + [pltpu.VMEM((49, 8, 256), f32)],
    )(counts, hid, halo, cotb, chalo, k7, k5, k3, pbias, xblk, dn, dnr, eall, gain, dh, gtaps)
    out = swap(n, lax.all_gather(outh, "head", axis=2, tiled=True))
    gx = swap(n, lax.all_gather(dh, "head", axis=2, tiled=True) + lnb)
    parts = wpart.transpose(2, 1, 0, 3, 4).reshape(4, 512, 256)
    gw = lax.psum_scatter(parts.astype(f32), "seq", scatter_dimension=1, tiled=True)
    gk, small = lax.psum((gk, small), "seq")
    gkall = lax.all_gather(gk, "head", axis=1, tiled=True)
    return out, gx, gw, small[0:2].reshape(8, 128), gkall


def layer_plain(n, counts, tok, cot, gain, bias, wqkv, woutt, taps, obias, pbias, k7, k5, k3):
    rows = tok.shape[1]
    made = layer_buffers(n, rows, wqkv.shape[1]) | dict(wpart=((8, 2, 4, 32, 256), bf16))

    def out(*names):
        return [sds(*made[name]) for name in names]

    def tmp(*names):
        return [pltpu.VMEM(*made[name]) for name in names]

    conv_tmp = tmp("kc", "zs", "pad")
    xblk, normed, xbar, wall, cotb, chalo, dh, dhrb = start_plain(
        n, counts, tok, cot, gain, bias, wqkv, woutt, k7, k5, k3, conv_tmp
    )
    qt, kt, vt, qlt, klt, dot, wback, a1, e3, blkb, blkd, halv, hald = call(
        functools.partial(scores_kernel, n),
        out("qt", "kt", "vt", "qlt", "klt", "dot", "wback", "a1", "e3", "blkb", "blkd", "halv", "hald"),
        [SMEM] + [VMEM] * 4,
        tmp("wt"),
    )(counts, normed, xbar, wall, dhrb)
    recvb, recvd, rhv, rhd = reduce_plain(n, blkb, blkd, halv, hald)
    dqz, res = call(
        functools.partial(chain_kernel, n), [sds((2, 64, MARKS)), sds((2, PART, MARKS), bf16)], [VMEM] * 4, tmp(*CHAIN[1:])
    )(recvb, recvd, qlt, klt)
    resall = spread_plain(n, res)
    po, dn, ep, wpart, gtaps = call(
        functools.partial(grads_kernel, n),
        out("po", "dn", "ep", "wpart", "gtaps"),
        [SMEM] + [VMEM] * 19,
        tmp("base", "tm", "th", "hv", "hdt", "hvr", "vr", "conv", "dconv", "gsum", "att", "dp", "dlm"),
    )(counts, normed, xbar, wall, wback, dhrb, qt, kt, vt, qlt, klt, dot, a1, e3, blkb, resall, rhv, rhd, taps, dqz)
    return late_plain(
        n, counts, cotb, chalo, xblk, dh, po, ep, dn, wpart, gtaps, gain, obias, pbias, k7, k5, k3, conv_tmp
    )


def shards(n, tokens, counts, ln_gain, ln_bias, w_qkv, conv_taps, w_out, out_bias, kernel7, kernel5, kernel3, ppeg_bias, cotangent):
    rows, wr = tokens.shape[1], w_qkv.shape[1]
    gain, bias, obias, pbias = (v[None, :] for v in (ln_gain, ln_bias, out_bias, ppeg_bias))
    args = (counts, tokens, cotangent, gain, bias, w_qkv, w_out.T, conv_taps, obias, pbias, kernel7, kernel5, kernel3)
    if n == 16:
        results, buffers = layer_results(n, rows, wr), layer_buffers(n, rows, wr)
        names = INPUTS + tuple(results) + tuple(buffers) + tuple(SEMS)
        made = call(
            functools.partial(layer_kernel, n, names),
            [sds(*v) for v in results.values()],
            [SMEM] + [VMEM] * 12,
            [pltpu.VMEM(*v) for v in buffers.values()] + [DMA((2, k)) for k in SEMS.values()],
            cid=0,
            vmem=60,
        )(*args)
    else:
        made = layer_plain(n, *args)
    vec = sds((1, 512))
    out, gx, gwqkv, gwoutt, ggain, gbias, gtaps, gob, k7o, k5o, k3o, gpb = call(
        result_kernel,
        [sds((2, rows, 512), bf16), sds((2, rows, 512)), sds((3, wr, 256)), sds((wr, 256)), vec, vec, sds((4, 33)), vec,
         sds((7, 7, 512)), sds((5, 5, 512)), sds((3, 3, 512)), vec],
        [VMEM] * 5,
    )(*made)
    return out, gx, ggain[0], gbias[0], gwqkv, gtaps, gwoutt.T, gob[0], k7o, k5o, k3o, gpb[0]


def solution(mesh):
    rows, cols = P(None, "seq", None), P(None, "seq", "head")
    return jax.shard_map(
        functools.partial(shards, mesh.shape["seq"]),
        mesh=mesh,
        in_specs=(rows, P(), P(), P(), cols, P("head", None), P("head", "seq"), P(), P(), P(), P(), P(), rows),
        out_specs=(rows, rows, P(), P(), cols, P("head", None), P("head", "seq"), P(), P(), P(), P(), P()),
        check_vma=False,
    )
```
